32 devices in a mesh: row: 16 (over z, y, x), col: 2 (over core).
Axes of the slice: x: 2, y: 2, z: 4, core: 2. Of those that a mesh axis runs over, the one named last changes fastest.
Arguments:
- grad_out: bfloat16 [64, 256, 512], P(None, 'row', 'col'), may hold values from -6 to 6
- row_feat: bfloat16 [256, 64], P('row'), may hold values from -6 to 6
- col_feat: bfloat16 [512, 64], P('col'), may hold values from -6 to 6
- conv_one: bfloat16 [3, 3, 64, 64], replicated, may hold values from -0.25 to 0.25
- bias_one: float32 [64], replicated, may hold values from -3 to 3
- conv_two: bfloat16 [3, 3, 64, 64], replicated, may hold values from -0.25 to 0.25
Outputs:
- row_grad: float32 [256, 64], P('row')
- col_grad: float32 [512, 64], P('col')
- grad_conv_one: float32 [3, 3, 64, 64], replicated
- grad_bias: float32 [64], replicated
- grad_conv_two: float32 [3, 3, 64, 64], replicated
The draws below stay inside these ranges and needn't reach their ends.
All inputs are finite; a program needn't handle non-finite values.
Results may differ from the reference program's by a relative error of at most 0.0065.
Values may be sent and summed in bfloat16 or wider, within the bound.
A program may use at most 128 MiB of HBM per device.

```python
import math
import jax
import jax.numpy as jnp
from jax import lax

C = 64
NR = 256
NC = 512


def levels(rng, shape, shards, least, high):
    def one(position, shards_of):
        draws = jax.random.uniform(jax.random.fold_in(jax.random.fold_in(rng, 6), position), (shards_of,), jnp.float32, least / len(shards), high / len(shards))
        return jnp.repeat(jnp.exp(draws), shape[position] // shards_of).reshape((-1,) + (1,) * (len(shape) - position - 1))

    level = one(*shards[0])
    for cut in shards[1:]:
        level = level * one(*cut)
    return level


def bell_draw(own_key, dims, width, bound, split=(), dtype=jnp.bfloat16):
    entries = width * jax.random.normal(own_key, dims, jnp.float32)
    if split:
        entries = entries * levels(own_key, dims, split, -0.22, 0.18)
    return jnp.clip(entries, -bound, bound).astype(dtype)


def setup_inputs(seed: int = 0) -> dict:
    key_list = jax.random.split(jax.random.key(seed), 7)
    grad_out = bell_draw(key_list[0], (C, NR, NC), 1.0, 6.0, ((1, 16), (2, 2)))
    row_feat = bell_draw(key_list[1], (NR, C), 1.0, 6.0, ((0, 16),))
    col_feat = bell_draw(key_list[2], (NC, C), 1.0, 6.0, ((0, 2),))
    conv_one = bell_draw(key_list[3], (3, 3, C, C), (9 * C) ** -0.5, 0.25)
    bias_one = bell_draw(key_list[4], (C,), 0.5, 3.0, (), jnp.float32)
    conv_two = bell_draw(key_list[5], (3, 3, C, C), (9 * C) ** -0.5, 0.25)
    return {"grad_out": grad_out, "row_feat": row_feat, "col_feat": col_feat, "conv_one": conv_one, "bias_one": bias_one, "conv_two": conv_two}


def shifted(padded, shift_r, shift_c, rows, cols):
    return padded[:, 8 + 8 * shift_r:8 + 8 * shift_r + rows, 8 + 8 * shift_c:8 + 8 * shift_c + cols]

def pad_map(field):
    return jnp.pad(field, ((0, 0), (8, 8), (8, 8)))

def forward_conv(kernel, field):
    rows, cols = (field.shape[1], field.shape[2])
    padded = pad_map(field)
    total = jnp.zeros((kernel.shape[2], rows, cols), jnp.float32)
    for tap_r in range(3):
        for tap_c in range(3):
            piece = shifted(padded, tap_r - 1, tap_c - 1, rows, cols).astype(jnp.float32)
            total = total + jnp.einsum('oi,irc->orc', kernel[tap_r, tap_c].astype(jnp.float32), piece)
    return total

def transpose_conv(kernel, field):
    rows, cols = (field.shape[1], field.shape[2])
    padded = pad_map(field)
    total = jnp.zeros((kernel.shape[3], rows, cols), jnp.float32)
    for tap_r in range(3):
        for tap_c in range(3):
            piece = shifted(padded, 1 - tap_r, 1 - tap_c, rows, cols).astype(jnp.float32)
            total = total + jnp.einsum('oi,orc->irc', kernel[tap_r, tap_c].astype(jnp.float32), piece)
    return total

def kernel_grad(upper, field):
    rows, cols = (field.shape[1], field.shape[2])
    padded = pad_map(field)
    upper_f = upper.astype(jnp.float32)
    taps = []
    for tap_r in range(3):
        line = []
        for tap_c in range(3):
            piece = shifted(padded, tap_r - 1, tap_c - 1, rows, cols).astype(jnp.float32)
            line.append(jnp.einsum('orc,irc->oi', upper_f, piece))
        taps.append(jnp.stack(line))
    return jnp.stack(taps)

def reference(grad_out, row_feat, col_feat, conv_one, bias_one, conv_two):
    rows, cols = (grad_out.shape[1], grad_out.shape[2])
    field = (row_feat.T.astype(jnp.float32)[:, :, None] + col_feat.T.astype(jnp.float32)[:, None, :]).astype(jnp.bfloat16)
    pre = forward_conv(conv_one, field) + bias_one[:, None, None]
    act = jax.nn.silu(pre).astype(jnp.bfloat16)
    back = transpose_conv(conv_two, grad_out)
    sig = jax.nn.sigmoid(pre)
    inner = (back * (sig * (1.0 + pre * (1.0 - sig)))).astype(jnp.bfloat16)
    grad_in = grad_out.astype(jnp.float32) + transpose_conv(conv_one, inner)
    row_grad = lax.optimization_barrier(jnp.sum(grad_in, axis=2)).T / math.sqrt(cols)
    col_grad = lax.optimization_barrier(jnp.sum(grad_in, axis=1)).T / math.sqrt(rows)
    whole = math.sqrt(rows * cols)
    grad_conv_one = kernel_grad(inner, field) / whole
    grad_bias = lax.optimization_barrier(jnp.sum(inner.astype(jnp.float32), axis=(1, 2))) / whole
    grad_conv_two = kernel_grad(grad_out, act) / whole
    return (row_grad, col_grad, grad_conv_one, grad_bias, grad_conv_two)
```

```python
import functools
import math

import jax
import jax.numpy as jnp
from jax import lax
from jax.experimental import pallas as pl
from jax.experimental.pallas import tpu as pltpu
from jax.sharding import PartitionSpec as P

F32 = jnp.float32
BF16 = jnp.bfloat16
MESH = pl.DeviceIdType.MESH
NN = (((1,), (0,)), ((), ()))
NT = (((1,), (1,)), ((), ()))


def mm(x, y, dims=NN):
    return lax.dot_general(x, y, dims, preferred_element_type=F32)


def round_up(value, unit):
    return -(-value // unit) * unit


def kernel(
    n, nc, share, chunk,
    g_ref, row_ref, col_ref, k1_ref, bias_ref, k2_ref,
    rg_ref, cg_ref, g1_ref, gb_ref, g2_ref,
    rowbuf, colbuf, rrecv, crecv,
    gs, zb, act_s, inn_s, a_s, b_s, t_s, u_s, m3,
    pk, pk32, xtra, xtra32, p_recv, x_recv,
    dd, dd32, nb, nb_recv, d_recv, full, pfull,
    fs_sem, fr_sem, ps_sem, pr_sem, xs_sem, xr_sem,
    ds_sem, dr_sem, ns_sem, nr_sem, as_sem, ar_sem, cs_sem, cr_sem,
):
    row = lax.axis_index("row")
    col = lax.axis_index("col")
    rows, cols, wide = 16, 256, 384

    def row_peer(d):
        return lax.rem(row + d, n)

    def col_peer(d):
        return lax.rem(col + d, nc)

    barrier = pltpu.get_barrier_semaphore()
    for d in range(1, n):
        pl.semaphore_signal(barrier, inc=1, device_id=(row_peer(d), col), device_id_type=MESH)
    for d in range(1, nc):
        pl.semaphore_signal(barrier, inc=1, device_id=(row, col_peer(d)), device_id_type=MESH)

    def remote(src, dst, send, recv, to):
        return pltpu.make_async_remote_copy(
            src_ref=src, dst_ref=dst, send_sem=send, recv_sem=recv, device_id=to, device_id_type=MESH
        )

    pa = lax.broadcasted_iota(jnp.int32, (256, 256), 0)
    pb = lax.broadcasted_iota(jnp.int32, (256, 256), 1)
    perm = ((pa % 16) * 16 + pa // 16 == pb).astype(F32).astype(BF16)
    sa = lax.broadcasted_iota(jnp.int32, (256, wide), 0)
    sb = lax.broadcasted_iota(jnp.int32, (256, wide), 1)
    shifts = jnp.concatenate(
        [(lax.rem(sa + 8 * (b - 1) + wide, wide) == sb).astype(F32).astype(BF16) for b in range(3)], axis=1
    )

    def build(og, carry):
        x = g_ref[pl.ds(og * 16, 16)].reshape(256, cols)
        y = mm(mm(perm, x).astype(BF16), shifts).astype(BF16)
        for r in range(rows):
            h, k = r // 8, r % 8
            for b in range(3):
                gs[k, pl.ds(pl.multiple_of(b * 64 + og * 16, 16), 16), h * wide : (h + 1) * wide] = y[
                    16 * r : 16 * r + 16, b * wide : (b + 1) * wide
                ]
        return carry

    lax.fori_loop(0, 4, build, 0)

    pl.semaphore_wait(barrier, (n - 1) + (nc - 1))
    feats = [
        remote(row_ref, rrecv.at[0], fs_sem.at[0], fr_sem.at[0], (row_peer(1), col)),
        remote(row_ref, rrecv.at[1], fs_sem.at[1], fr_sem.at[1], (row_peer(n - 1), col)),
        remote(col_ref.at[pl.ds(cols - 16, 16)], crecv.at[0], fs_sem.at[2], fr_sem.at[2], (row, col_peer(1))),
        remote(col_ref.at[pl.ds(0, 16)], crecv.at[1], fs_sem.at[3], fr_sem.at[3], (row, col_peer(nc - 1))),
    ]
    for copy in feats:
        copy.start()

    w2 = jnp.concatenate(
        [k2_ref[a].reshape(192, 64).astype(F32).T.astype(BF16) for a in range(3)], axis=0
    )
    lane = lax.broadcasted_iota(jnp.int32, (64, 128), 1)

    def spread(k, carry):
        gsum, rsum = carry
        both = gs[k]
        z = mm(w2, both)
        lo, hi = z[:, :wide], z[:, wide:]
        zb[0, k] = lo[0:64]
        zb[1, k] = lo[64:128] + hi[0:64]
        zb[2, k] = lo[128:192] + hi[64:128]
        zb[3, k] = hi[128:192]
        mid = both[64:128].astype(F32)
        first, second = mid[:, 0:cols], mid[:, wide : wide + cols]
        rsum = jnp.where(lane == 8 + k, jnp.sum(first, axis=1, keepdims=True), rsum)
        rsum = jnp.where(lane == 16 + k, jnp.sum(second, axis=1, keepdims=True), rsum)
        return gsum + first + second, rsum

    gsum, rsum = lax.fori_loop(
        0, 8, spread, (jnp.zeros((64, cols), F32), jnp.zeros((64, 128), F32))
    )

    ma = lax.broadcasted_iota(jnp.int32, (wide, 128), 0)
    cut_low = jnp.logical_and(ma < 8, col == 0)
    cut_high = jnp.logical_and(jnp.logical_and(ma >= cols - 8, ma < cols), col == nc - 1)
    m3[:, 0:128] = jnp.where(cut_low, 0.0, 1.0).astype(BF16)
    m3[:, 128:256] = jnp.ones((wide, 128), BF16)
    m3[:, 256:384] = jnp.where(cut_high, 0.0, 1.0).astype(BF16)

    rowbuf[...] = jnp.zeros_like(rowbuf)
    colbuf[...] = jnp.zeros_like(colbuf)
    rowbuf[16:32, 0:64] = row_ref[...].astype(F32)
    colbuf[8 : 8 + cols, 0:64] = col_ref[...].astype(F32)
    colbuf[392:400, 0:64] = col_ref[0:16].astype(F32)[0:8]
    for copy in feats:
        copy.wait_recv()
    rowbuf[0:16, 0:64] = jnp.where(row > 0, rrecv[0].astype(F32), 0.0)
    rowbuf[32:48, 0:64] = jnp.where(row < n - 1, rrecv[1].astype(F32), 0.0)
    left = jnp.where(col > 0, crecv[0].astype(F32), 0.0)
    colbuf[376:392, 0:64] = left
    colbuf[0:8, 0:64] = left[8:16]
    colbuf[264:280, 0:64] = jnp.where(col < nc - 1, crecv[1].astype(F32), 0.0)

    a_all = jnp.zeros((192, 128), F32)
    for a in range(3):
        a_all += mm(
            k1_ref[a].reshape(192, 64), rowbuf[8 * a : 8 * a + 128, 0:64].astype(BF16), NT
        )
    for g in range(4):
        turned = a_all if g == 0 else pltpu.roll(a_all, 128 - 8 * g, 1)
        a_s[g] = turned
    b_all = jnp.zeros((192, wide), F32)
    for b in range(3):
        k1_b = jnp.concatenate([k1_ref[a, b] for a in range(3)], axis=0)
        b_all += mm(k1_b, colbuf[8 * b : 8 * b + wide, 0:64].astype(BF16), NT)
    eye = lax.broadcasted_iota(jnp.int32, (64, 64), 0) == lax.broadcasted_iota(jnp.int32, (64, 64), 1)
    bias = jnp.sum(jnp.where(eye, bias_ref[...], 0.0), axis=1, keepdims=True)
    b_s[...] = b_all

    lanes = lax.broadcasted_iota(jnp.int32, (1, wide), 1)
    on_left = jnp.logical_and(lanes >= wide - 8, col > 0)
    on_right = jnp.logical_and(jnp.logical_and(lanes >= cols, lanes < cols + 8), col < nc - 1)
    inside_cols = jnp.where(
        jnp.logical_or(lanes < cols, jnp.logical_or(on_left, on_right)), 1.0, 0.0
    ).astype(F32)
    lane1 = lax.broadcasted_iota(jnp.int32, (1, 128), 1)
    low_cut = jnp.where(jnp.logical_and(lane1 < 8, col == 0), 1.0, 0.0).astype(F32)
    high_cut = jnp.where(jnp.logical_and(lane1 >= 120, col == nc - 1), 1.0, 0.0).astype(F32)
    total = rows * n
    lane3 = lax.rem(lax.broadcasted_iota(jnp.int32, (64, wide), 1), 128)
    t_s[...] = jnp.zeros_like(t_s)
    u_s[...] = jnp.zeros_like(u_s)

    def group(g, carry):
        start = row * rows + 8 * (g - 1)

        def flag(first):
            return jnp.where(jnp.logical_and(first >= 0, first < total), 1.0, 0.0).astype(F32)

        flags = [flag(start + 8 * (a - 1)) for a in range(3)]
        base = bias + sum(b_s[64 * a : 64 * a + 64] * flags[a] for a in range(3))
        inside = inside_cols * flag(start)
        a_g = a_s[g]
        a_low, a_high = a_g[0:64], a_g[128:192]
        a_sum = a_low + a_g[64:128] + a_high
        v = jnp.zeros((64, wide), F32)
        for k in range(8):
            mid = base + a_sum[:, k : k + 1]
            pre = jnp.concatenate(
                [
                    mid[:, 0:128] - a_low[:, k : k + 1] * low_cut,
                    mid[:, 128:256] - a_high[:, k : k + 1] * high_cut,
                    mid[:, 256:384],
                ],
                axis=1,
            )
            sig = 0.5 + 0.5 * jnp.tanh(0.5 * pre)
            kept = sig * inside
            act = pre * kept
            act_s[g, k] = act.astype(BF16)
            inner = zb[g, k] * (kept + act * (1.0 - sig))
            inn_s[64 * k : 64 * k + 64] = inner.astype(BF16)
            v = v + inner
        for a in range(3):
            u_s[64 * a : 64 * a + 64] += v * flags[a]
        sums = mm(inn_s[...], m3[...])
        t = t_s[...]
        for k in range(8):
            t = jnp.where(lane3 == 8 * g + k, sums[64 * k : 64 * k + 64], t)
        t_s[...] = t
        return carry

    lax.fori_loop(0, 4, group, 0)

    def second(k, acc):
        a0, a1, a2, a3 = act_s[0, k], act_s[1, k], act_s[2, k], act_s[3, k]
        low = jnp.concatenate([a2, a0, a2, a1], axis=0)
        high = jnp.concatenate([a3, a1, a3, a2], axis=0)
        return acc + mm(gs[k], jnp.concatenate([low, high], axis=1), NT)

    two = lax.fori_loop(0, 8, second, jnp.zeros((192, 256), F32))
    hi_half = lax.broadcasted_iota(jnp.int32, (192, 128), 1) >= 64
    two_taps = [two[:, 0:128], two[:, 128:256], pltpu.roll(two[:, 0:128], 64, 1)]

    t_all = jnp.concatenate([t_s[:, 0:128], t_s[:, 128:256], t_s[:, 256:384]], axis=0)
    t_b = t_all.astype(BF16)
    u_all = u_s[...]
    u_b = u_all.astype(BF16)
    by_col = [mm(u_b, colbuf[8 * b : 8 * b + wide].astype(BF16)) for b in range(3)]
    for a in range(3):
        by_row = mm(t_b, rowbuf[8 * a : 8 * a + 128].astype(BF16))
        for b in range(3):
            tap = by_row[64 * b : 64 * b + 64] + by_col[b][64 * a : 64 * a + 64]
            tap = jnp.where(hi_half[0:64], two_taps[a][64 * b : 64 * b + 64], tap)
            at = 64 * (3 * a + b)
            pk32[at : at + 64] = tap
            pk[at : at + 64] = tap.astype(BF16)
    if nc * share > 576:
        pk32[576:] = jnp.zeros((nc * share - 576, 128), F32)
        pk[576:] = jnp.zeros((nc * share - 576, 128), BF16)

    t_t = t_all.T
    xtra32[...] = jnp.zeros_like(xtra32)
    for a in range(3):
        part = mm(t_t.astype(BF16), k1_ref[a].reshape(192, 64))
        xtra32[8 * a : 8 * a + 32, 0:64] += part[0:32]
    xtra32[16:32, 0:64] += rsum.T[8:24]
    xtra32[48:49, 0:64] = jnp.sum(t_t, axis=0, keepdims=True)[:, 64:128]
    u_t = u_all.T.astype(BF16)
    parts = []
    for b in range(3):
        k1_b = jnp.concatenate([k1_ref[a, b] for a in range(3)], axis=0)
        parts.append(mm(u_t, k1_b))
    col_part = (
        jnp.concatenate([parts[0][8:], parts[0][:8]], axis=0)
        + parts[1]
        + jnp.concatenate([parts[2][wide - 8 :], parts[2][: wide - 8]], axis=0)
    )
    xtra32[64:80, 0:64] = col_part[cols : cols + 16]
    xtra32[80:96, 0:64] = col_part[wide - 16 : wide]
    xtra[...] = xtra32[...].astype(BF16)

    copies = []
    for d in range(1, nc):
        to = (row, col_peer(d))
        src = pk.at[pl.ds(pl.multiple_of(col_peer(d) * share, 16), share)]
        copies.append(remote(src, p_recv.at[d - 1], ps_sem.at[d - 1], pr_sem.at[d - 1], to))
        copies.append(remote(xtra, x_recv.at[d - 1], xs_sem.at[d - 1], xr_sem.at[d - 1], to))
    for copy in copies:
        copy.start()
    col_main = col_part[0:cols] + gsum.T
    for copy in copies:
        copy.wait_recv()
    mine = pk32[pl.ds(pl.multiple_of(col * share, 16), share)]
    line = xtra32[0:64]
    for d in range(1, nc):
        mine = mine + p_recv[d - 1].astype(F32)
        line = line + x_recv[d - 1, 0:64].astype(F32)
    from_left = jnp.where(col > 0, x_recv[0, 64:80].astype(F32), 0.0)
    from_right = jnp.where(col < nc - 1, x_recv[nc - 2, 80:96].astype(F32), 0.0)
    col_main = jnp.concatenate(
        [
            col_main[0:16] + from_left[:, 0:64],
            col_main[16 : cols - 16],
            col_main[cols - 16 :] + from_right[:, 0:64],
        ],
        axis=0,
    )

    dd32[0:share] = mine
    dd32[share : share + 128, 0:64] = col_main[0:128]
    dd32[share : share + 128, 64:128] = col_main[128:256]
    dd32[share + 128 : share + 144] = line[48:64]
    if n * chunk > share + 144:
        dd32[share + 144 :] = jnp.zeros((n * chunk - share - 144, 128), F32)
    dd[...] = dd32[...].astype(BF16)
    nb[...] = line[0:48].astype(BF16)
    scatter = []
    for d in range(1, n):
        src = dd.at[pl.ds(pl.multiple_of(row_peer(d) * chunk, 16), chunk)]
        scatter.append(remote(src, d_recv.at[d - 1], ds_sem.at[d - 1], dr_sem.at[d - 1], (row_peer(d), col)))
    near = [
        remote(nb.at[pl.ds(32, 16)], nb_recv.at[0], ns_sem.at[0], nr_sem.at[0], (row_peer(1), col)),
        remote(nb.at[pl.ds(0, 16)], nb_recv.at[1], ns_sem.at[1], nr_sem.at[1], (row_peer(n - 1), col)),
    ]
    for copy in scatter + near:
        copy.start()
    spot = pl.ds(pl.multiple_of(row * chunk, 16), chunk)
    done = dd32[spot]
    for copy in scatter:
        copy.wait_recv()
    for d in range(1, n):
        done = done + d_recv[d - 1].astype(F32)
    full[spot] = done.astype(BF16)
    gather = []
    for d in range(1, n):
        gather.append(remote(full.at[spot], full.at[spot], as_sem.at[d - 1], ar_sem.at[d - 1], (row_peer(d), col)))
    for copy in gather:
        copy.start()
    for copy in near:
        copy.wait_recv()
    low = jnp.where(row > 0, nb_recv[0].astype(F32), 0.0)
    high = jnp.where(row < n - 1, nb_recv[1].astype(F32), 0.0)
    rg_ref[...] = (line[16:32] + low + high)[:, 0:64] * (1.0 / math.sqrt(cols * nc))
    for d in range(1, n):
        other = pl.ds(pl.multiple_of(row_peer(n - d) * chunk, 16), chunk)
        remote(full.at[spot], full.at[other], as_sem.at[d - 1], ar_sem.at[d - 1], (row_peer(d), col)).wait_recv()

    own = pl.ds(pl.multiple_of(col * share, 16), share)
    last = []
    for d in range(1, nc):
        last.append(remote(full.at[pl.ds(0, share)], pfull.at[own], cs_sem.at[d - 1], cr_sem.at[d - 1], (row, col_peer(d))))
    for copy in last:
        copy.start()
    whole = 1.0 / math.sqrt(total * cols * nc)
    pfull[own] = full[0:share]
    tall = 1.0 / math.sqrt(total)
    cg_ref[0:128] = full[share : share + 128].astype(F32)[:, 0:64] * tall
    cg_ref[128:256] = full[share : share + 128].astype(F32)[:, 64:128] * tall
    gb_ref[...] = full[share + 128 : share + 144].astype(F32)[0:1, 0:64] * whole
    for d in range(1, nc):
        other = pl.ds(pl.multiple_of(col_peer(nc - d) * share, 16), share)
        remote(full.at[pl.ds(0, share)], pfull.at[other], cs_sem.at[d - 1], cr_sem.at[d - 1], (row, col_peer(d))).wait_recv()
    for a in range(3):
        for b in range(3):
            at = 64 * (3 * a + b)
            tap = pfull[at : at + 64].astype(F32) * whole
            g1_ref[a, b] = tap[:, 0:64]
            g2_ref[a, b] = tap[:, 64:128]
    for copy in feats + copies + scatter + near + gather + last:
        copy.wait_send()


def shards(n, nc, grad_out, row_feat, col_feat, conv_one, bias_one, conv_two):
    share = round_up(-(-576 // nc), 16)
    chunk = round_up(-(-(share + 144) // n), 16)
    vmem = pl.BlockSpec(memory_space=pltpu.VMEM)
    dma = pltpu.SemaphoreType.DMA
    scratch = [
        pltpu.VMEM((160, 128), F32),
        pltpu.VMEM((400, 128), F32),
        pltpu.VMEM((2, 16, 64), BF16),
        pltpu.VMEM((2, 16, 64), BF16),
        pltpu.VMEM((8, 192, 768), BF16),
        pltpu.VMEM((4, 8, 64, 384), F32),
        pltpu.VMEM((4, 8, 64, 384), BF16),
        pltpu.VMEM((512, 384), BF16),
        pltpu.VMEM((4, 192, 128), F32),
        pltpu.VMEM((192, 384), F32),
        pltpu.VMEM((64, 384), F32),
        pltpu.VMEM((192, 384), F32),
        pltpu.VMEM((384, 384), BF16),
        pltpu.VMEM((nc * share, 128), BF16),
        pltpu.VMEM((nc * share, 128), F32),
        pltpu.VMEM((96, 128), BF16),
        pltpu.VMEM((96, 128), F32),
        pltpu.VMEM((nc - 1, share, 128), BF16),
        pltpu.VMEM((nc - 1, 96, 128), BF16),
        pltpu.VMEM((n * chunk, 128), BF16),
        pltpu.VMEM((n * chunk, 128), F32),
        pltpu.VMEM((48, 128), BF16),
        pltpu.VMEM((2, 16, 128), BF16),
        pltpu.VMEM((n - 1, chunk, 128), BF16),
        pltpu.VMEM((n * chunk, 128), BF16),
        pltpu.VMEM((nc * share, 128), BF16),
        dma((4,)), dma((4,)),
        dma((nc - 1,)), dma((nc - 1,)),
        dma((nc - 1,)), dma((nc - 1,)),
        dma((n - 1,)), dma((n - 1,)),
        dma((2,)), dma((2,)),
        dma((n - 1,)), dma((n - 1,)),
        dma((nc - 1,)), dma((nc - 1,)),
    ]
    out = pl.pallas_call(
        functools.partial(kernel, n, nc, share, chunk),
        out_shape=(
            jax.ShapeDtypeStruct((16, 64), F32),
            jax.ShapeDtypeStruct((256, 64), F32),
            jax.ShapeDtypeStruct((3, 3, 64, 64), F32),
            jax.ShapeDtypeStruct((1, 64), F32),
            jax.ShapeDtypeStruct((3, 3, 64, 64), F32),
        ),
        in_specs=[vmem] * 6,
        out_specs=(vmem,) * 5,
        scratch_shapes=scratch,
        compiler_params=pltpu.CompilerParams(
            collective_id=0, has_side_effects=True, vmem_limit_bytes=48 * 2**20
        ),
    )(grad_out, row_feat, col_feat, conv_one, bias_one.reshape(1, 64), conv_two)
    return (out[0], out[1], out[2], out[3].reshape(64), out[4])


def solution(mesh):
    n, nc = mesh.shape["row"], mesh.shape["col"]
    in_specs = (P(None, "row", "col"), P("row", None), P("col", None), P(), P(), P())
    out_specs = (P("row", None), P("col", None), P(), P(), P())
    return jax.shard_map(
        functools.partial(shards, n, nc), mesh=mesh, in_specs=in_specs, out_specs=out_specs, check_vma=False
    )
```

```python
import functools
import math

import jax
import jax.numpy as jnp
from jax import lax
from jax.experimental import pallas as pl
from jax.experimental.pallas import tpu as pltpu
from jax.sharding import PartitionSpec as P

F32 = jnp.float32
BF16 = jnp.bfloat16
MESH = pl.DeviceIdType.MESH
NN = (((1,), (0,)), ((), ()))
NT = (((1,), (1,)), ((), ()))


def mm(x, y, dims=NN):
    return lax.dot_general(x, y, dims, preferred_element_type=F32)


def round_up(value, unit):
    return -(-value // unit) * unit


def kernel(
    n, nc, share, chunk,
    g_hbm, row_hbm, col_hbm, k1_hbm, bias_hbm, k2_hbm,
    rg_ref, full, pfull,
    g_ref, row_ref, col_ref, k1_ref, bias_ref, k2_ref, csend, in_sem, k1t, k2t,
    rowbuf, colbuf, rrecv, crecv,
    gs, zb, act_s, inn_s, a_s, b_s, t_s, u_s, m3,
    pk, pk32, xtra, xtra32, p_recv, x_recv,
    dd, dd32, nb, nb_recv, d_recv,
    fs_sem, fr_sem, ps_sem, pr_sem, xs_sem, xr_sem,
    ds_sem, dr_sem, ns_sem, nr_sem, as_sem, ar_sem, cs_sem, cr_sem,
):
    row = lax.axis_index("row")
    col = lax.axis_index("col")
    rows, cols, wide = 16, 256, 384

    def row_peer(d):
        return lax.rem(row + d, n)

    def col_peer(d):
        return lax.rem(col + d, nc)

    loads = [
        pltpu.make_async_copy(src, dst, in_sem.at[i])
        for i, (src, dst) in enumerate(
            [(g_hbm, g_ref), (row_hbm, row_ref), (col_hbm, col_ref), (k1_hbm, k1_ref), (bias_hbm, bias_ref), (k2_hbm, k2_ref)]
        )
    ]
    for load in loads:
        load.start()
    barrier = pltpu.get_barrier_semaphore()
    for d in range(1, n):
        pl.semaphore_signal(barrier, inc=1, device_id=(row_peer(d), col), device_id_type=MESH)
    for d in range(1, nc):
        pl.semaphore_signal(barrier, inc=1, device_id=(row, col_peer(d)), device_id_type=MESH)

    def remote(src, dst, send, recv, to):
        return pltpu.make_async_remote_copy(
            src_ref=src, dst_ref=dst, send_sem=send, recv_sem=recv, device_id=to, device_id_type=MESH
        )

    pa = lax.broadcasted_iota(jnp.int32, (256, 256), 0)
    pb = lax.broadcasted_iota(jnp.int32, (256, 256), 1)
    perm = ((pa & 15) * 16 + (pa >> 4) == pb).astype(F32).astype(BF16)
    sa = lax.broadcasted_iota(jnp.int32, (256, wide), 0)
    sb = lax.broadcasted_iota(jnp.int32, (256, wide), 1)
    gap = sb - sa
    shifts = jnp.concatenate(
        [
            jnp.logical_or(gap == -8, gap == wide - 8).astype(F32).astype(BF16),
            (gap == 0).astype(F32).astype(BF16),
            (gap == 8).astype(F32).astype(BF16),
        ],
        axis=1,
    )
    rowbuf[...] = jnp.zeros_like(rowbuf)
    colbuf[...] = jnp.zeros_like(colbuf)
    loads[1].wait()
    loads[2].wait()
    rowbuf[16:32, 0:64] = row_ref[...].astype(F32)
    col_t = col_ref[...].astype(F32).T
    colbuf[8 : 8 + cols, 0:64] = col_t
    colbuf[392:400, 0:64] = col_t[0:8]
    csend[0] = col_t[cols - 16 : cols].astype(BF16)
    csend[1] = col_t[0:16].astype(BF16)
    loads[0].wait()

    def build(og, carry):
        x = g_ref[pl.ds(og * 16, 16)].reshape(256, cols)
        y = mm(mm(perm, x).astype(BF16), shifts).astype(BF16)
        for r in range(rows):
            h, k = r // 8, r % 8
            for b in range(3):
                gs[k, pl.ds(pl.multiple_of(b * 64 + og * 16, 16), 16), h * wide : (h + 1) * wide] = y[
                    16 * r : 16 * r + 16, b * wide : (b + 1) * wide
                ]
        return carry

    lax.fori_loop(0, 4, build, 0)

    pl.semaphore_wait(barrier, (n - 1) + (nc - 1))
    feats = [
        remote(row_ref, rrecv.at[0], fs_sem.at[0], fr_sem.at[0], (row_peer(1), col)),
        remote(row_ref, rrecv.at[1], fs_sem.at[1], fr_sem.at[1], (row_peer(n - 1), col)),
        remote(csend.at[0], crecv.at[0], fs_sem.at[2], fr_sem.at[2], (row, col_peer(1))),
        remote(csend.at[1], crecv.at[1], fs_sem.at[3], fr_sem.at[3], (row, col_peer(nc - 1))),
    ]
    for copy in feats:
        copy.start()

    for load in loads[3:]:
        load.wait()
    for a in range(3):
        k2t[64 * a : 64 * a + 64] = k2_ref[a].reshape(192, 64).astype(F32).T.astype(BF16)
    w2 = k2t[...]
    lane = lax.broadcasted_iota(jnp.int32, (64, 128), 1)

    def spread(k, carry):
        gsum, rsum = carry
        both = gs[k]
        z = mm(w2, both)
        lo, hi = z[:, :wide], z[:, wide:]
        zb[0, k] = lo[0:64]
        zb[1, k] = lo[64:128] + hi[0:64]
        zb[2, k] = lo[128:192] + hi[64:128]
        zb[3, k] = hi[128:192]
        mid = both[64:128].astype(F32)
        first, second = mid[:, 0:cols], mid[:, wide : wide + cols]
        rsum = jnp.where(lane == 8 + k, jnp.sum(first, axis=1, keepdims=True), rsum)
        rsum = jnp.where(lane == 16 + k, jnp.sum(second, axis=1, keepdims=True), rsum)
        return gsum + first + second, rsum

    gsum, rsum = lax.fori_loop(
        0, 8, spread, (jnp.zeros((64, cols), F32), jnp.zeros((64, 128), F32))
    )

    ma = lax.broadcasted_iota(jnp.int32, (wide, 128), 0)
    cut_low = jnp.logical_and(ma < 8, col == 0)
    cut_high = jnp.logical_and(jnp.logical_and(ma >= cols - 8, ma < cols), col == nc - 1)
    m3[:, 0:128] = jnp.ones((wide, 128), BF16)
    m3[:, 128:256] = jnp.where(jnp.logical_or(cut_low, cut_high), 1.0, 0.0).astype(BF16)
    for b in range(3):
        k1_b = jnp.concatenate([k1_ref[a, b] for a in range(3)], axis=0)
        k1t[b] = k1_b.astype(F32).T.astype(BF16)
    for copy in feats:
        copy.wait_recv()
    rowbuf[0:16, 0:64] = jnp.where(row > 0, rrecv[0].astype(F32), 0.0)
    rowbuf[32:48, 0:64] = jnp.where(row < n - 1, rrecv[1].astype(F32), 0.0)
    left = jnp.where(col > 0, crecv[0].astype(F32), 0.0)
    colbuf[376:392, 0:64] = left
    colbuf[0:8, 0:64] = left[8:16]
    colbuf[264:280, 0:64] = jnp.where(col < nc - 1, crecv[1].astype(F32), 0.0)

    a_all = jnp.zeros((192, 128), F32)
    for a in range(3):
        a_all += mm(
            k1_ref[a].reshape(192, 64), rowbuf[8 * a : 8 * a + 128, 0:64].astype(BF16), NT
        )
    for g in range(4):
        turned = a_all if g == 0 else pltpu.roll(a_all, 128 - 8 * g, 1)
        a_s[g] = turned
    b_all = jnp.zeros((192, wide), F32)
    for b in range(3):
        k1_b = jnp.concatenate([k1_ref[a, b] for a in range(3)], axis=0)
        b_all += mm(k1_b, colbuf[8 * b : 8 * b + wide, 0:64].astype(BF16), NT)
    eye = lax.broadcasted_iota(jnp.int32, (64, 64), 0) == lax.broadcasted_iota(jnp.int32, (64, 64), 1)
    bias = jnp.sum(jnp.where(eye, bias_ref[...], 0.0), axis=1, keepdims=True)
    b_s[...] = b_all

    lanes = lax.broadcasted_iota(jnp.int32, (1, wide), 1)
    on_left = jnp.logical_and(lanes >= wide - 8, col > 0)
    on_right = jnp.logical_and(jnp.logical_and(lanes >= cols, lanes < cols + 8), col < nc - 1)
    inside_cols = jnp.where(
        jnp.logical_or(lanes < cols, jnp.logical_or(on_left, on_right)), 1.0, 0.0
    ).astype(F32)
    lane1 = lax.broadcasted_iota(jnp.int32, (1, 128), 1)
    low_cut = jnp.where(jnp.logical_and(lane1 < 8, col == 0), 1.0, 0.0).astype(F32)
    high_cut = jnp.where(jnp.logical_and(lane1 >= 120, col == nc - 1), 1.0, 0.0).astype(F32)
    total = rows * n
    lane2 = lax.broadcasted_iota(jnp.int32, (64, 256), 1) & 127
    t_s[...] = jnp.zeros_like(t_s)
    u_s[...] = jnp.zeros_like(u_s)

    def group(g, carry):
        start = row * rows + 8 * (g - 1)

        def flag(first):
            return jnp.where(jnp.logical_and(first >= 0, first < total), 1.0, 0.0).astype(F32)

        flags = [flag(start + 8 * (a - 1)) for a in range(3)]
        base = bias + sum(b_s[64 * a : 64 * a + 64] * flags[a] for a in range(3))
        inside = inside_cols * flag(start)
        a_g = a_s[g]
        a_low, a_high = a_g[0:64], a_g[128:192]
        a_sum = a_low + a_g[64:128] + a_high
        cuts = [(a_low, low_cut), (a_high, high_cut), None]
        for tile in range(3):
            at = slice(128 * tile, 128 * tile + 128)
            v = jnp.zeros((64, 128), F32)
            for k in range(8):
                pre = base[:, at] + a_sum[:, k : k + 1]
                if cuts[tile] is not None:
                    pre = pre - cuts[tile][0][:, k : k + 1] * cuts[tile][1]
                sig = 0.5 + 0.5 * jnp.tanh(0.5 * pre)
                kept = sig * inside[:, at] if tile == 2 else sig * flag(start)
                act = pre * kept
                act_s[g, k, :, at] = act.astype(BF16)
                inner = zb[g, k, :, at] * (kept + act * (1.0 - sig))
                inn_s[64 * k : 64 * k + 64, at] = inner.astype(BF16)
                v = v + inner
            for a in range(3):
                u_s[64 * a : 64 * a + 64, at] += v * flags[a]
        sums = mm(inn_s[...], m3[...])
        t = t_s[...]
        for k in range(8):
            t = jnp.where(lane2 == 8 * g + k, sums[64 * k : 64 * k + 64], t)
        t_s[...] = t
        return carry

    lax.fori_loop(0, 4, group, 0)

    def second(k, acc):
        a0, a1, a2, a3 = act_s[0, k], act_s[1, k], act_s[2, k], act_s[3, k]
        low = jnp.concatenate([a2, a0, a2, a1], axis=0)
        high = jnp.concatenate([a3, a1, a3, a2], axis=0)
        return acc + mm(gs[k], jnp.concatenate([low, high], axis=1), NT)

    two = lax.fori_loop(0, 8, second, jnp.zeros((192, 256), F32))
    hi_half = lax.broadcasted_iota(jnp.int32, (192, 128), 1) >= 64
    two_taps = [two[:, 0:128], two[:, 128:256], pltpu.roll(two[:, 0:128], 64, 1)]

    t_mid, t_cut = t_s[:, 0:128], t_s[:, 128:256]
    t_all = jnp.concatenate(
        [jnp.where(col == 0, t_mid - t_cut, t_mid), t_mid, jnp.where(col == nc - 1, t_mid - t_cut, t_mid)], axis=0
    )
    t_b = t_all.astype(BF16)
    u_all = u_s[...]
    u_b = u_all.astype(BF16)
    by_col = [mm(u_b, colbuf[8 * b : 8 * b + wide].astype(BF16)) for b in range(3)]
    for a in range(3):
        by_row = mm(t_b, rowbuf[8 * a : 8 * a + 128].astype(BF16))
        for b in range(3):
            tap = by_row[64 * b : 64 * b + 64] + by_col[b][64 * a : 64 * a + 64]
            tap = jnp.where(hi_half[0:64], two_taps[a][64 * b : 64 * b + 64], tap)
            at = 64 * (3 * a + b)
            pk32[at : at + 64] = tap
            pk[at : at + 64] = tap.astype(BF16)
    if nc * share > 576:
        pk32[576:] = jnp.zeros((nc * share - 576, 128), F32)
        pk[576:] = jnp.zeros((nc * share - 576, 128), BF16)

    t_t = t_all.T
    xtra32[...] = jnp.zeros_like(xtra32)
    for a in range(3):
        part = mm(t_t.astype(BF16), k1_ref[a].reshape(192, 64))
        xtra32[8 * a : 8 * a + 32, 0:64] += part[0:32]
    xtra32[16:32, 0:64] += rsum.T[8:24]
    xtra32[48:49, 0:64] = jnp.sum(t_t, axis=0, keepdims=True)[:, 64:128]
    parts = [mm(k1t[b], u_b) for b in range(3)]
    col_part = pltpu.roll(parts[0], wide - 8, 1) + parts[1] + pltpu.roll(parts[2], 8, 1)
    xtra32[64:128] = col_part[:, cols:wide]
    xtra[...] = xtra32[...].astype(BF16)

    copies = []
    for d in range(1, nc):
        to = (row, col_peer(d))
        src = pk.at[pl.ds(pl.multiple_of(col_peer(d) * share, 16), share)]
        copies.append(remote(src, p_recv.at[d - 1], ps_sem.at[d - 1], pr_sem.at[d - 1], to))
        copies.append(remote(xtra, x_recv.at[d - 1], xs_sem.at[d - 1], xr_sem.at[d - 1], to))
    for copy in copies:
        copy.start()
    col_main = col_part[:, 0:cols] + gsum
    for copy in copies:
        copy.wait_recv()
    mine = pk32[pl.ds(pl.multiple_of(col * share, 16), share)]
    line = xtra32[0:64]
    for d in range(1, nc):
        mine = mine + p_recv[d - 1].astype(F32)
        line = line + x_recv[d - 1, 0:64].astype(F32)
    side = lax.broadcasted_iota(jnp.int32, (64, 128), 1)
    from_left = jnp.where(jnp.logical_and(side < 16, col > 0), x_recv[0, 64:128].astype(F32), 0.0)
    from_right = jnp.where(jnp.logical_and(side >= 112, col < nc - 1), x_recv[nc - 2, 64:128].astype(F32), 0.0)

    dd32[0:share] = mine
    dd32[share : share + 64] = col_main[:, 0:128] + from_left
    dd32[share + 64 : share + 128] = col_main[:, 128:256] + from_right
    dd32[share + 128 : share + 144] = line[48:64]
    if n * chunk > share + 144:
        dd32[share + 144 :] = jnp.zeros((n * chunk - share - 144, 128), F32)
    dd[...] = dd32[...].astype(BF16)
    nb[...] = line[0:48].astype(BF16)
    scatter = []
    for d in range(1, n):
        src = dd.at[pl.ds(pl.multiple_of(row_peer(d) * chunk, 16), chunk)]
        scatter.append(remote(src, d_recv.at[d - 1], ds_sem.at[d - 1], dr_sem.at[d - 1], (row_peer(d), col)))
    near = [
        remote(nb.at[pl.ds(32, 16)], nb_recv.at[0], ns_sem.at[0], nr_sem.at[0], (row_peer(1), col)),
        remote(nb.at[pl.ds(0, 16)], nb_recv.at[1], ns_sem.at[1], nr_sem.at[1], (row_peer(n - 1), col)),
    ]
    for copy in scatter + near:
        copy.start()
    spot = pl.ds(pl.multiple_of(row * chunk, 16), chunk)
    done = dd32[spot]
    for copy in scatter:
        copy.wait_recv()
    for d in range(1, n):
        done = done + d_recv[d - 1].astype(F32)
    full[spot] = done.astype(BF16)
    gather = []
    for d in range(1, n):
        gather.append(remote(full.at[spot], full.at[spot], as_sem.at[d - 1], ar_sem.at[d - 1], (row_peer(d), col)))
    for copy in gather:
        copy.start()
    for copy in near:
        copy.wait_recv()
    low = jnp.where(row > 0, nb_recv[0].astype(F32), 0.0)
    high = jnp.where(row < n - 1, nb_recv[1].astype(F32), 0.0)
    rg_ref[...] = line[16:32] + low + high
    for d in range(1, n):
        other = pl.ds(pl.multiple_of(row_peer(n - d) * chunk, 16), chunk)
        remote(full.at[spot], full.at[other], as_sem.at[d - 1], ar_sem.at[d - 1], (row_peer(d), col)).wait_recv()

    own = pl.ds(pl.multiple_of(col * share, 16), share)
    last = []
    for d in range(1, nc):
        last.append(remote(full.at[pl.ds(0, share)], pfull.at[own], cs_sem.at[d - 1], cr_sem.at[d - 1], (row, col_peer(d))))
    for copy in last:
        copy.start()
    pfull[own] = full[0:share]
    for d in range(1, nc):
        other = pl.ds(pl.multiple_of(col_peer(nc - d) * share, 16), share)
        remote(full.at[pl.ds(0, share)], pfull.at[other], cs_sem.at[d - 1], cr_sem.at[d - 1], (row, col_peer(d))).wait_recv()
    for copy in feats + copies + scatter + near + gather + last:
        copy.wait_send()


def finish(n, nc, share, rg_in, full, pfull, rg_ref, cg_ref, g1_ref, gb_ref, g2_ref):
    whole = 1.0 / math.sqrt(16 * n * 256 * nc)
    tall = 1.0 / math.sqrt(16 * n)
    rg_ref[...] = rg_in[:, 0:64] * (1.0 / math.sqrt(256 * nc))
    cg_ref[:, 0:128] = full[share : share + 64].astype(F32) * tall
    cg_ref[:, 128:256] = full[share + 64 : share + 128].astype(F32) * tall
    gb_ref[...] = full[share + 128 : share + 144].astype(F32)[0:1, 0:64] * whole
    for a in range(3):
        for b in range(3):
            at = 64 * (3 * a + b)
            tap = pfull[at : at + 64].astype(F32) * whole
            g1_ref[a, b] = tap[:, 0:64]
            g2_ref[a, b] = tap[:, 64:128]


def shards(n, nc, grad_out, row_feat, col_feat, conv_one, bias_one, conv_two):
    share = round_up(-(-576 // nc), 16)
    chunk = round_up(-(-(share + 144) // n), 16)
    vmem = pl.BlockSpec(memory_space=pltpu.VMEM)
    dma = pltpu.SemaphoreType.DMA
    scratch = [
        pltpu.VMEM((64, 16, 256), BF16),
        pltpu.VMEM((16, 64), BF16),
        pltpu.VMEM((64, 256), BF16),
        pltpu.VMEM((3, 3, 64, 64), BF16),
        pltpu.VMEM((1, 64), F32),
        pltpu.VMEM((3, 3, 64, 64), BF16),
        pltpu.VMEM((2, 16, 64), BF16),
        dma((6,)),
        pltpu.VMEM((3, 64, 192), BF16),
        pltpu.VMEM((192, 192), BF16),
        pltpu.VMEM((160, 128), F32),
        pltpu.VMEM((400, 128), F32),
        pltpu.VMEM((2, 16, 64), BF16),
        pltpu.VMEM((2, 16, 64), BF16),
        pltpu.VMEM((8, 192, 768), BF16),
        pltpu.VMEM((4, 8, 64, 384), F32),
        pltpu.VMEM((4, 8, 64, 384), BF16),
        pltpu.VMEM((512, 384), BF16),
        pltpu.VMEM((4, 192, 128), F32),
        pltpu.VMEM((192, 384), F32),
        pltpu.VMEM((64, 256), F32),
        pltpu.VMEM((192, 384), F32),
        pltpu.VMEM((384, 256), BF16),
        pltpu.VMEM((nc * share, 128), BF16),
        pltpu.VMEM((nc * share, 128), F32),
        pltpu.VMEM((128, 128), BF16),
        pltpu.VMEM((128, 128), F32),
        pltpu.VMEM((nc - 1, share, 128), BF16),
        pltpu.VMEM((nc - 1, 128, 128), BF16),
        pltpu.VMEM((n * chunk, 128), BF16),
        pltpu.VMEM((n * chunk, 128), F32),
        pltpu.VMEM((48, 128), BF16),
        pltpu.VMEM((2, 16, 128), BF16),
        pltpu.VMEM((n - 1, chunk, 128), BF16),
        dma((4,)), dma((4,)),
        dma((nc - 1,)), dma((nc - 1,)),
        dma((nc - 1,)), dma((nc - 1,)),
        dma((n - 1,)), dma((n - 1,)),
        dma((2,)), dma((2,)),
        dma((n - 1,)), dma((n - 1,)),
        dma((nc - 1,)), dma((nc - 1,)),
    ]
    sums = pl.pallas_call(
        functools.partial(kernel, n, nc, share, chunk),
        out_shape=(
            jax.ShapeDtypeStruct((16, 128), F32),
            jax.ShapeDtypeStruct((n * chunk, 128), BF16),
            jax.ShapeDtypeStruct((nc * share, 128), BF16),
        ),
        in_specs=[pl.BlockSpec(memory_space=pltpu.HBM)] * 6,
        out_specs=(vmem,) * 3,
        scratch_shapes=scratch,
        compiler_params=pltpu.CompilerParams(
            collective_id=0, has_side_effects=True, vmem_limit_bytes=60 * 2**20
        ),
    )(grad_out, row_feat, col_feat.T, conv_one, bias_one.reshape(1, 64), conv_two)
    out = pl.pallas_call(
        functools.partial(finish, n, nc, share),
        out_shape=(
            jax.ShapeDtypeStruct((16, 64), F32),
            jax.ShapeDtypeStruct((64, 256), F32),
            jax.ShapeDtypeStruct((3, 3, 64, 64), F32),
            jax.ShapeDtypeStruct((1, 64), F32),
            jax.ShapeDtypeStruct((3, 3, 64, 64), F32),
        ),
        in_specs=[vmem] * 3,
        out_specs=(vmem,) * 5,
        compiler_params=pltpu.CompilerParams(vmem_limit_bytes=60 * 2**20),
    )(*sums)
    return (out[0], out[1].T, out[2], out[3].reshape(64), out[4])


def solution(mesh):
    n, nc = mesh.shape["row"], mesh.shape["col"]
    in_specs = (P(None, "row", "col"), P("row", None), P("col", None), P(), P(), P())
    out_specs = (P("row", None), P("col", None), P(), P(), P())
    return jax.shard_map(
        functools.partial(shards, n, nc), mesh=mesh, in_specs=in_specs, out_specs=out_specs, check_vma=False
    )
```

```python
import functools
import math

import jax
import jax.numpy as jnp
from jax import lax
from jax.experimental import pallas as pl
from jax.experimental.pallas import tpu as pltpu
from jax.sharding import PartitionSpec as P

F32 = jnp.float32
BF16 = jnp.bfloat16
MESH = pl.DeviceIdType.MESH
NN = (((1,), (0,)), ((), ()))
NT = (((1,), (1,)), ((), ()))


def mm(x, y, dims=NN):
    return lax.dot_general(x, y, dims, preferred_element_type=F32)


def round_up(value, unit):
    return -(-value // unit) * unit


def kernel(
    n, nc, share, chunk,
    g_hbm, row_hbm, col_hbm, k1_hbm, bias_hbm, k2_hbm,
    rg_ref, full, pfull,
    g_ref, row_ref, col_ref, k1_ref, bias_ref, k2_ref, csend, in_sem, k1t, k2t,
    rowbuf, colbuf, rrecv, crecv,
    gs, zb, act_s, inn_s, a_s, b_s, t_s, u_s, m3,
    pk, pk32, xtra, xtra32, p_recv, x_recv,
    dd, dd32, nb, nb_recv, d_recv,
    fs_sem, fr_sem, ps_sem, pr_sem, xs_sem, xr_sem,
    ds_sem, dr_sem, ns_sem, nr_sem, as_sem, ar_sem, cs_sem, cr_sem,
):
    row = lax.axis_index("row")
    col = lax.axis_index("col")
    rows, cols, wide = 16, 256, 384

    def row_peer(d):
        return lax.rem(row + d, n)

    def col_peer(d):
        return lax.rem(col + d, nc)

    loads = [
        pltpu.make_async_copy(src, dst, in_sem.at[i])
        for i, (src, dst) in enumerate(
            [(g_hbm, g_ref), (row_hbm, row_ref), (col_hbm, col_ref), (k1_hbm, k1_ref), (bias_hbm, bias_ref), (k2_hbm, k2_ref)]
        )
    ]
    for load in loads:
        load.start()
    barrier = pltpu.get_barrier_semaphore()
    for d in range(1, n):
        pl.semaphore_signal(barrier, inc=1, device_id=(row_peer(d), col), device_id_type=MESH)
    for d in range(1, nc):
        pl.semaphore_signal(barrier, inc=1, device_id=(row, col_peer(d)), device_id_type=MESH)

    def remote(src, dst, send, recv, to):
        return pltpu.make_async_remote_copy(
            src_ref=src, dst_ref=dst, send_sem=send, recv_sem=recv, device_id=to, device_id_type=MESH
        )

    pa = lax.broadcasted_iota(jnp.int32, (256, 256), 0)
    pb = lax.broadcasted_iota(jnp.int32, (256, 256), 1)
    perm = ((pa & 15) * 16 + (pa >> 4) == pb).astype(F32).astype(BF16)
    sa = lax.broadcasted_iota(jnp.int32, (256, wide), 0)
    sb = lax.broadcasted_iota(jnp.int32, (256, wide), 1)
    gap = sb - sa
    shifts = jnp.concatenate(
        [
            jnp.logical_or(gap == -8, gap == wide - 8).astype(F32).astype(BF16),
            (gap == 0).astype(F32).astype(BF16),
            (gap == 8).astype(F32).astype(BF16),
        ],
        axis=1,
    )
    rowbuf[...] = jnp.zeros_like(rowbuf)
    colbuf[...] = jnp.zeros_like(colbuf)
    loads[1].wait()
    loads[2].wait()
    rowbuf[16:32, 0:64] = row_ref[...].astype(F32)
    col_t = col_ref[...].astype(F32).T
    colbuf[8 : 8 + cols, 0:64] = col_t
    colbuf[392:400, 0:64] = col_t[0:8]
    csend[0] = col_t[cols - 16 : cols].astype(BF16)
    csend[1] = col_t[0:16].astype(BF16)
    loads[0].wait()

    def build(og, carry):
        x = g_ref[pl.ds(og * 16, 16)].reshape(256, cols)
        y = mm(mm(perm, x).astype(BF16), shifts).astype(BF16)
        for r in range(rows):
            h, k = r // 8, r % 8
            for b in range(3):
                gs[k, pl.ds(pl.multiple_of(b * 64 + og * 16, 16), 16), h * wide : (h + 1) * wide] = y[
                    16 * r : 16 * r + 16, b * wide : (b + 1) * wide
                ]
        return carry

    lax.fori_loop(0, 4, build, 0, unroll=True)

    pl.semaphore_wait(barrier, (n - 1) + (nc - 1))
    feats = [
        remote(row_ref, rrecv.at[0], fs_sem.at[0], fr_sem.at[0], (row_peer(1), col)),
        remote(row_ref, rrecv.at[1], fs_sem.at[1], fr_sem.at[1], (row_peer(n - 1), col)),
        remote(csend.at[0], crecv.at[0], fs_sem.at[2], fr_sem.at[2], (row, col_peer(1))),
        remote(csend.at[1], crecv.at[1], fs_sem.at[3], fr_sem.at[3], (row, col_peer(nc - 1))),
    ]
    for copy in feats:
        copy.start()

    for load in loads[3:]:
        load.wait()
    for a in range(3):
        k2t[64 * a : 64 * a + 64] = k2_ref[a].reshape(192, 64).astype(F32).T.astype(BF16)
    w2 = k2t[...]
    lane = lax.broadcasted_iota(jnp.int32, (64, 128), 1)

    def spread(k, carry):
        gsum, rsum = carry
        both = gs[k]
        z = mm(w2, both)
        lo, hi = z[:, :wide], z[:, wide:]
        zb[0, k] = lo[0:64]
        zb[1, k] = lo[64:128] + hi[0:64]
        zb[2, k] = lo[128:192] + hi[64:128]
        zb[3, k] = hi[128:192]
        mid = both[64:128].astype(F32)
        first, second = mid[:, 0:cols], mid[:, wide : wide + cols]
        rsum = jnp.where(lane == 8 + k, jnp.sum(first, axis=1, keepdims=True), rsum)
        rsum = jnp.where(lane == 16 + k, jnp.sum(second, axis=1, keepdims=True), rsum)
        return gsum + first + second, rsum

    gsum, rsum = lax.fori_loop(
        0, 8, spread, (jnp.zeros((64, cols), F32), jnp.zeros((64, 128), F32)), unroll=4
    )

    ma = lax.broadcasted_iota(jnp.int32, (wide, 128), 0)
    cut_low = jnp.logical_and(ma < 8, col == 0)
    cut_high = jnp.logical_and(jnp.logical_and(ma >= cols - 8, ma < cols), col == nc - 1)
    m3[:, 0:128] = jnp.ones((wide, 128), BF16)
    m3[:, 128:256] = jnp.where(jnp.logical_or(cut_low, cut_high), 1.0, 0.0).astype(BF16)
    for b in range(3):
        k1_b = jnp.concatenate([k1_ref[a, b] for a in range(3)], axis=0)
        k1t[b] = k1_b.astype(F32).T.astype(BF16)
    for copy in feats:
        copy.wait_recv()
    rowbuf[0:16, 0:64] = jnp.where(row > 0, rrecv[0].astype(F32), 0.0)
    rowbuf[32:48, 0:64] = jnp.where(row < n - 1, rrecv[1].astype(F32), 0.0)
    left = jnp.where(col > 0, crecv[0].astype(F32), 0.0)
    colbuf[376:392, 0:64] = left
    colbuf[0:8, 0:64] = left[8:16]
    colbuf[264:280, 0:64] = jnp.where(col < nc - 1, crecv[1].astype(F32), 0.0)

    a_all = jnp.zeros((192, 128), F32)
    for a in range(3):
        a_all += mm(
            k1_ref[a].reshape(192, 64), rowbuf[8 * a : 8 * a + 128, 0:64].astype(BF16), NT
        )
    for g in range(4):
        turned = a_all if g == 0 else pltpu.roll(a_all, 128 - 8 * g, 1)
        a_s[g] = turned
    b_all = jnp.zeros((192, wide), F32)
    for b in range(3):
        k1_b = jnp.concatenate([k1_ref[a, b] for a in range(3)], axis=0)
        b_all += mm(k1_b, colbuf[8 * b : 8 * b + wide, 0:64].astype(BF16), NT)
    eye = lax.broadcasted_iota(jnp.int32, (64, 64), 0) == lax.broadcasted_iota(jnp.int32, (64, 64), 1)
    bias = jnp.sum(jnp.where(eye, bias_ref[...], 0.0), axis=1, keepdims=True)
    b_s[...] = b_all

    lanes = lax.broadcasted_iota(jnp.int32, (1, wide), 1)
    on_left = jnp.logical_and(lanes >= wide - 8, col > 0)
    on_right = jnp.logical_and(jnp.logical_and(lanes >= cols, lanes < cols + 8), col < nc - 1)
    inside_cols = jnp.where(
        jnp.logical_or(lanes < cols, jnp.logical_or(on_left, on_right)), 1.0, 0.0
    ).astype(F32)
    lane1 = lax.broadcasted_iota(jnp.int32, (1, 128), 1)
    low_cut = jnp.where(jnp.logical_and(lane1 < 8, col == 0), 1.0, 0.0).astype(F32)
    high_cut = jnp.where(jnp.logical_and(lane1 >= 120, col == nc - 1), 1.0, 0.0).astype(F32)
    total = rows * n
    lane2 = lax.broadcasted_iota(jnp.int32, (64, 256), 1) & 127
    t_s[...] = jnp.zeros_like(t_s)
    u_s[...] = jnp.zeros_like(u_s)

    def group(g, carry):
        start = row * rows + 8 * (g - 1)

        def flag(first):
            return jnp.where(jnp.logical_and(first >= 0, first < total), 1.0, 0.0).astype(F32)

        flags = [flag(start + 8 * (a - 1)) for a in range(3)]
        base = bias + sum(b_s[64 * a : 64 * a + 64] * flags[a] for a in range(3))
        inside = inside_cols * flag(start)
        a_g = a_s[g]
        a_low, a_high = a_g[0:64], a_g[128:192]
        a_sum = a_low + a_g[64:128] + a_high
        cuts = [(a_low, low_cut), (a_high, high_cut), None]
        for tile in range(3):
            at = slice(128 * tile, 128 * tile + 128)
            v = jnp.zeros((64, 128), F32)
            for k in range(8):
                pre = base[:, at] + a_sum[:, k : k + 1]
                if cuts[tile] is not None:
                    pre = pre - cuts[tile][0][:, k : k + 1] * cuts[tile][1]
                sig = 0.5 + 0.5 * jnp.tanh(0.5 * pre)
                kept = sig * inside[:, at] if tile == 2 else sig * flag(start)
                act = pre * kept
                act_s[g, k, :, at] = act.astype(BF16)
                inner = zb[g, k, :, at] * (kept + act * (1.0 - sig))
                inn_s[64 * k : 64 * k + 64, at] = inner.astype(BF16)
                v = v + inner
            for a in range(3):
                u_s[64 * a : 64 * a + 64, at] += v * flags[a]
        sums = mm(inn_s[...], m3[...])
        t = t_s[...]
        for k in range(8):
            t = jnp.where(lane2 == 8 * g + k, sums[64 * k : 64 * k + 64], t)
        t_s[...] = t
        return carry

    lax.fori_loop(0, 4, group, 0)

    def second(k, acc):
        a0, a1, a2, a3 = act_s[0, k], act_s[1, k], act_s[2, k], act_s[3, k]
        low = jnp.concatenate([a2, a0, a2, a1], axis=0)
        high = jnp.concatenate([a3, a1, a3, a2], axis=0)
        return acc + mm(gs[k], jnp.concatenate([low, high], axis=1), NT)

    two = lax.fori_loop(0, 8, second, jnp.zeros((192, 256), F32), unroll=True)
    hi_half = lax.broadcasted_iota(jnp.int32, (192, 128), 1) >= 64
    two_taps = [two[:, 0:128], two[:, 128:256], pltpu.roll(two[:, 0:128], 64, 1)]

    t_mid, t_cut = t_s[:, 0:128], t_s[:, 128:256]
    t_all = jnp.concatenate(
        [jnp.where(col == 0, t_mid - t_cut, t_mid), t_mid, jnp.where(col == nc - 1, t_mid - t_cut, t_mid)], axis=0
    )
    t_b = t_all.astype(BF16)
    u_all = u_s[...]
    u_b = u_all.astype(BF16)
    by_col = [mm(u_b, colbuf[8 * b : 8 * b + wide].astype(BF16)) for b in range(3)]
    for a in range(3):
        by_row = mm(t_b, rowbuf[8 * a : 8 * a + 128].astype(BF16))
        for b in range(3):
            tap = by_row[64 * b : 64 * b + 64] + by_col[b][64 * a : 64 * a + 64]
            tap = jnp.where(hi_half[0:64], two_taps[a][64 * b : 64 * b + 64], tap)
            at = 64 * (3 * a + b)
            pk32[at : at + 64] = tap
            pk[at : at + 64] = tap.astype(BF16)
    if nc * share > 576:
        pk32[576:] = jnp.zeros((nc * share - 576, 128), F32)
        pk[576:] = jnp.zeros((nc * share - 576, 128), BF16)

    t_t = t_all.T
    xtra32[...] = jnp.zeros_like(xtra32)
    for a in range(3):
        part = mm(t_t.astype(BF16), k1_ref[a].reshape(192, 64))
        xtra32[8 * a : 8 * a + 32, 0:64] += part[0:32]
    xtra32[16:32, 0:64] += rsum.T[8:24]
    xtra32[48:49, 0:64] = jnp.sum(t_t, axis=0, keepdims=True)[:, 64:128]
    parts = [mm(k1t[b], u_b) for b in range(3)]
    col_part = pltpu.roll(parts[0], wide - 8, 1) + parts[1] + pltpu.roll(parts[2], 8, 1)
    xtra32[64:128] = col_part[:, cols:wide]
    xtra[...] = xtra32[...].astype(BF16)

    copies = []
    for d in range(1, nc):
        to = (row, col_peer(d))
        src = pk.at[pl.ds(pl.multiple_of(col_peer(d) * share, 16), share)]
        copies.append(remote(src, p_recv.at[d - 1], ps_sem.at[d - 1], pr_sem.at[d - 1], to))
        copies.append(remote(xtra, x_recv.at[d - 1], xs_sem.at[d - 1], xr_sem.at[d - 1], to))
    for copy in copies:
        copy.start()
    col_main = col_part[:, 0:cols] + gsum
    for copy in copies:
        copy.wait_recv()
    mine = pk32[pl.ds(pl.multiple_of(col * share, 16), share)]
    line = xtra32[0:64]
    for d in range(1, nc):
        mine = mine + p_recv[d - 1].astype(F32)
        line = line + x_recv[d - 1, 0:64].astype(F32)
    side = lax.broadcasted_iota(jnp.int32, (64, 128), 1)
    from_left = jnp.where(jnp.logical_and(side < 16, col > 0), x_recv[0, 64:128].astype(F32), 0.0)
    from_right = jnp.where(jnp.logical_and(side >= 112, col < nc - 1), x_recv[nc - 2, 64:128].astype(F32), 0.0)

    dd32[0:share] = mine
    dd32[share : share + 64] = col_main[:, 0:128] + from_left
    dd32[share + 64 : share + 128] = col_main[:, 128:256] + from_right
    dd32[share + 128 : share + 144] = line[48:64]
    if n * chunk > share + 144:
        dd32[share + 144 :] = jnp.zeros((n * chunk - share - 144, 128), F32)
    dd[...] = dd32[...].astype(BF16)
    nb[...] = line[0:48].astype(BF16)
    scatter = []
    for d in range(1, n):
        src = dd.at[pl.ds(pl.multiple_of(row_peer(d) * chunk, 16), chunk)]
        scatter.append(remote(src, d_recv.at[d - 1], ds_sem.at[d - 1], dr_sem.at[d - 1], (row_peer(d), col)))
    near = [
        remote(nb.at[pl.ds(32, 16)], nb_recv.at[0], ns_sem.at[0], nr_sem.at[0], (row_peer(1), col)),
        remote(nb.at[pl.ds(0, 16)], nb_recv.at[1], ns_sem.at[1], nr_sem.at[1], (row_peer(n - 1), col)),
    ]
    for copy in scatter + near:
        copy.start()
    spot = pl.ds(pl.multiple_of(row * chunk, 16), chunk)
    done = dd32[spot]
    for copy in scatter:
        copy.wait_recv()
    for d in range(1, n):
        done = done + d_recv[d - 1].astype(F32)
    full[spot] = done.astype(BF16)
    gather = []
    for d in range(1, n):
        gather.append(remote(full.at[spot], full.at[spot], as_sem.at[d - 1], ar_sem.at[d - 1], (row_peer(d), col)))
    for copy in gather:
        copy.start()
    for copy in near:
        copy.wait_recv()
    low = jnp.where(row > 0, nb_recv[0].astype(F32), 0.0)
    high = jnp.where(row < n - 1, nb_recv[1].astype(F32), 0.0)
    rg_ref[...] = line[16:32] + low + high
    for d in range(1, n):
        other = pl.ds(pl.multiple_of(row_peer(n - d) * chunk, 16), chunk)
        remote(full.at[spot], full.at[other], as_sem.at[d - 1], ar_sem.at[d - 1], (row_peer(d), col)).wait_recv()

    own = pl.ds(pl.multiple_of(col * share, 16), share)
    last = []
    for d in range(1, nc):
        last.append(remote(full.at[pl.ds(0, share)], pfull.at[own], cs_sem.at[d - 1], cr_sem.at[d - 1], (row, col_peer(d))))
    for copy in last:
        copy.start()
    pfull[own] = full[0:share]
    for d in range(1, nc):
        other = pl.ds(pl.multiple_of(col_peer(nc - d) * share, 16), share)
        remote(full.at[pl.ds(0, share)], pfull.at[other], cs_sem.at[d - 1], cr_sem.at[d - 1], (row, col_peer(d))).wait_recv()
    for copy in feats + copies + scatter + near + gather + last:
        copy.wait_send()


def finish(n, nc, share, rg_in, full, pfull, rg_ref, cg_ref, g1_ref, gb_ref, g2_ref):
    whole = 1.0 / math.sqrt(16 * n * 256 * nc)
    tall = 1.0 / math.sqrt(16 * n)
    rg_ref[...] = rg_in[:, 0:64] * (1.0 / math.sqrt(256 * nc))
    cg_ref[:, 0:128] = full[share : share + 64].astype(F32) * tall
    cg_ref[:, 128:256] = full[share + 64 : share + 128].astype(F32) * tall
    gb_ref[...] = full[share + 128 : share + 144].astype(F32)[0:1, 0:64] * whole
    for a in range(3):
        for b in range(3):
            at = 64 * (3 * a + b)
            tap = pfull[at : at + 64].astype(F32) * whole
            g1_ref[a, b] = tap[:, 0:64]
            g2_ref[a, b] = tap[:, 64:128]


def shards(n, nc, grad_out, row_feat, col_feat, conv_one, bias_one, conv_two):
    share = round_up(-(-576 // nc), 16)
    chunk = round_up(-(-(share + 144) // n), 16)
    vmem = pl.BlockSpec(memory_space=pltpu.VMEM)
    dma = pltpu.SemaphoreType.DMA
    scratch = [
        pltpu.VMEM((64, 16, 256), BF16),
        pltpu.VMEM((16, 64), BF16),
        pltpu.VMEM((64, 256), BF16),
        pltpu.VMEM((3, 3, 64, 64), BF16),
        pltpu.VMEM((1, 64), F32),
        pltpu.VMEM((3, 3, 64, 64), BF16),
        pltpu.VMEM((2, 16, 64), BF16),
        dma((6,)),
        pltpu.VMEM((3, 64, 192), BF16),
        pltpu.VMEM((192, 192), BF16),
        pltpu.VMEM((160, 128), F32),
        pltpu.VMEM((400, 128), F32),
        pltpu.VMEM((2, 16, 64), BF16),
        pltpu.VMEM((2, 16, 64), BF16),
        pltpu.VMEM((8, 192, 768), BF16),
        pltpu.VMEM((4, 8, 64, 384), F32),
        pltpu.VMEM((4, 8, 64, 384), BF16),
        pltpu.VMEM((512, 384), BF16),
        pltpu.VMEM((4, 192, 128), F32),
        pltpu.VMEM((192, 384), F32),
        pltpu.VMEM((64, 256), F32),
        pltpu.VMEM((192, 384), F32),
        pltpu.VMEM((384, 256), BF16),
        pltpu.VMEM((nc * share, 128), BF16),
        pltpu.VMEM((nc * share, 128), F32),
        pltpu.VMEM((128, 128), BF16),
        pltpu.VMEM((128, 128), F32),
        pltpu.VMEM((nc - 1, share, 128), BF16),
        pltpu.VMEM((nc - 1, 128, 128), BF16),
        pltpu.VMEM((n * chunk, 128), BF16),
        pltpu.VMEM((n * chunk, 128), F32),
        pltpu.VMEM((48, 128), BF16),
        pltpu.VMEM((2, 16, 128), BF16),
        pltpu.VMEM((n - 1, chunk, 128), BF16),
        dma((4,)), dma((4,)),
        dma((nc - 1,)), dma((nc - 1,)),
        dma((nc - 1,)), dma((nc - 1,)),
        dma((n - 1,)), dma((n - 1,)),
        dma((2,)), dma((2,)),
        dma((n - 1,)), dma((n - 1,)),
        dma((nc - 1,)), dma((nc - 1,)),
    ]
    sums = pl.pallas_call(
        functools.partial(kernel, n, nc, share, chunk),
        out_shape=(
            jax.ShapeDtypeStruct((16, 128), F32),
            jax.ShapeDtypeStruct((n * chunk, 128), BF16),
            jax.ShapeDtypeStruct((nc * share, 128), BF16),
        ),
        in_specs=[pl.BlockSpec(memory_space=pltpu.HBM)] * 6,
        out_specs=(vmem,) * 3,
        scratch_shapes=scratch,
        compiler_params=pltpu.CompilerParams(
            collective_id=0, has_side_effects=True, vmem_limit_bytes=60 * 2**20
        ),
    )(grad_out, row_feat, col_feat.T, conv_one, bias_one.reshape(1, 64), conv_two)
    out = pl.pallas_call(
        functools.partial(finish, n, nc, share),
        out_shape=(
            jax.ShapeDtypeStruct((16, 64), F32),
            jax.ShapeDtypeStruct((64, 256), F32),
            jax.ShapeDtypeStruct((3, 3, 64, 64), F32),
            jax.ShapeDtypeStruct((1, 64), F32),
            jax.ShapeDtypeStruct((3, 3, 64, 64), F32),
        ),
        in_specs=[vmem] * 3,
        out_specs=(vmem,) * 5,
        compiler_params=pltpu.CompilerParams(vmem_limit_bytes=60 * 2**20),
    )(*sums)
    return (out[0], out[1].T, out[2], out[3].reshape(64), out[4])


def solution(mesh):
    n, nc = mesh.shape["row"], mesh.shape["col"]
    in_specs = (P(None, "row", "col"), P("row", None), P("col", None), P(), P(), P())
    out_specs = (P("row", None), P("col", None), P(), P(), P())
    return jax.shard_map(
        functools.partial(shards, n, nc), mesh=mesh, in_specs=in_specs, out_specs=out_specs, check_vma=False
    )
```

```python
import functools
import math

import jax
import jax.numpy as jnp
from jax import lax
from jax.experimental import pallas as pl
from jax.experimental.pallas import tpu as pltpu
from jax.sharding import PartitionSpec as P

F32 = jnp.float32
BF16 = jnp.bfloat16
MESH = pl.DeviceIdType.MESH
NN = (((1,), (0,)), ((), ()))
NT = (((1,), (1,)), ((), ()))


def mm(x, y, dims=NN):
    return lax.dot_general(x, y, dims, preferred_element_type=F32)


def twice(x):
    return jnp.concatenate([x, x], axis=1)


def round_up(value, unit):
    return -(-value // unit) * unit


def kernel(
    n, nc, share,
    g_hbm, row_hbm, col_hbm, k1_hbm, bias_hbm, k2_hbm,
    rg_ref, full_b, whole_a, whole_b,
    g_ref, row_ref, col_ref, k1_ref, bias_ref, k2_ref, csend, in_sem, k1t, k2t,
    rowbuf, colbuf, rrecv, crecv,
    gs, zb, act_s, inn_s, a_s, b_s, t_s, u_s, m3,
    pk_a, pk32_a, pk_b, pk32_b, xtra, xtra32, p_recv_a, p_recv_b, x_recv,
    dd_a, dd32_a, dd_b, dd32_b, nb, nb_recv, d_recv_a, d_recv_b, full_a,
    fs_sem, fr_sem, psa_sem, pra_sem, psb_sem, prb_sem, xs_sem, xr_sem,
    dsa_sem, dra_sem, dsb_sem, drb_sem, ns_sem, nr_sem,
    asa_sem, ara_sem, asb_sem, arb_sem, csa_sem, cra_sem, csb_sem, crb_sem,
):
    row = lax.axis_index("row")
    col = lax.axis_index("col")
    rows, cols, wide = 16, 256, 384

    def row_peer(d):
        return lax.rem(row + d, n)

    def col_peer(d):
        return lax.rem(col + d, nc)

    loads = [
        pltpu.make_async_copy(src, dst, in_sem.at[i])
        for i, (src, dst) in enumerate(
            [(g_hbm, g_ref), (row_hbm, row_ref), (col_hbm, col_ref), (k1_hbm, k1_ref), (bias_hbm, bias_ref), (k2_hbm, k2_ref)]
        )
    ]
    for load in loads:
        load.start()
    barrier = pltpu.get_barrier_semaphore()
    for d in range(1, n):
        pl.semaphore_signal(barrier, inc=1, device_id=(row_peer(d), col), device_id_type=MESH)
    for d in range(1, nc):
        pl.semaphore_signal(barrier, inc=1, device_id=(row, col_peer(d)), device_id_type=MESH)

    def remote(src, dst, send, recv, to):
        return pltpu.make_async_remote_copy(
            src_ref=src, dst_ref=dst, send_sem=send, recv_sem=recv, device_id=to, device_id_type=MESH
        )

    pa = lax.broadcasted_iota(jnp.int32, (256, 256), 0)
    pb = lax.broadcasted_iota(jnp.int32, (256, 256), 1)
    perm = ((pa & 15) * 16 + (pa >> 4) == pb).astype(F32).astype(BF16)
    sa = lax.broadcasted_iota(jnp.int32, (256, wide), 0)
    sb = lax.broadcasted_iota(jnp.int32, (256, wide), 1)
    gap = sb - sa
    shifts = jnp.concatenate(
        [
            jnp.logical_or(gap == -8, gap == wide - 8).astype(F32).astype(BF16),
            (gap == 8).astype(F32).astype(BF16),
        ],
        axis=1,
    )
    rowbuf[...] = jnp.zeros_like(rowbuf)
    colbuf[...] = jnp.zeros_like(colbuf)
    loads[1].wait()
    loads[2].wait()
    rowbuf[16:32] = twice(row_ref[...].astype(F32))
    col_t = col_ref[...].astype(F32).T
    colbuf[8 : 8 + cols] = twice(col_t)
    colbuf[392:400] = twice(col_t[0:8])
    csend[0] = col_t[cols - 16 : cols].astype(BF16)
    csend[1] = col_t[0:16].astype(BF16)
    loads[0].wait()

    blank = jnp.zeros((256, wide - cols), BF16)

    def build(og):
        x = g_ref[pl.ds(og * 16, 16)].reshape(256, cols)
        plain = mm(perm, x).astype(BF16)
        moved = mm(plain, shifts).astype(BF16)
        turns = [moved[:, :wide], jnp.concatenate([plain, blank], axis=1), moved[:, wide:]]
        for r in range(rows):
            h, k = r // 8, r % 8
            for b in range(3):
                gs[k, pl.ds(b * 64 + og * 16, 16), h * wide : (h + 1) * wide] = turns[b][16 * r : 16 * r + 16]

    for og in range(4):
        build(og)

    pl.semaphore_wait(barrier, (n - 1) + (nc - 1))
    feats = [
        remote(row_ref, rrecv.at[0], fs_sem.at[0], fr_sem.at[0], (row_peer(1), col)),
        remote(row_ref, rrecv.at[1], fs_sem.at[1], fr_sem.at[1], (row_peer(n - 1), col)),
        remote(csend.at[0], crecv.at[0], fs_sem.at[2], fr_sem.at[2], (row, col_peer(1))),
        remote(csend.at[1], crecv.at[1], fs_sem.at[3], fr_sem.at[3], (row, col_peer(nc - 1))),
    ]
    for copy in feats:
        copy.start()

    for load in loads[3:]:
        load.wait()
    for a in range(3):
        k2t[64 * a : 64 * a + 64] = k2_ref[a].reshape(192, 64).astype(F32).T.astype(BF16)
    w2 = k2t[...]
    lane = lax.broadcasted_iota(jnp.int32, (64, 128), 1)

    def spread(k, carry):
        gsum, rsum = carry
        both = gs[k]
        z = mm(w2, both)
        lo, hi = z[:, :wide], z[:, wide:]
        zb[0, k] = lo[0:64]
        zb[1, k] = lo[64:128] + hi[0:64]
        zb[2, k] = lo[128:192] + hi[64:128]
        zb[3, k] = hi[128:192]
        mid = both[64:128].astype(F32)
        first, second = mid[:, 0:cols], mid[:, wide : wide + cols]
        rsum = jnp.where(lane == 8 + k, jnp.sum(first, axis=1, keepdims=True), rsum)
        rsum = jnp.where(lane == 16 + k, jnp.sum(second, axis=1, keepdims=True), rsum)
        return gsum + first + second, rsum

    gsum, rsum = lax.fori_loop(
        0, 8, spread, (jnp.zeros((64, cols), F32), jnp.zeros((64, 128), F32)), unroll=4
    )

    ma = lax.broadcasted_iota(jnp.int32, (wide, 128), 0)
    cut_low = jnp.logical_and(ma < 8, col == 0)
    cut_high = jnp.logical_and(jnp.logical_and(ma >= cols - 8, ma < cols), col == nc - 1)
    m3[:, 0:128] = jnp.ones((wide, 128), BF16)
    m3[:, 128:256] = jnp.where(jnp.logical_or(cut_low, cut_high), 1.0, 0.0).astype(BF16)
    for b in range(3):
        k1_b = jnp.concatenate([k1_ref[a, b] for a in range(3)], axis=0)
        k1t[b] = k1_b.astype(F32).T.astype(BF16)
    for copy in feats:
        copy.wait_recv()
    rowbuf[0:16] = twice(jnp.where(row > 0, rrecv[0].astype(F32), 0.0))
    rowbuf[32:48] = twice(jnp.where(row < n - 1, rrecv[1].astype(F32), 0.0))
    left = twice(jnp.where(col > 0, crecv[0].astype(F32), 0.0))
    colbuf[376:392] = left
    colbuf[0:8] = left[8:16]
    colbuf[264:280] = twice(jnp.where(col < nc - 1, crecv[1].astype(F32), 0.0))

    a_all = jnp.zeros((192, 128), F32)
    for a in range(3):
        a_all += mm(
            k1_ref[a].reshape(192, 64), rowbuf[8 * a : 8 * a + 128, 0:64].astype(BF16), NT
        )
    for g in range(4):
        turned = a_all if g == 0 else pltpu.roll(a_all, 128 - 8 * g, 1)
        a_s[g] = turned
    b_all = jnp.zeros((192, wide), F32)
    for b in range(3):
        k1_b = jnp.concatenate([k1_ref[a, b] for a in range(3)], axis=0)
        b_all += mm(k1_b, colbuf[8 * b : 8 * b + wide, 0:64].astype(BF16), NT)
    eye = lax.broadcasted_iota(jnp.int32, (64, 64), 0) == lax.broadcasted_iota(jnp.int32, (64, 64), 1)
    bias = jnp.sum(jnp.where(eye, bias_ref[...], 0.0), axis=1, keepdims=True)
    b_s[...] = b_all

    lanes = lax.broadcasted_iota(jnp.int32, (1, wide), 1)
    on_left = jnp.logical_and(lanes >= wide - 8, col > 0)
    on_right = jnp.logical_and(jnp.logical_and(lanes >= cols, lanes < cols + 8), col < nc - 1)
    inside_cols = jnp.where(
        jnp.logical_or(lanes < cols, jnp.logical_or(on_left, on_right)), 1.0, 0.0
    ).astype(F32)
    lane1 = lax.broadcasted_iota(jnp.int32, (1, 128), 1)
    low_cut = jnp.where(jnp.logical_and(lane1 < 8, col == 0), 1.0, 0.0).astype(F32)
    high_cut = jnp.where(jnp.logical_and(lane1 >= 120, col == nc - 1), 1.0, 0.0).astype(F32)
    total = rows * n
    lane2 = lax.broadcasted_iota(jnp.int32, (64, 256), 1) & 127
    t_s[...] = jnp.zeros_like(t_s)
    u_s[...] = jnp.zeros_like(u_s)

    def group(g, carry):
        start = row * rows + 8 * (g - 1)

        def flag(first):
            return jnp.where(jnp.logical_and(first >= 0, first < total), 1.0, 0.0).astype(F32)

        flags = [flag(start + 8 * (a - 1)) for a in range(3)]
        base = bias + sum(b_s[64 * a : 64 * a + 64] * flags[a] for a in range(3))
        inside = inside_cols * flag(start)
        a_g = a_s[g]
        a_low, a_high = a_g[0:64], a_g[128:192]
        a_sum = a_low + a_g[64:128] + a_high
        cuts = [(a_low, low_cut), (a_high, high_cut), None]
        for tile in range(3):
            at = slice(128 * tile, 128 * tile + 128)
            v = jnp.zeros((64, 128), F32)
            for k in range(8):
                pre = base[:, at] + a_sum[:, k : k + 1]
                if cuts[tile] is not None:
                    pre = pre - cuts[tile][0][:, k : k + 1] * cuts[tile][1]
                sig = 0.5 + 0.5 * jnp.tanh(0.5 * pre)
                kept = sig * inside[:, at] if tile == 2 else sig * flag(start)
                act = pre * kept
                act_s[g, k, :, at] = act.astype(BF16)
                inner = zb[g, k, :, at] * (kept + act * (1.0 - sig))
                inn_s[64 * k : 64 * k + 64, at] = inner.astype(BF16)
                v = v + inner
            for a in range(3):
                u_s[64 * a : 64 * a + 64, at] += v * flags[a]
        sums = mm(inn_s[...], m3[...])
        t = t_s[...]
        for k in range(8):
            t = jnp.where(lane2 == 8 * g + k, sums[64 * k : 64 * k + 64], t)
        t_s[...] = t
        return carry

    lax.fori_loop(0, 4, group, 0, unroll=2)

    def second(k, acc):
        a0, a1, a2, a3 = act_s[0, k], act_s[1, k], act_s[2, k], act_s[3, k]
        low = jnp.concatenate([a0, a1, a2, a2], axis=0)
        high = jnp.concatenate([a1, a2, a3, a3], axis=0)
        return acc + mm(gs[k], jnp.concatenate([low, high], axis=1), NT)

    two = lax.fori_loop(0, 8, second, jnp.zeros((192, 256), F32), unroll=True)
    hi_half = lax.broadcasted_iota(jnp.int32, (192, 128), 1) >= 64

    def to_col(src, dst, send, recv, per_peer):
        made = []
        for d in range(1, nc):
            part = src.at[pl.ds(pl.multiple_of(col_peer(d) * share, 16), share)] if per_peer else src
            made.append(remote(part, dst.at[d - 1], send.at[d - 1], recv.at[d - 1], (row, col_peer(d))))
        for copy in made:
            copy.start()
        return made

    def mine_of(pk32, p_recv):
        got = pk32[pl.ds(pl.multiple_of(col * share, 16), share)]
        for d in range(1, nc):
            got = got + p_recv[d - 1].astype(F32)
        return got

    def rounds(units):
        return [(q, units - q * n) for q in range(-(-units // n))]

    def guarded(test, limit, act):
        if limit >= n:
            act()
        else:
            pl.when(test < limit)(act)

    def piece(unit):
        return pl.ds(pl.multiple_of(unit * 16, 16), 16)

    def scatter(src, units, dst, send, recv):
        made = []
        for q, limit in rounds(units):
            for d in range(1, n):
                p = row_peer(d)
                at = piece(jnp.minimum(q * n + p, units - 1))
                copy = remote(src.at[at], dst.at[q, d - 1], send.at[q, d - 1], recv.at[q, d - 1], (p, col))
                guarded(p, limit, copy.start)
                made.append((copy, p, limit))
        return made

    def gather(made, own32, units, got, out, send, recv):
        sent, late = [], []
        for q, limit in rounds(units):
            at = piece(jnp.minimum(q * n + row, units - 1))

            def own(q=q, limit=limit, at=at):
                for copy, _, lim in made:
                    if lim == limit:
                        copy.wait_recv()
                done = own32[at]
                for d in range(1, n):
                    done = done + got[q, d - 1].astype(F32)
                out[at] = done.astype(BF16)
                for d in range(1, n):
                    remote(out.at[at], out.at[at], send.at[q, d - 1], recv.at[q, d - 1], (row_peer(d), col)).start()

            guarded(row, limit, own)
            for d in range(1, n):
                p = row_peer(n - d)
                there = piece(jnp.minimum(q * n + p, units - 1))
                late.append((remote(out.at[at], out.at[there], send.at[q, d - 1], recv.at[q, d - 1], (row_peer(d), col)), p, limit))
                sent.append((remote(out.at[at], out.at[at], send.at[q, d - 1], recv.at[q, d - 1], (row_peer(d), col)), row, limit))
        return sent, late

    def share_out(src, out, send, recv):
        own = pl.ds(pl.multiple_of(col * share, 16), share)
        made = []
        for d in range(1, nc):
            made.append(remote(src.at[pl.ds(0, share)], out.at[own], send.at[d - 1], recv.at[d - 1], (row, col_peer(d))))
        for copy in made:
            copy.start()
        out[own] = src[0:share]
        return made

    def share_in(src, out, send, recv):
        for d in range(1, nc):
            other = pl.ds(pl.multiple_of(col_peer(nc - d) * share, 16), share)
            remote(src.at[pl.ds(0, share)], out.at[other], send.at[d - 1], recv.at[d - 1], (row, col_peer(d))).wait_recv()

    def pack(first, low, high, pk32, pk):
        pk32[0:192] = first
        pk32[192:288] = jnp.where(hi_half[0:96], high, low)
        if nc * share > 288:
            pk32[288:] = jnp.zeros((nc * share - 288, 128), F32)
        pk[...] = pk32[...].astype(BF16)

    units_a, units_b = share // 16, share // 16 + 9
    pack(two[:, 0:128], two[0:96, 128:256], two[96:192, 128:256], pk32_a, pk_a)
    cols_a = to_col(pk_a, p_recv_a, psa_sem, pra_sem, True)

    t_mid, t_cut = t_s[:, 0:128], t_s[:, 128:256]
    t_all = jnp.concatenate(
        [jnp.where(col == 0, t_mid - t_cut, t_mid), t_mid, jnp.where(col == nc - 1, t_mid - t_cut, t_mid)], axis=0
    )
    t_b = t_all.astype(BF16)
    u_b = u_s[...].astype(BF16)
    by_col = [mm(u_b, colbuf[8 * b : 8 * b + wide].astype(BF16)) for b in range(3)]
    ones = []
    for a in range(3):
        by_row = mm(t_b, rowbuf[8 * a : 8 * a + 128].astype(BF16))
        ones.append(by_row + jnp.concatenate([by_col[b][64 * a : 64 * a + 64] for b in range(3)], axis=0))
    pack(jnp.where(hi_half, ones[1], ones[0]), ones[2][0:96], ones[2][96:192], pk32_b, pk_b)
    cols_b = to_col(pk_b, p_recv_b, psb_sem, prb_sem, True)

    for copy in cols_a:
        copy.wait_recv()
    dd32_a[...] = mine_of(pk32_a, p_recv_a)
    dd_a[...] = dd32_a[...].astype(BF16)
    rows_a = scatter(dd_a, units_a, d_recv_a, dsa_sem, dra_sem)

    t_t = t_all.T
    xtra32[...] = jnp.zeros_like(xtra32)
    for a in range(3):
        part = mm(t_t.astype(BF16), k1_ref[a].reshape(192, 64))
        xtra32[8 * a : 8 * a + 32, 0:64] += part[0:32]
    xtra32[16:32, 0:64] += rsum.T[8:24]
    xtra32[48:49, 0:64] = jnp.sum(t_t, axis=0, keepdims=True)[:, 64:128]
    parts = [mm(k1t[b], u_b) for b in range(3)]
    col_part = pltpu.roll(parts[0], wide - 8, 1) + parts[1] + pltpu.roll(parts[2], 8, 1)
    xtra32[64:128] = col_part[:, cols:wide]
    xtra[...] = xtra32[...].astype(BF16)
    cols_x = to_col(xtra, x_recv, xs_sem, xr_sem, False)

    col_main = col_part[:, 0:cols] + gsum
    for copy in cols_b:
        copy.wait_recv()
    dd32_b[0:share] = mine_of(pk32_b, p_recv_b)
    for copy in cols_x:
        copy.wait_recv()
    line = xtra32[0:64]
    for d in range(1, nc):
        line = line + x_recv[d - 1, 0:64].astype(F32)
    side = lax.broadcasted_iota(jnp.int32, (64, 128), 1)
    from_left = jnp.where(jnp.logical_and(side < 16, col > 0), x_recv[0, 64:128].astype(F32), 0.0)
    from_right = jnp.where(jnp.logical_and(side >= 112, col < nc - 1), x_recv[nc - 2, 64:128].astype(F32), 0.0)
    dd32_b[share : share + 64] = col_main[:, 0:128] + from_left
    dd32_b[share + 64 : share + 128] = col_main[:, 128:256] + from_right
    dd32_b[share + 128 : share + 144] = line[48:64]
    dd_b[...] = dd32_b[...].astype(BF16)
    rows_b = scatter(dd_b, units_b, d_recv_b, dsb_sem, drb_sem)
    nb[...] = line[0:48].astype(BF16)
    near = [
        remote(nb.at[pl.ds(32, 16)], nb_recv.at[0], ns_sem.at[0], nr_sem.at[0], (row_peer(1), col)),
        remote(nb.at[pl.ds(0, 16)], nb_recv.at[1], ns_sem.at[1], nr_sem.at[1], (row_peer(n - 1), col)),
    ]
    for copy in near:
        copy.start()

    sent_a, late_a = gather(rows_a, dd32_a, units_a, d_recv_a, full_a, asa_sem, ara_sem)
    sent_b, late_b = gather(rows_b, dd32_b, units_b, d_recv_b, full_b, asb_sem, arb_sem)
    for copy in near:
        copy.wait_recv()
    low = jnp.where(row > 0, nb_recv[0].astype(F32), 0.0)
    high = jnp.where(row < n - 1, nb_recv[1].astype(F32), 0.0)
    rg_ref[...] = line[16:32] + low + high
    for copy, p, limit in late_a:
        guarded(p, limit, copy.wait_recv)
    out_a = share_out(full_a, whole_a, csa_sem, cra_sem)
    for copy, p, limit in late_b:
        guarded(p, limit, copy.wait_recv)
    out_b = share_out(full_b, whole_b, csb_sem, crb_sem)
    share_in(full_a, whole_a, csa_sem, cra_sem)
    share_in(full_b, whole_b, csb_sem, crb_sem)
    for copy in feats + cols_a + cols_b + cols_x + near + out_a + out_b:
        copy.wait_send()
    for copy, p, limit in rows_a + rows_b + sent_a + sent_b:
        guarded(p, limit, copy.wait_send)


def finish(n, nc, share, rg_in, full_b, whole_a, whole_b, rg_ref, cg_ref, g1_ref, gb_ref, g2_ref):
    whole = 1.0 / math.sqrt(16 * n * 256 * nc)
    tall = 1.0 / math.sqrt(16 * n)
    rg_ref[...] = rg_in[:, 0:64] * (1.0 / math.sqrt(256 * nc))
    cg_ref[:, 0:128] = full_b[share : share + 64].astype(F32) * tall
    cg_ref[:, 128:256] = full_b[share + 64 : share + 128].astype(F32) * tall
    gb_ref[...] = full_b[share + 128 : share + 144].astype(F32)[0:1, 0:64] * whole
    for src, dst in ((whole_b, g1_ref), (whole_a, g2_ref)):
        for b in range(3):
            both = src[64 * b : 64 * b + 64].astype(F32) * whole
            dst[0, b] = both[:, 0:64]
            dst[1, b] = both[:, 64:128]
        rest = src[192:288].astype(F32) * whole
        dst[2, 0] = rest[0:64, 0:64]
        dst[2, 1, 0:32] = rest[64:96, 0:64]
        dst[2, 1, 32:64] = rest[0:32, 64:128]
        dst[2, 2] = rest[32:96, 64:128]


def shards(n, nc, grad_out, row_feat, col_feat, conv_one, bias_one, conv_two):
    share = round_up(-(-288 // nc), 16)
    units_a, units_b = share // 16, share // 16 + 9
    turns_a, turns_b = -(-units_a // n), -(-units_b // n)
    vmem = pl.BlockSpec(memory_space=pltpu.VMEM)
    dma = pltpu.SemaphoreType.DMA
    scratch = [
        pltpu.VMEM((64, 16, 256), BF16),
        pltpu.VMEM((16, 64), BF16),
        pltpu.VMEM((64, 256), BF16),
        pltpu.VMEM((3, 3, 64, 64), BF16),
        pltpu.VMEM((1, 64), F32),
        pltpu.VMEM((3, 3, 64, 64), BF16),
        pltpu.VMEM((2, 16, 64), BF16),
        dma((6,)),
        pltpu.VMEM((3, 64, 192), BF16),
        pltpu.VMEM((192, 192), BF16),
        pltpu.VMEM((160, 128), F32),
        pltpu.VMEM((400, 128), F32),
        pltpu.VMEM((2, 16, 64), BF16),
        pltpu.VMEM((2, 16, 64), BF16),
        pltpu.VMEM((8, 192, 768), BF16),
        pltpu.VMEM((4, 8, 64, 384), F32),
        pltpu.VMEM((4, 8, 64, 384), BF16),
        pltpu.VMEM((512, 384), BF16),
        pltpu.VMEM((4, 192, 128), F32),
        pltpu.VMEM((192, 384), F32),
        pltpu.VMEM((64, 256), F32),
        pltpu.VMEM((192, 384), F32),
        pltpu.VMEM((384, 256), BF16),
        pltpu.VMEM((nc * share, 128), BF16),
        pltpu.VMEM((nc * share, 128), F32),
        pltpu.VMEM((nc * share, 128), BF16),
        pltpu.VMEM((nc * share, 128), F32),
        pltpu.VMEM((128, 128), BF16),
        pltpu.VMEM((128, 128), F32),
        pltpu.VMEM((nc - 1, share, 128), BF16),
        pltpu.VMEM((nc - 1, share, 128), BF16),
        pltpu.VMEM((nc - 1, 128, 128), BF16),
        pltpu.VMEM((16 * units_a, 128), BF16),
        pltpu.VMEM((16 * units_a, 128), F32),
        pltpu.VMEM((16 * units_b, 128), BF16),
        pltpu.VMEM((16 * units_b, 128), F32),
        pltpu.VMEM((48, 128), BF16),
        pltpu.VMEM((2, 16, 128), BF16),
        pltpu.VMEM((turns_a, n - 1, 16, 128), BF16),
        pltpu.VMEM((turns_b, n - 1, 16, 128), BF16),
        pltpu.VMEM((16 * units_a, 128), BF16),
        dma((4,)), dma((4,)),
        *[dma((nc - 1,))] * 6,
        *[dma((turns_a, n - 1))] * 2,
        *[dma((turns_b, n - 1))] * 2,
        dma((2,)), dma((2,)),
        *[dma((turns_a, n - 1))] * 2,
        *[dma((turns_b, n - 1))] * 2,
        *[dma((nc - 1,))] * 4,
    ]
    sums = pl.pallas_call(
        functools.partial(kernel, n, nc, share),
        out_shape=(
            jax.ShapeDtypeStruct((16, 128), F32),
            jax.ShapeDtypeStruct((16 * units_b, 128), BF16),
            jax.ShapeDtypeStruct((nc * share, 128), BF16),
            jax.ShapeDtypeStruct((nc * share, 128), BF16),
        ),
        in_specs=[pl.BlockSpec(memory_space=pltpu.HBM)] * 6,
        out_specs=(vmem,) * 4,
        scratch_shapes=scratch,
        compiler_params=pltpu.CompilerParams(
            collective_id=0, has_side_effects=True, vmem_limit_bytes=60 * 2**20
        ),
    )(grad_out, row_feat, col_feat.T, conv_one, bias_one.reshape(1, 64), conv_two)
    out = pl.pallas_call(
        functools.partial(finish, n, nc, share),
        out_shape=(
            jax.ShapeDtypeStruct((16, 64), F32),
            jax.ShapeDtypeStruct((64, 256), F32),
            jax.ShapeDtypeStruct((3, 3, 64, 64), F32),
            jax.ShapeDtypeStruct((1, 64), F32),
            jax.ShapeDtypeStruct((3, 3, 64, 64), F32),
        ),
        in_specs=[vmem] * 4,
        out_specs=(vmem,) * 5,
        compiler_params=pltpu.CompilerParams(vmem_limit_bytes=60 * 2**20),
    )(*sums)
    return (out[0], out[1].T, out[2], out[3].reshape(64), out[4])


def solution(mesh):
    n, nc = mesh.shape["row"], mesh.shape["col"]
    in_specs = (P(None, "row", "col"), P("row", None), P("col", None), P(), P(), P())
    out_specs = (P("row", None), P("col", None), P(), P(), P())
    return jax.shard_map(
        functools.partial(shards, n, nc), mesh=mesh, in_specs=in_specs, out_specs=out_specs, check_vma=False
    )
```

```python
import functools
import math

import jax
import jax.numpy as jnp
from jax import lax
from jax.experimental import pallas as pl
from jax.experimental.pallas import tpu as pltpu
from jax.sharding import PartitionSpec as P

F32 = jnp.float32
BF16 = jnp.bfloat16
MESH = pl.DeviceIdType.MESH
NN = (((1,), (0,)), ((), ()))
NT = (((1,), (1,)), ((), ()))


def mm(x, y, dims=NN):
    return lax.dot_general(x, y, dims, preferred_element_type=F32)


def round_up(value, unit):
    return -(-value // unit) * unit


def kernel(
    n, nc, share, chunk,
    g_hbm, row_hbm, col_hbm, k1_hbm, bias_hbm, k2_hbm,
    rg_ref, full, pfull,
    g_ref, row_ref, col_ref, k1_ref, bias_ref, k2_ref, csend, in_sem, k1t, k2t,
    rowbuf, colbuf, rrecv, crecv,
    gs, zb, act_s, inn_s, a_s, b_s, t_s, u_s, m3,
    pk, pk32, xtra, xtra32, p_recv, x_recv,
    dd, dd32, nb, nb_recv, d_recv,
    fs_sem, fr_sem, ps_sem, pr_sem, xs_sem, xr_sem,
    ds_sem, dr_sem, ns_sem, nr_sem, as_sem, ar_sem, cs_sem, cr_sem,
):
    row = lax.axis_index("row")
    col = lax.axis_index("col")
    rows, cols, wide = 16, 256, 384

    def row_peer(d):
        return lax.rem(row + d, n)

    def col_peer(d):
        return lax.rem(col + d, nc)

    loads = [
        pltpu.make_async_copy(src, dst, in_sem.at[i])
        for i, (src, dst) in enumerate(
            [(g_hbm, g_ref), (row_hbm, row_ref), (col_hbm, col_ref), (k1_hbm, k1_ref), (bias_hbm, bias_ref), (k2_hbm, k2_ref)]
        )
    ]
    for load in loads:
        load.start()
    barrier = pltpu.get_barrier_semaphore()
    for d in range(1, n):
        pl.semaphore_signal(barrier, inc=1, device_id=(row_peer(d), col), device_id_type=MESH)
    for d in range(1, nc):
        pl.semaphore_signal(barrier, inc=1, device_id=(row, col_peer(d)), device_id_type=MESH)

    def remote(src, dst, send, recv, to):
        return pltpu.make_async_remote_copy(
            src_ref=src, dst_ref=dst, send_sem=send, recv_sem=recv, device_id=to, device_id_type=MESH
        )

    pa = lax.broadcasted_iota(jnp.int32, (256, 256), 0)
    pb = lax.broadcasted_iota(jnp.int32, (256, 256), 1)
    perm = ((pa & 15) * 16 + (pa >> 4) == pb).astype(F32).astype(BF16)
    sa = lax.broadcasted_iota(jnp.int32, (256, wide), 0)
    sb = lax.broadcasted_iota(jnp.int32, (256, wide), 1)
    gap = sb - sa
    shifts = jnp.concatenate(
        [
            jnp.logical_or(gap == -8, gap == wide - 8).astype(F32).astype(BF16),
            (gap == 8).astype(F32).astype(BF16),
        ],
        axis=1,
    )
    rowbuf[...] = jnp.zeros_like(rowbuf)
    colbuf[...] = jnp.zeros_like(colbuf)
    loads[1].wait()
    loads[2].wait()
    rowbuf[16:32, 0:64] = row_ref[...].astype(F32)
    col_t = col_ref[...].astype(F32).T
    colbuf[8 : 8 + cols, 0:64] = col_t
    colbuf[392:400, 0:64] = col_t[0:8]
    csend[0] = col_t[cols - 16 : cols].astype(BF16)
    csend[1] = col_t[0:16].astype(BF16)
    loads[0].wait()

    blank = jnp.zeros((256, wide - cols), BF16)

    def build(og):
        x = g_ref[pl.ds(og * 16, 16)].reshape(256, cols)
        plain = mm(perm, x).astype(BF16)
        moved = mm(plain, shifts).astype(BF16)
        turns = [moved[:, :wide], jnp.concatenate([plain, blank], axis=1), moved[:, wide:]]
        for r in range(rows):
            h, k = r // 8, r % 8
            for b in range(3):
                gs[k, pl.ds(b * 64 + og * 16, 16), h * wide : (h + 1) * wide] = turns[b][16 * r : 16 * r + 16]

    for og in range(4):
        build(og)

    pl.semaphore_wait(barrier, (n - 1) + (nc - 1))
    feats = [
        remote(row_ref, rrecv.at[0], fs_sem.at[0], fr_sem.at[0], (row_peer(1), col)),
        remote(row_ref, rrecv.at[1], fs_sem.at[1], fr_sem.at[1], (row_peer(n - 1), col)),
        remote(csend.at[0], crecv.at[0], fs_sem.at[2], fr_sem.at[2], (row, col_peer(1))),
        remote(csend.at[1], crecv.at[1], fs_sem.at[3], fr_sem.at[3], (row, col_peer(nc - 1))),
    ]
    for copy in feats:
        copy.start()

    for load in loads[3:]:
        load.wait()
    for a in range(3):
        k2t[64 * a : 64 * a + 64] = k2_ref[a].reshape(192, 64).astype(F32).T.astype(BF16)
    w2 = k2t[...]
    lane = lax.broadcasted_iota(jnp.int32, (64, 128), 1)

    def spread(k, carry):
        gsum, rsum = carry
        both = gs[k]
        z = mm(w2, both)
        lo, hi = z[:, :wide], z[:, wide:]
        zb[0, k] = lo[0:64]
        zb[1, k] = lo[64:128] + hi[0:64]
        zb[2, k] = lo[128:192] + hi[64:128]
        zb[3, k] = hi[128:192]
        mid = both[64:128].astype(F32)
        first, second = mid[:, 0:cols], mid[:, wide : wide + cols]
        rsum = jnp.where(lane == 8 + k, jnp.sum(first, axis=1, keepdims=True), rsum)
        rsum = jnp.where(lane == 16 + k, jnp.sum(second, axis=1, keepdims=True), rsum)
        return gsum + first + second, rsum

    gsum, rsum = lax.fori_loop(
        0, 8, spread, (jnp.zeros((64, cols), F32), jnp.zeros((64, 128), F32)), unroll=4
    )

    ma = lax.broadcasted_iota(jnp.int32, (wide, 128), 0)
    cut_low = jnp.logical_and(ma < 8, col == 0)
    cut_high = jnp.logical_and(jnp.logical_and(ma >= cols - 8, ma < cols), col == nc - 1)
    m3[:, 0:128] = jnp.ones((wide, 128), BF16)
    m3[:, 128:256] = jnp.where(jnp.logical_or(cut_low, cut_high), 1.0, 0.0).astype(BF16)
    for b in range(3):
        k1_b = jnp.concatenate([k1_ref[a, b] for a in range(3)], axis=0)
        k1t[b] = k1_b.astype(F32).T.astype(BF16)
    for copy in feats:
        copy.wait_recv()
    rowbuf[0:16, 0:64] = jnp.where(row > 0, rrecv[0].astype(F32), 0.0)
    rowbuf[32:48, 0:64] = jnp.where(row < n - 1, rrecv[1].astype(F32), 0.0)
    left = jnp.where(col > 0, crecv[0].astype(F32), 0.0)
    colbuf[376:392, 0:64] = left
    colbuf[0:8, 0:64] = left[8:16]
    colbuf[264:280, 0:64] = jnp.where(col < nc - 1, crecv[1].astype(F32), 0.0)

    a_all = jnp.zeros((192, 128), F32)
    for a in range(3):
        a_all += mm(
            k1_ref[a].reshape(192, 64), rowbuf[8 * a : 8 * a + 128, 0:64].astype(BF16), NT
        )
    for g in range(4):
        turned = a_all if g == 0 else pltpu.roll(a_all, 128 - 8 * g, 1)
        a_s[g] = turned
    b_all = jnp.zeros((192, wide), F32)
    for b in range(3):
        k1_b = jnp.concatenate([k1_ref[a, b] for a in range(3)], axis=0)
        b_all += mm(k1_b, colbuf[8 * b : 8 * b + wide, 0:64].astype(BF16), NT)
    eye = lax.broadcasted_iota(jnp.int32, (64, 64), 0) == lax.broadcasted_iota(jnp.int32, (64, 64), 1)
    bias = jnp.sum(jnp.where(eye, bias_ref[...], 0.0), axis=1, keepdims=True)
    b_s[...] = b_all

    lanes = lax.broadcasted_iota(jnp.int32, (1, wide), 1)
    on_left = jnp.logical_and(lanes >= wide - 8, col > 0)
    on_right = jnp.logical_and(jnp.logical_and(lanes >= cols, lanes < cols + 8), col < nc - 1)
    inside_cols = jnp.where(
        jnp.logical_or(lanes < cols, jnp.logical_or(on_left, on_right)), 1.0, 0.0
    ).astype(F32)
    lane1 = lax.broadcasted_iota(jnp.int32, (1, 128), 1)
    low_cut = jnp.where(jnp.logical_and(lane1 < 8, col == 0), 1.0, 0.0).astype(F32)
    high_cut = jnp.where(jnp.logical_and(lane1 >= 120, col == nc - 1), 1.0, 0.0).astype(F32)
    total = rows * n
    lane2 = lax.broadcasted_iota(jnp.int32, (64, 256), 1) & 127
    t_s[...] = jnp.zeros_like(t_s)
    u_s[...] = jnp.zeros_like(u_s)

    def group(g, carry):
        start = row * rows + 8 * (g - 1)

        def flag(first):
            return jnp.where(jnp.logical_and(first >= 0, first < total), 1.0, 0.0).astype(F32)

        flags = [flag(start + 8 * (a - 1)) for a in range(3)]
        base = bias + sum(b_s[64 * a : 64 * a + 64] * flags[a] for a in range(3))
        inside = inside_cols * flag(start)
        a_g = a_s[g]
        a_low, a_high = a_g[0:64], a_g[128:192]
        a_sum = a_low + a_g[64:128] + a_high
        cuts = [(a_low, low_cut), (a_high, high_cut), None]
        for tile in range(3):
            at = slice(128 * tile, 128 * tile + 128)
            v = jnp.zeros((64, 128), F32)
            for k in range(8):
                pre = base[:, at] + a_sum[:, k : k + 1]
                if cuts[tile] is not None:
                    pre = pre - cuts[tile][0][:, k : k + 1] * cuts[tile][1]
                sig = 0.5 + 0.5 * jnp.tanh(0.5 * pre)
                kept = sig * inside[:, at] if tile == 2 else sig * flag(start)
                act = pre * kept
                act_s[g, k, :, at] = act.astype(BF16)
                inner = zb[g, k, :, at] * (kept + act * (1.0 - sig))
                inn_s[64 * k : 64 * k + 64, at] = inner.astype(BF16)
                v = v + inner
            for a in range(3):
                u_s[64 * a : 64 * a + 64, at] += v * flags[a]
        sums = mm(inn_s[...], m3[...])
        t = t_s[...]
        for k in range(8):
            t = jnp.where(lane2 == 8 * g + k, sums[64 * k : 64 * k + 64], t)
        t_s[...] = t
        return carry

    lax.fori_loop(0, 4, group, 0)

    def second(k, acc):
        a0, a1, a2, a3 = act_s[0, k], act_s[1, k], act_s[2, k], act_s[3, k]
        low = jnp.concatenate([a2, a0, a2, a1], axis=0)
        high = jnp.concatenate([a3, a1, a3, a2], axis=0)
        return acc + mm(gs[k], jnp.concatenate([low, high], axis=1), NT)

    two = lax.fori_loop(0, 8, second, jnp.zeros((192, 256), F32), unroll=True)
    hi_half = lax.broadcasted_iota(jnp.int32, (192, 128), 1) >= 64
    two_taps = [two[:, 0:128], two[:, 128:256], pltpu.roll(two[:, 0:128], 64, 1)]

    t_mid, t_cut = t_s[:, 0:128], t_s[:, 128:256]
    t_all = jnp.concatenate(
        [jnp.where(col == 0, t_mid - t_cut, t_mid), t_mid, jnp.where(col == nc - 1, t_mid - t_cut, t_mid)], axis=0
    )
    t_b = t_all.astype(BF16)
    u_all = u_s[...]
    u_b = u_all.astype(BF16)
    by_col = [mm(u_b, colbuf[8 * b : 8 * b + wide].astype(BF16)) for b in range(3)]
    for a in range(3):
        by_row = mm(t_b, rowbuf[8 * a : 8 * a + 128].astype(BF16))
        for b in range(3):
            tap = by_row[64 * b : 64 * b + 64] + by_col[b][64 * a : 64 * a + 64]
            tap = jnp.where(hi_half[0:64], two_taps[a][64 * b : 64 * b + 64], tap)
            at = 64 * (3 * a + b)
            pk32[at : at + 64] = tap
            pk[at : at + 64] = tap.astype(BF16)
    if nc * share > 576:
        pk32[576:] = jnp.zeros((nc * share - 576, 128), F32)
        pk[576:] = jnp.zeros((nc * share - 576, 128), BF16)

    cols_p, cols_x = [], []
    for d in range(1, nc):
        src = pk.at[pl.ds(pl.multiple_of(col_peer(d) * share, 16), share)]
        cols_p.append(remote(src, p_recv.at[d - 1], ps_sem.at[d - 1], pr_sem.at[d - 1], (row, col_peer(d))))
        cols_x.append(remote(xtra, x_recv.at[d - 1], xs_sem.at[d - 1], xr_sem.at[d - 1], (row, col_peer(d))))
    for copy in cols_p:
        copy.start()

    t_t = t_all.T
    xtra32[...] = jnp.zeros_like(xtra32)
    for a in range(3):
        part = mm(t_t.astype(BF16), k1_ref[a].reshape(192, 64))
        xtra32[8 * a : 8 * a + 32, 0:64] += part[0:32]
    xtra32[16:32, 0:64] += rsum.T[8:24]
    xtra32[48:49, 0:64] = jnp.sum(t_t, axis=0, keepdims=True)[:, 64:128]
    parts = [mm(k1t[b], u_b) for b in range(3)]
    col_part = pltpu.roll(parts[0], wide - 8, 1) + parts[1] + pltpu.roll(parts[2], 8, 1)
    xtra32[64:128] = col_part[:, cols:wide]
    xtra[...] = xtra32[...].astype(BF16)

    for copy in cols_x:
        copy.start()

    col_main = col_part[:, 0:cols] + gsum
    for copy in cols_p:
        copy.wait_recv()
    mine = pk32[pl.ds(pl.multiple_of(col * share, 16), share)]
    for d in range(1, nc):
        mine = mine + p_recv[d - 1].astype(F32)
    dd32[0:share] = mine
    for copy in cols_x:
        copy.wait_recv()
    line = xtra32[0:64]
    for d in range(1, nc):
        line = line + x_recv[d - 1, 0:64].astype(F32)
    side = lax.broadcasted_iota(jnp.int32, (64, 128), 1)
    from_left = jnp.where(jnp.logical_and(side < 16, col > 0), x_recv[0, 64:128].astype(F32), 0.0)
    from_right = jnp.where(jnp.logical_and(side >= 112, col < nc - 1), x_recv[nc - 2, 64:128].astype(F32), 0.0)

    dd32[share : share + 64] = col_main[:, 0:128] + from_left
    dd32[share + 64 : share + 128] = col_main[:, 128:256] + from_right
    dd32[share + 128 : share + 144] = line[48:64]
    if n * chunk > share + 144:
        dd32[share + 144 :] = jnp.zeros((n * chunk - share - 144, 128), F32)
    dd[...] = dd32[...].astype(BF16)
    nb[...] = line[0:48].astype(BF16)
    scatter = []
    for d in range(1, n):
        src = dd.at[pl.ds(pl.multiple_of(row_peer(d) * chunk, 16), chunk)]
        scatter.append(remote(src, d_recv.at[pl.ds((d - 1) * chunk, chunk)], ds_sem.at[0], dr_sem.at[0], (row_peer(d), col)))
    near = [
        remote(nb.at[pl.ds(32, 16)], nb_recv.at[0], ns_sem.at[0], nr_sem.at[0], (row_peer(1), col)),
        remote(nb.at[pl.ds(0, 16)], nb_recv.at[1], ns_sem.at[1], nr_sem.at[1], (row_peer(n - 1), col)),
    ]
    for copy in scatter + near:
        copy.start()
    spot = pl.ds(pl.multiple_of(row * chunk, 16), chunk)
    done = dd32[spot]
    most = (n - 1) * chunk
    all_in = remote(dd.at[pl.ds(0, most)], d_recv, ds_sem.at[0], dr_sem.at[0], (row_peer(1), col))
    all_in.wait_recv()
    for d in range(1, n):
        done = done + d_recv[(d - 1) * chunk : d * chunk].astype(F32)
    full[spot] = done.astype(BF16)
    gather = []
    for d in range(1, n):
        gather.append(remote(full.at[spot], full.at[spot], as_sem.at[0], ar_sem.at[0], (row_peer(d), col)))
    for copy in gather:
        copy.start()
    for copy in near:
        copy.wait_recv()
    low = jnp.where(row > 0, nb_recv[0].astype(F32), 0.0)
    high = jnp.where(row < n - 1, nb_recv[1].astype(F32), 0.0)
    rg_ref[...] = line[16:32] + low + high
    all_out = remote(full.at[pl.ds(0, most)], full.at[pl.ds(0, most)], as_sem.at[0], ar_sem.at[0], (row_peer(1), col))
    all_out.wait_recv()

    own = pl.ds(pl.multiple_of(col * share, 16), share)
    last = []
    for d in range(1, nc):
        last.append(remote(full.at[pl.ds(0, share)], pfull.at[own], cs_sem.at[d - 1], cr_sem.at[d - 1], (row, col_peer(d))))
    for copy in last:
        copy.start()
    pfull[own] = full[0:share]
    for d in range(1, nc):
        other = pl.ds(pl.multiple_of(col_peer(nc - d) * share, 16), share)
        remote(full.at[pl.ds(0, share)], pfull.at[other], cs_sem.at[d - 1], cr_sem.at[d - 1], (row, col_peer(d))).wait_recv()
    for copy in feats + cols_p + cols_x + [all_in, all_out] + near + last:
        copy.wait_send()


def finish(n, nc, share, rg_in, full, pfull, rg_ref, cg_ref, g1_ref, gb_ref, g2_ref):
    whole = 1.0 / math.sqrt(16 * n * 256 * nc)
    tall = 1.0 / math.sqrt(16 * n)
    rg_ref[...] = rg_in[:, 0:64] * (1.0 / math.sqrt(256 * nc))
    cg_ref[:, 0:128] = full[share : share + 64].astype(F32) * tall
    cg_ref[:, 128:256] = full[share + 64 : share + 128].astype(F32) * tall
    gb_ref[...] = full[share + 128 : share + 144].astype(F32)[0:1, 0:64] * whole
    for a in range(3):
        for b in range(3):
            at = 64 * (3 * a + b)
            tap = pfull[at : at + 64].astype(F32) * whole
            g1_ref[a, b] = tap[:, 0:64]
            g2_ref[a, b] = tap[:, 64:128]


def shards(n, nc, grad_out, row_feat, col_feat, conv_one, bias_one, conv_two):
    share = round_up(-(-576 // nc), 16)
    chunk = round_up(-(-(share + 144) // n), 16)
    vmem = pl.BlockSpec(memory_space=pltpu.VMEM)
    dma = pltpu.SemaphoreType.DMA
    scratch = [
        pltpu.VMEM((64, 16, 256), BF16),
        pltpu.VMEM((16, 64), BF16),
        pltpu.VMEM((64, 256), BF16),
        pltpu.VMEM((3, 3, 64, 64), BF16),
        pltpu.VMEM((1, 64), F32),
        pltpu.VMEM((3, 3, 64, 64), BF16),
        pltpu.VMEM((2, 16, 64), BF16),
        dma((6,)),
        pltpu.VMEM((3, 64, 192), BF16),
        pltpu.VMEM((192, 192), BF16),
        pltpu.VMEM((160, 128), F32),
        pltpu.VMEM((400, 128), F32),
        pltpu.VMEM((2, 16, 64), BF16),
        pltpu.VMEM((2, 16, 64), BF16),
        pltpu.VMEM((8, 192, 768), BF16),
        pltpu.VMEM((4, 8, 64, 384), F32),
        pltpu.VMEM((4, 8, 64, 384), BF16),
        pltpu.VMEM((512, 384), BF16),
        pltpu.VMEM((4, 192, 128), F32),
        pltpu.VMEM((192, 384), F32),
        pltpu.VMEM((64, 256), F32),
        pltpu.VMEM((192, 384), F32),
        pltpu.VMEM((384, 256), BF16),
        pltpu.VMEM((nc * share, 128), BF16),
        pltpu.VMEM((nc * share, 128), F32),
        pltpu.VMEM((128, 128), BF16),
        pltpu.VMEM((128, 128), F32),
        pltpu.VMEM((nc - 1, share, 128), BF16),
        pltpu.VMEM((nc - 1, 128, 128), BF16),
        pltpu.VMEM((n * chunk, 128), BF16),
        pltpu.VMEM((n * chunk, 128), F32),
        pltpu.VMEM((48, 128), BF16),
        pltpu.VMEM((2, 16, 128), BF16),
        pltpu.VMEM(((n - 1) * chunk, 128), BF16),
        dma((4,)), dma((4,)),
        dma((nc - 1,)), dma((nc - 1,)),
        dma((nc - 1,)), dma((nc - 1,)),
        dma((1,)), dma((1,)),
        dma((2,)), dma((2,)),
        dma((1,)), dma((1,)),
        dma((nc - 1,)), dma((nc - 1,)),
    ]
    sums = pl.pallas_call(
        functools.partial(kernel, n, nc, share, chunk),
        out_shape=(
            jax.ShapeDtypeStruct((16, 128), F32),
            jax.ShapeDtypeStruct((n * chunk, 128), BF16),
            jax.ShapeDtypeStruct((nc * share, 128), BF16),
        ),
        in_specs=[pl.BlockSpec(memory_space=pltpu.HBM)] * 6,
        out_specs=(vmem,) * 3,
        scratch_shapes=scratch,
        compiler_params=pltpu.CompilerParams(
            collective_id=0, has_side_effects=True, vmem_limit_bytes=60 * 2**20
        ),
    )(grad_out, row_feat, col_feat.T, conv_one, bias_one.reshape(1, 64), conv_two)
    out = pl.pallas_call(
        functools.partial(finish, n, nc, share),
        out_shape=(
            jax.ShapeDtypeStruct((16, 64), F32),
            jax.ShapeDtypeStruct((64, 256), F32),
            jax.ShapeDtypeStruct((3, 3, 64, 64), F32),
            jax.ShapeDtypeStruct((1, 64), F32),
            jax.ShapeDtypeStruct((3, 3, 64, 64), F32),
        ),
        in_specs=[vmem] * 3,
        out_specs=(vmem,) * 5,
        compiler_params=pltpu.CompilerParams(vmem_limit_bytes=60 * 2**20),
    )(*sums)
    return (out[0], out[1].T, out[2], out[3].reshape(64), out[4])


def solution(mesh):
    n, nc = mesh.shape["row"], mesh.shape["col"]
    in_specs = (P(None, "row", "col"), P("row", None), P("col", None), P(), P(), P())
    out_specs = (P("row", None), P("col", None), P(), P(), P())
    return jax.shard_map(
        functools.partial(shards, n, nc), mesh=mesh, in_specs=in_specs, out_specs=out_specs, check_vma=False
    )
```

```python
import functools
import math

import jax
import jax.numpy as jnp
from jax import lax
from jax.experimental import pallas as pl
from jax.experimental.pallas import tpu as pltpu
from jax.sharding import PartitionSpec as P

F32 = jnp.float32
BF16 = jnp.bfloat16
MESH = pl.DeviceIdType.MESH
NN = (((1,), (0,)), ((), ()))
NT = (((1,), (1,)), ((), ()))


def mm(x, y, dims=NN):
    return lax.dot_general(x, y, dims, preferred_element_type=F32)


def round_up(value, unit):
    return -(-value // unit) * unit


def kernel(
    n, nc, share, chunk,
    g_hbm, row_hbm, col_hbm, k1_hbm, bias_hbm, k2_hbm,
    rg_ref, full, pfull,
    g_ref, row_ref, col_ref, k1_ref, bias_ref, k2_ref, csend, in_sem, k1t, k2t,
    rowbuf, colbuf, rrecv, crecv,
    gs, zb, act_s, inn_s, a_s, b_s, t_s, u_s, m3, base_s, v_s,
    pk, pk32, xtra, xtra32, p_recv, x_recv,
    dd, dd32, nb, nb_recv, d_recv,
    fs_sem, fr_sem, ps_sem, pr_sem, xs_sem, xr_sem,
    ds_sem, dr_sem, ns_sem, nr_sem, as_sem, ar_sem, cs_sem, cr_sem,
):
    row = lax.axis_index("row")
    col = lax.axis_index("col")
    rows, cols, wide = 16, 256, 384

    def row_peer(d):
        return lax.rem(row + d, n)

    def col_peer(d):
        return lax.rem(col + d, nc)

    loads = [
        pltpu.make_async_copy(src, dst, in_sem.at[i])
        for i, (src, dst) in enumerate(
            [(g_hbm, g_ref), (row_hbm, row_ref), (col_hbm, col_ref), (k1_hbm, k1_ref), (bias_hbm, bias_ref), (k2_hbm, k2_ref)]
        )
    ]
    for load in loads:
        load.start()
    barrier = pltpu.get_barrier_semaphore()
    for d in range(1, n):
        pl.semaphore_signal(barrier, inc=1, device_id=(row_peer(d), col), device_id_type=MESH)
    for d in range(1, nc):
        pl.semaphore_signal(barrier, inc=1, device_id=(row, col_peer(d)), device_id_type=MESH)

    def remote(src, dst, send, recv, to):
        return pltpu.make_async_remote_copy(
            src_ref=src, dst_ref=dst, send_sem=send, recv_sem=recv, device_id=to, device_id_type=MESH
        )

    pa = lax.broadcasted_iota(jnp.int32, (256, 256), 0)
    pb = lax.broadcasted_iota(jnp.int32, (256, 256), 1)
    perm = ((pa & 15) * 16 + (pa >> 4) == pb).astype(F32).astype(BF16)
    sa = lax.broadcasted_iota(jnp.int32, (256, wide), 0)
    sb = lax.broadcasted_iota(jnp.int32, (256, wide), 1)
    gap = sb - sa
    shifts = jnp.concatenate(
        [
            jnp.logical_or(gap == -8, gap == wide - 8).astype(F32).astype(BF16),
            (gap == 8).astype(F32).astype(BF16),
        ],
        axis=1,
    )
    rowbuf[...] = jnp.zeros_like(rowbuf)
    colbuf[...] = jnp.zeros_like(colbuf)
    loads[1].wait()
    loads[2].wait()
    rowbuf[16:32, 0:64] = row_ref[...].astype(F32)
    col_t = col_ref[...].astype(F32).T
    colbuf[8 : 8 + cols, 0:64] = col_t
    colbuf[392:400, 0:64] = col_t[0:8]
    csend[0] = col_t[cols - 16 : cols].astype(BF16)
    csend[1] = col_t[0:16].astype(BF16)
    loads[0].wait()

    blank = jnp.zeros((256, wide - cols), BF16)

    def build(og):
        x = g_ref[pl.ds(og * 16, 16)].reshape(256, cols)
        plain = mm(perm, x).astype(BF16)
        moved = mm(plain, shifts).astype(BF16)
        turns = [moved[:, :wide], jnp.concatenate([plain, blank], axis=1), moved[:, wide:]]
        for r in range(rows):
            h, k = r // 8, r % 8
            for b in range(3):
                gs[k, pl.ds(b * 64 + og * 16, 16), h * wide : (h + 1) * wide] = turns[b][16 * r : 16 * r + 16]

    for og in range(4):
        build(og)

    pl.semaphore_wait(barrier, (n - 1) + (nc - 1))
    feats = [
        remote(row_ref, rrecv.at[0], fs_sem.at[0], fr_sem.at[0], (row_peer(1), col)),
        remote(row_ref, rrecv.at[1], fs_sem.at[1], fr_sem.at[1], (row_peer(n - 1), col)),
        remote(csend.at[0], crecv.at[0], fs_sem.at[2], fr_sem.at[2], (row, col_peer(1))),
        remote(csend.at[1], crecv.at[1], fs_sem.at[3], fr_sem.at[3], (row, col_peer(nc - 1))),
    ]
    for copy in feats:
        copy.start()

    for load in loads[3:]:
        load.wait()
    for a in range(3):
        k2t[64 * a : 64 * a + 64] = (0.5 * k2_ref[a].reshape(192, 64).astype(F32).T).astype(BF16)
    w2 = k2t[...]
    lane = lax.broadcasted_iota(jnp.int32, (64, 128), 1)

    def spread(k, carry):
        gsum, rsum = carry
        both = gs[k]
        z = mm(w2, both)
        lo, hi = z[:, :wide], z[:, wide:]
        zb[0, k] = lo[0:64]
        zb[1, k] = lo[64:128] + hi[0:64]
        zb[2, k] = lo[128:192] + hi[64:128]
        zb[3, k] = hi[128:192]
        mid = both[64:128].astype(F32)
        first, second = mid[:, 0:cols], mid[:, wide : wide + cols]
        rsum = jnp.where(lane == 8 + k, jnp.sum(first, axis=1, keepdims=True), rsum)
        rsum = jnp.where(lane == 16 + k, jnp.sum(second, axis=1, keepdims=True), rsum)
        return gsum + first + second, rsum

    gsum, rsum = lax.fori_loop(
        0, 8, spread, (jnp.zeros((64, cols), F32), jnp.zeros((64, 128), F32)), unroll=4
    )

    ma = lax.broadcasted_iota(jnp.int32, (wide, 128), 0)
    cut_low = jnp.logical_and(ma < 8, col == 0)
    cut_high = jnp.logical_and(jnp.logical_and(ma >= cols - 8, ma < cols), col == nc - 1)
    m3[:, 0:128] = jnp.ones((wide, 128), BF16)
    m3[:, 128:256] = jnp.where(jnp.logical_or(cut_low, cut_high), 1.0, 0.0).astype(BF16)
    for b in range(3):
        k1_b = jnp.concatenate([k1_ref[a, b] for a in range(3)], axis=0)
        k1t[b] = k1_b.astype(F32).T.astype(BF16)
    for copy in feats:
        copy.wait_recv()
    rowbuf[0:16, 0:64] = jnp.where(row > 0, rrecv[0].astype(F32), 0.0)
    rowbuf[32:48, 0:64] = jnp.where(row < n - 1, rrecv[1].astype(F32), 0.0)
    left = jnp.where(col > 0, crecv[0].astype(F32), 0.0)
    colbuf[376:392, 0:64] = left
    colbuf[0:8, 0:64] = left[8:16]
    colbuf[264:280, 0:64] = jnp.where(col < nc - 1, crecv[1].astype(F32), 0.0)

    a_all = jnp.zeros((192, 128), F32)
    for a in range(3):
        a_all += mm(
            k1_ref[a].reshape(192, 64), rowbuf[8 * a : 8 * a + 128, 0:64].astype(BF16), NT
        )
    a_all = 0.5 * a_all
    for g in range(4):
        turned = a_all if g == 0 else pltpu.roll(a_all, 128 - 8 * g, 1)
        a_s[g, 0:64] = turned[0:64] + turned[64:128] + turned[128:192]
        a_s[g, 64:128] = jnp.where(col == 0, turned[0:64], turned[128:192])
    b_all = jnp.zeros((192, wide), F32)
    for b in range(3):
        k1_b = jnp.concatenate([k1_ref[a, b] for a in range(3)], axis=0)
        b_all += mm(k1_b, colbuf[8 * b : 8 * b + wide, 0:64].astype(BF16), NT)
    eye = lax.broadcasted_iota(jnp.int32, (64, 64), 0) == lax.broadcasted_iota(jnp.int32, (64, 64), 1)
    bias = 0.5 * jnp.sum(jnp.where(eye, bias_ref[...], 0.0), axis=1, keepdims=True)
    b_s[...] = 0.5 * b_all

    lanes = lax.broadcasted_iota(jnp.int32, (1, wide), 1)
    on_left = jnp.logical_and(lanes >= wide - 8, col > 0)
    on_right = jnp.logical_and(jnp.logical_and(lanes >= cols, lanes < cols + 8), col < nc - 1)
    inside_cols = jnp.where(
        jnp.logical_or(lanes < cols, jnp.logical_or(on_left, on_right)), 1.0, 0.0
    ).astype(F32)
    lane1 = lax.broadcasted_iota(jnp.int32, (1, 128), 1)
    low_cut = jnp.where(jnp.logical_and(lane1 < 8, col == 0), 1.0, 0.0).astype(F32)
    high_cut = jnp.where(jnp.logical_and(lane1 >= 120, col == nc - 1), 1.0, 0.0).astype(F32)
    total = rows * n
    lane2 = lax.broadcasted_iota(jnp.int32, (64, 256), 1) & 127
    t_s[...] = jnp.zeros_like(t_s)
    u_s[...] = jnp.zeros_like(u_s)

    def group(g, carry):
        start = row * rows + 8 * (g - 1)

        def flag(first):
            return jnp.where(jnp.logical_and(first >= 0, first < total), 1.0, 0.0).astype(F32)

        flags = [flag(start + 8 * (a - 1)) for a in range(3)]
        base_s[...] = bias + sum(b_s[64 * a : 64 * a + 64] * flags[a] for a in range(3))
        in_map = flag(start)
        masks = [in_map, in_map, inside_cols[:, 256:384] * in_map]
        cuts = [low_cut, high_cut, None]
        a_g = a_s[g]
        v_s[...] = jnp.zeros_like(v_s)
        for k in range(8):
            row_term = jnp.broadcast_to(a_g[0:64, k : k + 1], (64, 128))
            border = jnp.broadcast_to(a_g[64:128, k : k + 1], (64, 128))
            for tile in range(3):
                at = slice(128 * tile, 128 * tile + 128)
                half = base_s[:, at] + row_term
                if cuts[tile] is not None:
                    half = half - border * cuts[tile]
                p = (1.0 + jnp.tanh(half)) * masks[tile]
                act = half * p
                act_s[g, k, :, at] = act.astype(BF16)
                inner = zb[g, k, :, at] * (p + act * (2.0 - p))
                inn_s[64 * k : 64 * k + 64, at] = inner.astype(BF16)
                v_s[:, at] += inner
        v = v_s[...]
        for a in range(3):
            u_s[64 * a : 64 * a + 64] += v * flags[a]
        sums = mm(inn_s[...], m3[...])
        t = t_s[...]
        for k in range(8):
            t = jnp.where(lane2 == 8 * g + k, sums[64 * k : 64 * k + 64], t)
        t_s[...] = t
        return carry

    lax.fori_loop(0, 4, group, 0)

    def second(k, acc):
        a0, a1, a2, a3 = act_s[0, k], act_s[1, k], act_s[2, k], act_s[3, k]
        low = jnp.concatenate([a2, a0, a2, a1], axis=0)
        high = jnp.concatenate([a3, a1, a3, a2], axis=0)
        return acc + mm(gs[k], jnp.concatenate([low, high], axis=1), NT)

    two = lax.fori_loop(0, 8, second, jnp.zeros((192, 256), F32), unroll=True)
    hi_half = lax.broadcasted_iota(jnp.int32, (192, 128), 1) >= 64
    two_taps = [two[:, 0:128], two[:, 128:256], pltpu.roll(two[:, 0:128], 64, 1)]

    t_mid, t_cut = t_s[:, 0:128], t_s[:, 128:256]
    t_all = jnp.concatenate(
        [jnp.where(col == 0, t_mid - t_cut, t_mid), t_mid, jnp.where(col == nc - 1, t_mid - t_cut, t_mid)], axis=0
    )
    t_b = t_all.astype(BF16)
    u_all = u_s[...]
    u_b = u_all.astype(BF16)
    by_col = [mm(u_b, colbuf[8 * b : 8 * b + wide].astype(BF16)) for b in range(3)]
    for a in range(3):
        by_row = mm(t_b, rowbuf[8 * a : 8 * a + 128].astype(BF16))
        for b in range(3):
            tap = by_row[64 * b : 64 * b + 64] + by_col[b][64 * a : 64 * a + 64]
            tap = jnp.where(hi_half[0:64], two_taps[a][64 * b : 64 * b + 64], tap)
            at = 64 * (3 * a + b)
            pk32[at : at + 64] = tap
            pk[at : at + 64] = tap.astype(BF16)
    if nc * share > 576:
        pk32[576:] = jnp.zeros((nc * share - 576, 128), F32)
        pk[576:] = jnp.zeros((nc * share - 576, 128), BF16)

    cols_p, cols_x = [], []
    for d in range(1, nc):
        src = pk.at[pl.ds(pl.multiple_of(col_peer(d) * share, 16), share)]
        cols_p.append(remote(src, p_recv.at[d - 1], ps_sem.at[d - 1], pr_sem.at[d - 1], (row, col_peer(d))))
        cols_x.append(remote(xtra, x_recv.at[d - 1], xs_sem.at[d - 1], xr_sem.at[d - 1], (row, col_peer(d))))
    for copy in cols_p:
        copy.start()

    t_t = t_all.T
    xtra32[...] = jnp.zeros_like(xtra32)
    for a in range(3):
        part = mm(t_t.astype(BF16), k1_ref[a].reshape(192, 64))
        xtra32[8 * a : 8 * a + 32, 0:64] += part[0:32]
    xtra32[16:32, 0:64] += rsum.T[8:24]
    xtra32[48:49, 0:64] = jnp.sum(t_t, axis=0, keepdims=True)[:, 64:128]
    parts = [mm(k1t[b], u_b) for b in range(3)]
    col_part = pltpu.roll(parts[0], wide - 8, 1) + parts[1] + pltpu.roll(parts[2], 8, 1)
    xtra32[64:128] = col_part[:, cols:wide]
    xtra[...] = xtra32[...].astype(BF16)

    for copy in cols_x:
        copy.start()

    col_main = col_part[:, 0:cols] + gsum
    for copy in cols_p:
        copy.wait_recv()
    mine = pk32[pl.ds(pl.multiple_of(col * share, 16), share)]
    for d in range(1, nc):
        mine = mine + p_recv[d - 1].astype(F32)
    dd32[0:share] = mine
    for copy in cols_x:
        copy.wait_recv()
    line = xtra32[0:64]
    for d in range(1, nc):
        line = line + x_recv[d - 1, 0:64].astype(F32)
    side = lax.broadcasted_iota(jnp.int32, (64, 128), 1)
    from_left = jnp.where(jnp.logical_and(side < 16, col > 0), x_recv[0, 64:128].astype(F32), 0.0)
    from_right = jnp.where(jnp.logical_and(side >= 112, col < nc - 1), x_recv[nc - 2, 64:128].astype(F32), 0.0)

    dd32[share : share + 64] = col_main[:, 0:128] + from_left
    dd32[share + 64 : share + 128] = col_main[:, 128:256] + from_right
    dd32[share + 128 : share + 144] = line[48:64]
    if n * chunk > share + 144:
        dd32[share + 144 :] = jnp.zeros((n * chunk - share - 144, 128), F32)
    dd[...] = dd32[...].astype(BF16)
    nb[...] = line[0:48].astype(BF16)
    scatter = []
    for d in range(1, n):
        src = dd.at[pl.ds(pl.multiple_of(row_peer(d) * chunk, 16), chunk)]
        scatter.append(remote(src, d_recv.at[pl.ds((d - 1) * chunk, chunk)], ds_sem.at[0], dr_sem.at[0], (row_peer(d), col)))
    near = [
        remote(nb.at[pl.ds(32, 16)], nb_recv.at[0], ns_sem.at[0], nr_sem.at[0], (row_peer(1), col)),
        remote(nb.at[pl.ds(0, 16)], nb_recv.at[1], ns_sem.at[1], nr_sem.at[1], (row_peer(n - 1), col)),
    ]
    for copy in scatter + near:
        copy.start()
    spot = pl.ds(pl.multiple_of(row * chunk, 16), chunk)
    done = dd32[spot]
    most = (n - 1) * chunk
    all_in = remote(dd.at[pl.ds(0, most)], d_recv, ds_sem.at[0], dr_sem.at[0], (row_peer(1), col))
    all_in.wait_recv()
    for d in range(1, n):
        done = done + d_recv[(d - 1) * chunk : d * chunk].astype(F32)
    full[spot] = done.astype(BF16)
    gather = []
    for d in range(1, n):
        gather.append(remote(full.at[spot], full.at[spot], as_sem.at[0], ar_sem.at[0], (row_peer(d), col)))
    for copy in gather:
        copy.start()
    for copy in near:
        copy.wait_recv()
    low = jnp.where(row > 0, nb_recv[0].astype(F32), 0.0)
    high = jnp.where(row < n - 1, nb_recv[1].astype(F32), 0.0)
    rg_ref[...] = line[16:32] + low + high
    all_out = remote(full.at[pl.ds(0, most)], full.at[pl.ds(0, most)], as_sem.at[0], ar_sem.at[0], (row_peer(1), col))
    all_out.wait_recv()

    own = pl.ds(pl.multiple_of(col * share, 16), share)
    last = []
    for d in range(1, nc):
        last.append(remote(full.at[pl.ds(0, share)], pfull.at[own], cs_sem.at[d - 1], cr_sem.at[d - 1], (row, col_peer(d))))
    for copy in last:
        copy.start()
    pfull[own] = full[0:share]
    for d in range(1, nc):
        other = pl.ds(pl.multiple_of(col_peer(nc - d) * share, 16), share)
        remote(full.at[pl.ds(0, share)], pfull.at[other], cs_sem.at[d - 1], cr_sem.at[d - 1], (row, col_peer(d))).wait_recv()
    for copy in feats + cols_p + cols_x + [all_in, all_out] + near + last:
        copy.wait_send()


def finish(n, nc, share, rg_in, full, pfull, rg_ref, cg_ref, g1_ref, gb_ref, g2_ref):
    whole = 1.0 / math.sqrt(16 * n * 256 * nc)
    tall = 1.0 / math.sqrt(16 * n)
    rg_ref[...] = rg_in[:, 0:64] * (1.0 / math.sqrt(256 * nc))
    cg_ref[:, 0:128] = full[share : share + 64].astype(F32) * tall
    cg_ref[:, 128:256] = full[share + 64 : share + 128].astype(F32) * tall
    gb_ref[...] = full[share + 128 : share + 144].astype(F32)[0:1, 0:64] * whole
    for a in range(3):
        for b in range(3):
            at = 64 * (3 * a + b)
            tap = pfull[at : at + 64].astype(F32) * whole
            g1_ref[a, b] = tap[:, 0:64]
            g2_ref[a, b] = tap[:, 64:128]


def shards(n, nc, grad_out, row_feat, col_feat, conv_one, bias_one, conv_two):
    share = round_up(-(-576 // nc), 16)
    chunk = round_up(-(-(share + 144) // n), 16)
    vmem = pl.BlockSpec(memory_space=pltpu.VMEM)
    dma = pltpu.SemaphoreType.DMA
    scratch = [
        pltpu.VMEM((64, 16, 256), BF16),
        pltpu.VMEM((16, 64), BF16),
        pltpu.VMEM((64, 256), BF16),
        pltpu.VMEM((3, 3, 64, 64), BF16),
        pltpu.VMEM((1, 64), F32),
        pltpu.VMEM((3, 3, 64, 64), BF16),
        pltpu.VMEM((2, 16, 64), BF16),
        dma((6,)),
        pltpu.VMEM((3, 64, 192), BF16),
        pltpu.VMEM((192, 192), BF16),
        pltpu.VMEM((160, 128), F32),
        pltpu.VMEM((400, 128), F32),
        pltpu.VMEM((2, 16, 64), BF16),
        pltpu.VMEM((2, 16, 64), BF16),
        pltpu.VMEM((8, 192, 768), BF16),
        pltpu.VMEM((4, 8, 64, 384), F32),
        pltpu.VMEM((4, 8, 64, 384), BF16),
        pltpu.VMEM((512, 384), BF16),
        pltpu.VMEM((4, 128, 128), F32),
        pltpu.VMEM((192, 384), F32),
        pltpu.VMEM((64, 256), F32),
        pltpu.VMEM((192, 384), F32),
        pltpu.VMEM((384, 256), BF16),
        pltpu.VMEM((64, 384), F32),
        pltpu.VMEM((64, 384), F32),
        pltpu.VMEM((nc * share, 128), BF16),
        pltpu.VMEM((nc * share, 128), F32),
        pltpu.VMEM((128, 128), BF16),
        pltpu.VMEM((128, 128), F32),
        pltpu.VMEM((nc - 1, share, 128), BF16),
        pltpu.VMEM((nc - 1, 128, 128), BF16),
        pltpu.VMEM((n * chunk, 128), BF16),
        pltpu.VMEM((n * chunk, 128), F32),
        pltpu.VMEM((48, 128), BF16),
        pltpu.VMEM((2, 16, 128), BF16),
        pltpu.VMEM(((n - 1) * chunk, 128), BF16),
        dma((4,)), dma((4,)),
        dma((nc - 1,)), dma((nc - 1,)),
        dma((nc - 1,)), dma((nc - 1,)),
        dma((1,)), dma((1,)),
        dma((2,)), dma((2,)),
        dma((1,)), dma((1,)),
        dma((nc - 1,)), dma((nc - 1,)),
    ]
    sums = pl.pallas_call(
        functools.partial(kernel, n, nc, share, chunk),
        out_shape=(
            jax.ShapeDtypeStruct((16, 128), F32),
            jax.ShapeDtypeStruct((n * chunk, 128), BF16),
            jax.ShapeDtypeStruct((nc * share, 128), BF16),
        ),
        in_specs=[pl.BlockSpec(memory_space=pltpu.HBM)] * 6,
        out_specs=(vmem,) * 3,
        scratch_shapes=scratch,
        compiler_params=pltpu.CompilerParams(
            collective_id=0, has_side_effects=True, vmem_limit_bytes=60 * 2**20
        ),
    )(grad_out, row_feat, col_feat.T, conv_one, bias_one.reshape(1, 64), conv_two)
    out = pl.pallas_call(
        functools.partial(finish, n, nc, share),
        out_shape=(
            jax.ShapeDtypeStruct((16, 64), F32),
            jax.ShapeDtypeStruct((64, 256), F32),
            jax.ShapeDtypeStruct((3, 3, 64, 64), F32),
            jax.ShapeDtypeStruct((1, 64), F32),
            jax.ShapeDtypeStruct((3, 3, 64, 64), F32),
        ),
        in_specs=[vmem] * 3,
        out_specs=(vmem,) * 5,
        compiler_params=pltpu.CompilerParams(vmem_limit_bytes=60 * 2**20),
    )(*sums)
    return (out[0], out[1].T, out[2], out[3].reshape(64), out[4])


def solution(mesh):
    n, nc = mesh.shape["row"], mesh.shape["col"]
    in_specs = (P(None, "row", "col"), P("row", None), P("col", None), P(), P(), P())
    out_specs = (P("row", None), P("col", None), P(), P(), P())
    return jax.shard_map(
        functools.partial(shards, n, nc), mesh=mesh, in_specs=in_specs, out_specs=out_specs, check_vma=False
    )
```

```python
import functools
import math

import jax
import jax.numpy as jnp
from jax import lax
from jax.experimental import pallas as pl
from jax.experimental.pallas import tpu as pltpu
from jax.sharding import PartitionSpec as P

F32 = jnp.float32
BF16 = jnp.bfloat16
MESH = pl.DeviceIdType.MESH
NN = (((1,), (0,)), ((), ()))
NT = (((1,), (1,)), ((), ()))


def mm(x, y, dims=NN):
    return lax.dot_general(x, y, dims, preferred_element_type=F32)


def round_up(value, unit):
    return -(-value // unit) * unit


def kernel(
    n, nc, m, take, chunk,
    g_hbm, row_hbm, col_hbm, k1_hbm, bias_hbm, k2_hbm,
    misc_ref, whole_ref,
    g_ref, row_ref, col_ref, k1_ref, bias_ref, k2_ref, csend, in_sem, k1t, k2t,
    rowbuf, colbuf, rrecv, crecv,
    gs, zb, act_s, inn_s, a_s, b_s, t_s, u_s, m3, base_s, v_s,
    pk32, line, line_b, line_recv, near32, near_b, near_recv, acc32, acc_b, far_recv, total_b,
    fs_sem, fr_sem, ls_sem, lr_sem, ns_sem, nr_sem, zs_sem, zr_sem, ws_sem, wr_sem, os_sem, or_sem,
):
    row = lax.axis_index("row")
    col = lax.axis_index("col")
    rows, cols, wide = 16, 256, 384

    def row_peer(d):
        return lax.rem(row + d, n)

    def col_peer(d):
        return lax.rem(col + d, nc)

    loads = [
        pltpu.make_async_copy(src, dst, in_sem.at[i])
        for i, (src, dst) in enumerate(
            [(g_hbm, g_ref), (row_hbm, row_ref), (col_hbm, col_ref), (k1_hbm, k1_ref), (bias_hbm, bias_ref), (k2_hbm, k2_ref)]
        )
    ]
    for load in loads:
        load.start()
    barrier = pltpu.get_barrier_semaphore()
    nz = n // m
    plane, spot = lax.div(row, m), lax.rem(row, m)
    steps = [(dp, dc) for dp in range(m) for dc in range(nc) if dp or dc]

    def group_peer(dp, dc):
        return plane * m + lax.rem(spot + dp, m), col_peer(dc)

    def far_peer(d):
        return lax.rem(plane + d, nz) * m + spot, col

    friends = [group_peer(dp, dc) for dp, dc in steps] + [far_peer(d) for d in range(1, nz)]
    friends += [(row_peer(d), col_peer(dc)) for d in (1, n - 1) for dc in range(nc)]
    for friend in friends:
        pl.semaphore_signal(barrier, inc=1, device_id=friend, device_id_type=MESH)

    def remote(src, dst, send, recv, to):
        return pltpu.make_async_remote_copy(
            src_ref=src, dst_ref=dst, send_sem=send, recv_sem=recv, device_id=to, device_id_type=MESH
        )

    pa = lax.broadcasted_iota(jnp.int32, (256, 256), 0)
    pb = lax.broadcasted_iota(jnp.int32, (256, 256), 1)
    perm = ((pa & 15) * 16 + (pa >> 4) == pb).astype(F32).astype(BF16)
    sa = lax.broadcasted_iota(jnp.int32, (256, wide), 0)
    sb = lax.broadcasted_iota(jnp.int32, (256, wide), 1)
    gap = sb - sa
    shifts = jnp.concatenate(
        [
            jnp.logical_or(gap == -8, gap == wide - 8).astype(F32).astype(BF16),
            (gap == 8).astype(F32).astype(BF16),
        ],
        axis=1,
    )
    rowbuf[...] = jnp.zeros_like(rowbuf)
    colbuf[...] = jnp.zeros_like(colbuf)
    loads[1].wait()
    loads[2].wait()
    rowbuf[16:32, 0:64] = row_ref[...].astype(F32)
    col_t = col_ref[...].astype(F32).T
    colbuf[8 : 8 + cols, 0:64] = col_t
    colbuf[392:400, 0:64] = col_t[0:8]
    csend[0] = col_t[cols - 16 : cols].astype(BF16)
    csend[1] = col_t[0:16].astype(BF16)
    loads[0].wait()

    blank = jnp.zeros((256, wide - cols), BF16)

    def build(og):
        x = g_ref[pl.ds(og * 16, 16)].reshape(256, cols)
        plain = mm(perm, x).astype(BF16)
        moved = mm(plain, shifts).astype(BF16)
        turns = [moved[:, :wide], jnp.concatenate([plain, blank], axis=1), moved[:, wide:]]
        for r in range(rows):
            h, k = r // 8, r % 8
            for b in range(3):
                gs[k, pl.ds(b * 64 + og * 16, 16), h * wide : (h + 1) * wide] = turns[b][16 * r : 16 * r + 16]

    for og in range(4):
        build(og)

    pl.semaphore_wait(barrier, len(friends))
    feats = [
        remote(row_ref, rrecv.at[0], fs_sem.at[0], fr_sem.at[0], (row_peer(1), col)),
        remote(row_ref, rrecv.at[1], fs_sem.at[1], fr_sem.at[1], (row_peer(n - 1), col)),
        remote(csend.at[0], crecv.at[0], fs_sem.at[2], fr_sem.at[2], (row, col_peer(1))),
        remote(csend.at[1], crecv.at[1], fs_sem.at[3], fr_sem.at[3], (row, col_peer(nc - 1))),
    ]
    for copy in feats:
        copy.start()

    for load in loads[3:]:
        load.wait()
    for a in range(3):
        k2t[64 * a : 64 * a + 64] = (0.5 * k2_ref[a].reshape(192, 64).astype(F32).T).astype(BF16)
    w2 = k2t[...]
    lane = lax.broadcasted_iota(jnp.int32, (64, 128), 1)

    def spread(k, carry):
        gsum, rsum = carry
        both = gs[k]
        z = mm(w2, both)
        lo, hi = z[:, :wide], z[:, wide:]
        zb[0, k] = lo[0:64]
        zb[1, k] = lo[64:128] + hi[0:64]
        zb[2, k] = lo[128:192] + hi[64:128]
        zb[3, k] = hi[128:192]
        mid = both[64:128].astype(F32)
        first, second = mid[:, 0:cols], mid[:, wide : wide + cols]
        rsum = jnp.where(lane == 8 + k, jnp.sum(first, axis=1, keepdims=True), rsum)
        rsum = jnp.where(lane == 16 + k, jnp.sum(second, axis=1, keepdims=True), rsum)
        return gsum + first + second, rsum

    gsum, rsum = lax.fori_loop(
        0, 8, spread, (jnp.zeros((64, cols), F32), jnp.zeros((64, 128), F32)), unroll=4
    )

    ma = lax.broadcasted_iota(jnp.int32, (wide, 128), 0)
    cut_low = jnp.logical_and(ma < 8, col == 0)
    cut_high = jnp.logical_and(jnp.logical_and(ma >= cols - 8, ma < cols), col == nc - 1)
    m3[:, 0:128] = jnp.ones((wide, 128), BF16)
    m3[:, 128:256] = jnp.where(jnp.logical_or(cut_low, cut_high), 1.0, 0.0).astype(BF16)
    for b in range(3):
        k1_b = jnp.concatenate([k1_ref[a, b] for a in range(3)], axis=0)
        k1t[b] = k1_b.astype(F32).T.astype(BF16)
    for copy in feats:
        copy.wait_recv()
    rowbuf[0:16, 0:64] = jnp.where(row > 0, rrecv[0].astype(F32), 0.0)
    rowbuf[32:48, 0:64] = jnp.where(row < n - 1, rrecv[1].astype(F32), 0.0)
    left = jnp.where(col > 0, crecv[0].astype(F32), 0.0)
    colbuf[376:392, 0:64] = left
    colbuf[0:8, 0:64] = left[8:16]
    colbuf[264:280, 0:64] = jnp.where(col < nc - 1, crecv[1].astype(F32), 0.0)

    a_all = jnp.zeros((192, 128), F32)
    for a in range(3):
        a_all += mm(
            k1_ref[a].reshape(192, 64), rowbuf[8 * a : 8 * a + 128, 0:64].astype(BF16), NT
        )
    a_all = 0.5 * a_all
    for g in range(4):
        turned = a_all if g == 0 else pltpu.roll(a_all, 128 - 8 * g, 1)
        a_s[g, 0:64] = turned[0:64] + turned[64:128] + turned[128:192]
        a_s[g, 64:128] = jnp.where(col == 0, turned[0:64], turned[128:192])
    b_all = jnp.zeros((192, wide), F32)
    for b in range(3):
        k1_b = jnp.concatenate([k1_ref[a, b] for a in range(3)], axis=0)
        b_all += mm(k1_b, colbuf[8 * b : 8 * b + wide, 0:64].astype(BF16), NT)
    eye = lax.broadcasted_iota(jnp.int32, (64, 64), 0) == lax.broadcasted_iota(jnp.int32, (64, 64), 1)
    bias = 0.5 * jnp.sum(jnp.where(eye, bias_ref[...], 0.0), axis=1, keepdims=True)
    b_s[...] = 0.5 * b_all

    lanes = lax.broadcasted_iota(jnp.int32, (1, wide), 1)
    on_left = jnp.logical_and(lanes >= wide - 8, col > 0)
    on_right = jnp.logical_and(jnp.logical_and(lanes >= cols, lanes < cols + 8), col < nc - 1)
    inside_cols = jnp.where(
        jnp.logical_or(lanes < cols, jnp.logical_or(on_left, on_right)), 1.0, 0.0
    ).astype(F32)
    lane1 = lax.broadcasted_iota(jnp.int32, (1, 128), 1)
    low_cut = jnp.where(jnp.logical_and(lane1 < 8, col == 0), 1.0, 0.0).astype(F32)
    high_cut = jnp.where(jnp.logical_and(lane1 >= 120, col == nc - 1), 1.0, 0.0).astype(F32)
    total = rows * n
    lane2 = lax.broadcasted_iota(jnp.int32, (64, 256), 1) & 127
    t_s[...] = jnp.zeros_like(t_s)
    u_s[...] = jnp.zeros_like(u_s)

    def group(g, carry):
        start = row * rows + 8 * (g - 1)

        def flag(first):
            return jnp.where(jnp.logical_and(first >= 0, first < total), 1.0, 0.0).astype(F32)

        flags = [flag(start + 8 * (a - 1)) for a in range(3)]
        base_s[...] = bias + sum(b_s[64 * a : 64 * a + 64] * flags[a] for a in range(3))
        in_map = flag(start)
        masks = [in_map, in_map, inside_cols[:, 256:384] * in_map]
        cuts = [low_cut, high_cut, None]
        a_g = a_s[g]
        v_s[...] = jnp.zeros_like(v_s)
        for k in range(8):
            row_term = jnp.broadcast_to(a_g[0:64, k : k + 1], (64, 128))
            border = jnp.broadcast_to(a_g[64:128, k : k + 1], (64, 128))
            for tile in range(3):
                at = slice(128 * tile, 128 * tile + 128)
                half = base_s[:, at] + row_term
                if cuts[tile] is not None:
                    half = half - border * cuts[tile]
                p = (1.0 + jnp.tanh(half)) * masks[tile]
                act = half * p
                act_s[g, k, :, at] = act.astype(BF16)
                inner = zb[g, k, :, at] * (p + act * (2.0 - p))
                inn_s[64 * k : 64 * k + 64, at] = inner.astype(BF16)
                v_s[:, at] += inner
        v = v_s[...]
        for a in range(3):
            u_s[64 * a : 64 * a + 64] += v * flags[a]
        sums = mm(inn_s[...], m3[...])
        t = t_s[...]
        for k in range(8):
            t = jnp.where(lane2 == 8 * g + k, sums[64 * k : 64 * k + 64], t)
        t_s[...] = t
        return carry

    lax.fori_loop(0, 4, group, 0)

    def second(k, acc):
        a0, a1, a2, a3 = act_s[0, k], act_s[1, k], act_s[2, k], act_s[3, k]
        low = jnp.concatenate([a2, a0, a2, a1], axis=0)
        high = jnp.concatenate([a3, a1, a3, a2], axis=0)
        return acc + mm(gs[k], jnp.concatenate([low, high], axis=1), NT)

    two = lax.fori_loop(0, 8, second, jnp.zeros((192, 256), F32), unroll=True)
    hi_half = lax.broadcasted_iota(jnp.int32, (192, 128), 1) >= 64
    two_taps = [two[:, 0:128], two[:, 128:256], pltpu.roll(two[:, 0:128], 64, 1)]

    t_mid, t_cut = t_s[:, 0:128], t_s[:, 128:256]
    t_all = jnp.concatenate(
        [jnp.where(col == 0, t_mid - t_cut, t_mid), t_mid, jnp.where(col == nc - 1, t_mid - t_cut, t_mid)], axis=0
    )
    t_b = t_all.astype(BF16)
    u_all = u_s[...]
    u_b = u_all.astype(BF16)
    by_col = [mm(u_b, colbuf[8 * b : 8 * b + wide].astype(BF16)) for b in range(3)]
    for a in range(3):
        by_row = mm(t_b, rowbuf[8 * a : 8 * a + 128].astype(BF16))
        for b in range(3):
            tap = by_row[64 * b : 64 * b + 64] + by_col[b][64 * a : 64 * a + 64]
            tap = jnp.where(hi_half[0:64], two_taps[a][64 * b : 64 * b + 64], tap)
            at = 64 * (3 * a + b)
            pk32[at : at + 64] = tap
    if m * nc * take > 576:
        pk32[576:] = jnp.zeros((m * nc * take - 576, 128), F32)

    t_t = t_all.T
    near32[...] = jnp.zeros_like(near32)
    for a in range(3):
        part = mm(t_t.astype(BF16), k1_ref[a].reshape(192, 64))
        near32[8 * a : 8 * a + 32, 0:64] += part[0:32]
    near32[16:32, 0:64] += rsum.T[8:24]
    near_b[...] = near32[...].astype(BF16)
    near = []
    for q in range(3):
        for dc in range(nc):
            if q != 1 or dc:
                near.append(
                    remote(
                        near_b.at[pl.ds(16 * q, 16)], near_recv.at[pl.ds(16 * (q * nc + dc), 16)],
                        ns_sem.at[0], nr_sem.at[0], (row_peer((q - 1 + n) % n), col_peer(dc)),
                    )
                )
    bias_sum = jnp.sum(t_t, axis=0, keepdims=True)[:, 64:128]
    parts = [mm(k1t[b], u_b) for b in range(3)]
    col_part = pltpu.roll(parts[0], wide - 8, 1) + parts[1] + pltpu.roll(parts[2], 8, 1)
    col_main, edge = col_part[:, 0:cols] + gsum, col_part[:, cols:wide]
    side = lax.broadcasted_iota(jnp.int32, (64, 128), 1)
    to_right, to_left = jnp.where(side < 16, edge, 0.0), jnp.where(side >= 112, edge, 0.0)

    size, strip = nz * chunk, 128 // m
    line[...] = jnp.zeros_like(line)
    for c in range(nc):
        halves = jnp.concatenate(
            [
                jnp.where(col == c, col_main[:, 0:128], jnp.where(col + 1 == c, to_right, 0.0)),
                jnp.where(col == c, col_main[:, 128:256], jnp.where(col - 1 == c, to_left, 0.0)),
            ],
            axis=0,
        )
        for p in range(m):
            at = (p * nc + c) * size
            line[at : at + take] = pk32[(p * nc + c) * take : (p * nc + c + 1) * take]
            line[at + take : at + take + strip] = halves[p * strip : (p + 1) * strip]
            line[at + take + strip : at + take + strip + 1, 0:64] = bias_sum
    line_b[...] = line[...].astype(BF16)

    def part_of(p, c):
        return pl.multiple_of((p * nc + c) * size, 16)

    for i, (dp, dc) in enumerate(steps):
        src = line_b.at[pl.ds(part_of(lax.rem(spot + dp, m), col_peer(dc)), size)]
        remote(src, line_recv.at[pl.ds(i * size, size)], ls_sem.at[0], lr_sem.at[0], group_peer(dp, dc)).start()
    for copy in near:
        copy.start()
    next_door = (row_peer(1), col)
    most = len(steps) * size
    line_all = remote(line_b.at[pl.ds(0, most)], line_recv, ls_sem.at[0], lr_sem.at[0], next_door)
    own = pl.ds(part_of(spot, col), size)
    acc = line[own]
    line_all.wait_recv()
    for i in range(len(steps)):
        acc = acc + line_recv[i * size : (i + 1) * size].astype(F32)
    acc32[...] = acc
    acc_b[...] = acc.astype(BF16)

    for d in range(1, nz):
        src = acc_b.at[pl.ds(pl.multiple_of(lax.rem(plane + d, nz) * chunk, 16), chunk)]
        remote(src, far_recv.at[pl.ds((d - 1) * chunk, chunk)], zs_sem.at[0], zr_sem.at[0], far_peer(d)).start()
    rest = (nz - 1) * chunk
    far_all = remote(acc_b.at[pl.ds(0, rest)], far_recv, zs_sem.at[0], zr_sem.at[0], next_door)
    mine = pl.ds(pl.multiple_of(plane * chunk, 16), chunk)
    done = acc32[mine]
    far_all.wait_recv()
    for d in range(nz - 1):
        done = done + far_recv[d * chunk : (d + 1) * chunk].astype(F32)
    total_b[mine] = done.astype(BF16)
    for d in range(1, nz):
        remote(total_b.at[mine], total_b.at[mine], zs_sem.at[1], zr_sem.at[1], far_peer(d)).start()

    near_all = remote(near_recv.at[pl.ds(0, 16 * len(near))], near_recv.at[pl.ds(0, 16 * len(near))], ns_sem.at[0], nr_sem.at[0], next_door)
    near_all.wait_recv()
    here = near32[16:32]
    for dc in range(nc):
        here = here + jnp.where(row < n - 1, near_recv[16 * dc : 16 * dc + 16].astype(F32), 0.0)
        here = here + jnp.where(row > 0, near_recv[16 * (2 * nc + dc) : 16 * (2 * nc + dc) + 16].astype(F32), 0.0)
        if dc:
            here = here + near_recv[16 * (nc + dc) : 16 * (nc + dc) + 16].astype(F32)
    misc_ref[0:16] = here

    plane_all = remote(total_b.at[pl.ds(0, rest)], total_b.at[pl.ds(0, rest)], zs_sem.at[1], zr_sem.at[1], next_door)
    plane_all.wait_recv()

    long, short = round_up(take + strip + 1, 16), round_up(take, 16)
    place = part_of(spot, col)
    for dp, dc in steps:
        if dc:
            there = pl.ds(place, short)
            remote(total_b.at[pl.ds(0, short)], whole_ref.at[there], os_sem.at[0], or_sem.at[0], group_peer(dp, dc)).start()
        else:
            there = pl.ds(place, long)
            remote(total_b.at[pl.ds(0, long)], whole_ref.at[there], ws_sem.at[0], wr_sem.at[0], group_peer(dp, dc)).start()
    whole_ref[own] = total_b[...]
    waits = []
    for count, sems in (((m - 1) * long, (ws_sem, wr_sem)), ((len(steps) - m + 1) * short, (os_sem, or_sem))):
        if count:
            span = pl.ds(0, count)
            waits.append(remote(whole_ref.at[span], whole_ref.at[span], sems[0].at[0], sems[1].at[0], next_door))
    for copy in waits:
        copy.wait_recv()
    for p in range(m):
        at = part_of(p, col) + take
        misc_ref[16 + p * strip : 16 + (p + 1) * strip] = whole_ref[pl.ds(pl.multiple_of(at - take, 16), size)].astype(F32)[take : take + strip]
    misc_ref[144:152] = total_b[...].astype(F32)[take + strip : take + strip + 8]
    for copy in feats + [line_all, far_all, near_all, plane_all] + waits:
        copy.wait_send()


def finish(n, nc, m, take, size, misc, whole_in, rg_ref, cg_ref, g1_ref, gb_ref, g2_ref):
    whole = 1.0 / math.sqrt(16 * n * 256 * nc)
    tall = 1.0 / math.sqrt(16 * n)
    rg_ref[...] = misc[0:16, 0:64] * (1.0 / math.sqrt(256 * nc))
    cg_ref[:, 0:128] = misc[16:80] * tall
    cg_ref[:, 128:256] = misc[80:144] * tall
    gb_ref[...] = misc[144:145, 0:64] * whole
    pieces = [whole_in[i * size : i * size + round_up(take, 16)].astype(F32)[0:take] * whole for i in range(m * nc)]
    taps = jnp.concatenate(pieces, axis=0)
    for a in range(3):
        for b in range(3):
            at = 64 * (3 * a + b)
            g1_ref[a, b] = taps[at : at + 64, 0:64]
            g2_ref[a, b] = taps[at : at + 64, 64:128]


def shards(n, nc, grad_out, row_feat, col_feat, conv_one, bias_one, conv_two):
    m = 4 if n % 4 == 0 and n > 4 else 1
    take = round_up(-(-576 // (m * nc)), 8)
    chunk = round_up(-(-(take + 128 // m + 8) // (n // m)), 16)
    size, parts = chunk * (n // m), m * nc
    vmem = pl.BlockSpec(memory_space=pltpu.VMEM)
    dma = pltpu.SemaphoreType.DMA
    scratch = [
        pltpu.VMEM((64, 16, 256), BF16),
        pltpu.VMEM((16, 64), BF16),
        pltpu.VMEM((64, 256), BF16),
        pltpu.VMEM((3, 3, 64, 64), BF16),
        pltpu.VMEM((1, 64), F32),
        pltpu.VMEM((3, 3, 64, 64), BF16),
        pltpu.VMEM((2, 16, 64), BF16),
        dma((6,)),
        pltpu.VMEM((3, 64, 192), BF16),
        pltpu.VMEM((192, 192), BF16),
        pltpu.VMEM((160, 128), F32),
        pltpu.VMEM((400, 128), F32),
        pltpu.VMEM((2, 16, 64), BF16),
        pltpu.VMEM((2, 16, 64), BF16),
        pltpu.VMEM((8, 192, 768), BF16),
        pltpu.VMEM((4, 8, 64, 384), F32),
        pltpu.VMEM((4, 8, 64, 384), BF16),
        pltpu.VMEM((512, 384), BF16),
        pltpu.VMEM((4, 128, 128), F32),
        pltpu.VMEM((192, 384), F32),
        pltpu.VMEM((64, 256), F32),
        pltpu.VMEM((192, 384), F32),
        pltpu.VMEM((384, 256), BF16),
        pltpu.VMEM((64, 384), F32),
        pltpu.VMEM((64, 384), F32),
        pltpu.VMEM((parts * take, 128), F32),
        pltpu.VMEM((parts * size, 128), F32),
        pltpu.VMEM((parts * size, 128), BF16),
        pltpu.VMEM(((parts - 1) * size, 128), BF16),
        pltpu.VMEM((48, 128), F32),
        pltpu.VMEM((48, 128), BF16),
        pltpu.VMEM((3 * nc * 16, 128), BF16),
        pltpu.VMEM((size, 128), F32),
        pltpu.VMEM((size, 128), BF16),
        pltpu.VMEM((size - chunk, 128), BF16),
        pltpu.VMEM((size, 128), BF16),
        dma((4,)), dma((4,)),
        *[dma((1,))] * 4,
        *[dma((2,))] * 2,
        *[dma((1,))] * 4,
    ]
    sums = pl.pallas_call(
        functools.partial(kernel, n, nc, m, take, chunk),
        out_shape=(
            jax.ShapeDtypeStruct((152, 128), F32),
            jax.ShapeDtypeStruct((parts * size, 128), BF16),
        ),
        in_specs=[pl.BlockSpec(memory_space=pltpu.HBM)] * 6,
        out_specs=(vmem,) * 2,
        scratch_shapes=scratch,
        compiler_params=pltpu.CompilerParams(
            collective_id=0, has_side_effects=True, vmem_limit_bytes=60 * 2**20
        ),
    )(grad_out, row_feat, col_feat.T, conv_one, bias_one.reshape(1, 64), conv_two)
    out = pl.pallas_call(
        functools.partial(finish, n, nc, m, take, size),
        out_shape=(
            jax.ShapeDtypeStruct((16, 64), F32),
            jax.ShapeDtypeStruct((64, 256), F32),
            jax.ShapeDtypeStruct((3, 3, 64, 64), F32),
            jax.ShapeDtypeStruct((1, 64), F32),
            jax.ShapeDtypeStruct((3, 3, 64, 64), F32),
        ),
        in_specs=[vmem] * 2,
        out_specs=(vmem,) * 5,
        compiler_params=pltpu.CompilerParams(vmem_limit_bytes=60 * 2**20),
    )(*sums)
    return (out[0], out[1].T, out[2], out[3].reshape(64), out[4])


def solution(mesh):
    n, nc = mesh.shape["row"], mesh.shape["col"]
    in_specs = (P(None, "row", "col"), P("row", None), P("col", None), P(), P(), P())
    out_specs = (P("row", None), P("col", None), P(), P(), P())
    return jax.shard_map(
        functools.partial(shards, n, nc), mesh=mesh, in_specs=in_specs, out_specs=out_specs, check_vma=False
    )
```

```python
import functools
import math

import jax
import jax.numpy as jnp
from jax import lax
from jax.experimental import pallas as pl
from jax.experimental.pallas import tpu as pltpu
from jax.sharding import PartitionSpec as P

F32 = jnp.float32
BF16 = jnp.bfloat16
MESH = pl.DeviceIdType.MESH
NN = (((1,), (0,)), ((), ()))
NT = (((1,), (1,)), ((), ()))


def mm(x, y, dims=NN):
    return lax.dot_general(x, y, dims, preferred_element_type=F32)


def round_up(value, unit):
    return -(-value // unit) * unit


def kernel(
    n, nc, share, chunk,
    g_hbm, row_hbm, col_hbm, k1_hbm, bias_hbm, k2_hbm,
    rg_ref, full, pfull,
    g_ref, row_ref, col_ref, k1_ref, bias_ref, k2_ref, csend, in_sem, k1t, k2t,
    rowbuf, colbuf, rrecv, crecv,
    gs, zb, act_s, inn_s, a_s, b_s, t_s, u_s, m3, base_s, v_s,
    pk, pk32, xtra, xtra32, p_recv, x_recv,
    dd, dd32, nb, nb_recv, d_recv,
    fs_sem, fr_sem, ps_sem, pr_sem, xs_sem, xr_sem,
    ds_sem, dr_sem, ns_sem, nr_sem, as_sem, ar_sem, cs_sem, cr_sem,
):
    row = lax.axis_index("row")
    col = lax.axis_index("col")
    rows, cols, wide = 16, 256, 384

    def row_peer(d):
        return lax.rem(row + d, n)

    def col_peer(d):
        return lax.rem(col + d, nc)

    loads = [
        pltpu.make_async_copy(src, dst, in_sem.at[i])
        for i, (src, dst) in enumerate(
            [(g_hbm, g_ref), (row_hbm, row_ref), (col_hbm, col_ref), (k1_hbm, k1_ref), (bias_hbm, bias_ref), (k2_hbm, k2_ref)]
        )
    ]
    for load in loads:
        load.start()
    barrier = pltpu.get_barrier_semaphore()
    for d in range(1, n):
        pl.semaphore_signal(barrier, inc=1, device_id=(row_peer(d), col), device_id_type=MESH)
    for d in range(1, nc):
        pl.semaphore_signal(barrier, inc=1, device_id=(row, col_peer(d)), device_id_type=MESH)

    def remote(src, dst, send, recv, to):
        return pltpu.make_async_remote_copy(
            src_ref=src, dst_ref=dst, send_sem=send, recv_sem=recv, device_id=to, device_id_type=MESH
        )

    pa = lax.broadcasted_iota(jnp.int32, (256, 256), 0)
    pb = lax.broadcasted_iota(jnp.int32, (256, 256), 1)
    perm = ((pa & 15) * 16 + (pa >> 4) == pb).astype(F32).astype(BF16)
    sa = lax.broadcasted_iota(jnp.int32, (256, wide), 0)
    sb = lax.broadcasted_iota(jnp.int32, (256, wide), 1)
    gap = sb - sa
    shifts = jnp.concatenate(
        [
            jnp.logical_or(gap == -8, gap == wide - 8).astype(F32).astype(BF16),
            (gap == 8).astype(F32).astype(BF16),
        ],
        axis=1,
    )
    rowbuf[...] = jnp.zeros_like(rowbuf)
    colbuf[...] = jnp.zeros_like(colbuf)
    loads[1].wait()
    loads[2].wait()
    rowbuf[16:32, 0:64] = row_ref[...].astype(F32)
    col_t = col_ref[...].astype(F32).T
    colbuf[8 : 8 + cols, 0:64] = col_t
    colbuf[392:400, 0:64] = col_t[0:8]
    csend[0] = col_t[cols - 16 : cols].astype(BF16)
    csend[1] = col_t[0:16].astype(BF16)
    loads[0].wait()

    blank = jnp.zeros((256, wide - cols), BF16)

    def build(og):
        x = g_ref[pl.ds(og * 16, 16)].reshape(256, cols)
        plain = mm(perm, x).astype(BF16)
        moved = mm(plain, shifts).astype(BF16)
        turns = [moved[:, :wide], jnp.concatenate([plain, blank], axis=1), moved[:, wide:]]
        for r in range(rows):
            h, k = r // 8, r % 8
            for b in range(3):
                gs[k, pl.ds(b * 64 + og * 16, 16), h * wide : (h + 1) * wide] = turns[b][16 * r : 16 * r + 16]

    for og in range(4):
        build(og)

    pl.semaphore_wait(barrier, (n - 1) + (nc - 1))
    feats = [
        remote(row_ref, rrecv.at[0], fs_sem.at[0], fr_sem.at[0], (row_peer(1), col)),
        remote(row_ref, rrecv.at[1], fs_sem.at[1], fr_sem.at[1], (row_peer(n - 1), col)),
        remote(csend.at[0], crecv.at[0], fs_sem.at[2], fr_sem.at[2], (row, col_peer(1))),
        remote(csend.at[1], crecv.at[1], fs_sem.at[3], fr_sem.at[3], (row, col_peer(nc - 1))),
    ]
    for copy in feats:
        copy.start()

    for load in loads[3:]:
        load.wait()
    for a in range(3):
        k2t[64 * a : 64 * a + 64] = (0.5 * k2_ref[a].reshape(192, 64).astype(F32).T).astype(BF16)
    w2 = k2t[...]
    lane = lax.broadcasted_iota(jnp.int32, (64, 128), 1)

    def spread(k, carry):
        gsum, rsum = carry
        both = gs[k]
        z = mm(w2, both)
        lo, hi = z[:, :wide], z[:, wide:]
        zb[0, k] = lo[0:64]
        zb[1, k] = lo[64:128] + hi[0:64]
        zb[2, k] = lo[128:192] + hi[64:128]
        zb[3, k] = hi[128:192]
        mid = both[64:128].astype(F32)
        first, second = mid[:, 0:cols], mid[:, wide : wide + cols]
        rsum = jnp.where(lane == 8 + k, jnp.sum(first, axis=1, keepdims=True), rsum)
        rsum = jnp.where(lane == 16 + k, jnp.sum(second, axis=1, keepdims=True), rsum)
        return gsum + first + second, rsum

    gsum, rsum = lax.fori_loop(
        0, 8, spread, (jnp.zeros((64, cols), F32), jnp.zeros((64, 128), F32)), unroll=True
    )

    ma = lax.broadcasted_iota(jnp.int32, (wide, 128), 0)
    cut_low = jnp.logical_and(ma < 8, col == 0)
    cut_high = jnp.logical_and(jnp.logical_and(ma >= cols - 8, ma < cols), col == nc - 1)
    m3[:, 0:128] = jnp.ones((wide, 128), BF16)
    m3[:, 128:256] = jnp.where(jnp.logical_or(cut_low, cut_high), 1.0, 0.0).astype(BF16)
    for b in range(3):
        k1_b = jnp.concatenate([k1_ref[a, b] for a in range(3)], axis=0)
        k1t[b] = k1_b.astype(F32).T.astype(BF16)
    for copy in feats:
        copy.wait_recv()
    rowbuf[0:16, 0:64] = jnp.where(row > 0, rrecv[0].astype(F32), 0.0)
    rowbuf[32:48, 0:64] = jnp.where(row < n - 1, rrecv[1].astype(F32), 0.0)
    left = jnp.where(col > 0, crecv[0].astype(F32), 0.0)
    colbuf[376:392, 0:64] = left
    colbuf[0:8, 0:64] = left[8:16]
    colbuf[264:280, 0:64] = jnp.where(col < nc - 1, crecv[1].astype(F32), 0.0)

    a_all = jnp.zeros((192, 128), F32)
    for a in range(3):
        a_all += mm(
            k1_ref[a].reshape(192, 64), rowbuf[8 * a : 8 * a + 128, 0:64].astype(BF16), NT
        )
    a_all = 0.5 * a_all
    for g in range(4):
        turned = a_all if g == 0 else pltpu.roll(a_all, 128 - 8 * g, 1)
        a_s[g, 0:64] = turned[0:64] + turned[64:128] + turned[128:192]
        a_s[g, 64:128] = jnp.where(col == 0, turned[0:64], turned[128:192])
    b_all = jnp.zeros((192, wide), F32)
    for b in range(3):
        k1_b = jnp.concatenate([k1_ref[a, b] for a in range(3)], axis=0)
        b_all += mm(k1_b, colbuf[8 * b : 8 * b + wide, 0:64].astype(BF16), NT)
    eye = lax.broadcasted_iota(jnp.int32, (64, 64), 0) == lax.broadcasted_iota(jnp.int32, (64, 64), 1)
    bias = 0.5 * jnp.sum(jnp.where(eye, bias_ref[...], 0.0), axis=1, keepdims=True)
    b_s[...] = 0.5 * b_all

    lanes = lax.broadcasted_iota(jnp.int32, (1, wide), 1)
    on_left = jnp.logical_and(lanes >= wide - 8, col > 0)
    on_right = jnp.logical_and(jnp.logical_and(lanes >= cols, lanes < cols + 8), col < nc - 1)
    inside_cols = jnp.where(
        jnp.logical_or(lanes < cols, jnp.logical_or(on_left, on_right)), 1.0, 0.0
    ).astype(F32)
    lane1 = lax.broadcasted_iota(jnp.int32, (1, 128), 1)
    low_cut = jnp.where(jnp.logical_and(lane1 < 8, col == 0), 1.0, 0.0).astype(F32)
    high_cut = jnp.where(jnp.logical_and(lane1 >= 120, col == nc - 1), 1.0, 0.0).astype(F32)
    total = rows * n
    lane2 = lax.broadcasted_iota(jnp.int32, (64, 256), 1) & 127
    t_s[...] = jnp.zeros_like(t_s)
    u_s[...] = jnp.zeros_like(u_s)

    def group(g, carry):
        start = row * rows + 8 * (g - 1)

        def flag(first):
            return jnp.where(jnp.logical_and(first >= 0, first < total), 1.0, 0.0).astype(F32)

        flags = [flag(start + 8 * (a - 1)) for a in range(3)]
        base_s[...] = bias + sum(b_s[64 * a : 64 * a + 64] * flags[a] for a in range(3))
        in_map = flag(start)
        masks = [in_map, in_map, inside_cols[:, 256:384] * in_map]
        cuts = [low_cut, high_cut, None]
        a_g = a_s[g]
        v_s[...] = jnp.zeros_like(v_s)
        for k in range(8):
            row_term = jnp.broadcast_to(a_g[0:64, k : k + 1], (64, 128))
            border = jnp.broadcast_to(a_g[64:128, k : k + 1], (64, 128))
            for tile in range(3):
                at = slice(128 * tile, 128 * tile + 128)
                half = base_s[:, at] + row_term
                if cuts[tile] is not None:
                    half = half - border * cuts[tile]
                p = (1.0 + jnp.tanh(half)) * masks[tile]
                act = half * p
                act_s[g, k, :, at] = act.astype(BF16)
                inner = zb[g, k, :, at] * (p + act * (2.0 - p))
                inn_s[64 * k : 64 * k + 64, at] = inner.astype(BF16)
                v_s[:, at] += inner
        v = v_s[...]
        for a in range(3):
            u_s[64 * a : 64 * a + 64] += v * flags[a]
        sums = mm(inn_s[...], m3[...])
        t = t_s[...]
        for k in range(8):
            t = jnp.where(lane2 == 8 * g + k, sums[64 * k : 64 * k + 64], t)
        t_s[...] = t
        return carry

    lax.fori_loop(0, 4, group, 0)

    def second(k, acc):
        a0, a1, a2, a3 = act_s[0, k], act_s[1, k], act_s[2, k], act_s[3, k]
        low = jnp.concatenate([a2, a0, a2, a1], axis=0)
        high = jnp.concatenate([a3, a1, a3, a2], axis=0)
        return acc + mm(gs[k], jnp.concatenate([low, high], axis=1), NT)

    two = lax.fori_loop(0, 8, second, jnp.zeros((192, 256), F32), unroll=True)
    hi_half = lax.broadcasted_iota(jnp.int32, (192, 128), 1) >= 64
    two_taps = [two[:, 0:128], two[:, 128:256], pltpu.roll(two[:, 0:128], 64, 1)]

    t_mid, t_cut = t_s[:, 0:128], t_s[:, 128:256]
    t_all = jnp.concatenate(
        [jnp.where(col == 0, t_mid - t_cut, t_mid), t_mid, jnp.where(col == nc - 1, t_mid - t_cut, t_mid)], axis=0
    )
    t_b = t_all.astype(BF16)
    u_all = u_s[...]
    u_b = u_all.astype(BF16)
    by_col = [mm(u_b, colbuf[8 * b : 8 * b + wide].astype(BF16)) for b in range(3)]
    for a in range(3):
        by_row = mm(t_b, rowbuf[8 * a : 8 * a + 128].astype(BF16))
        for b in range(3):
            tap = by_row[64 * b : 64 * b + 64] + by_col[b][64 * a : 64 * a + 64]
            tap = jnp.where(hi_half[0:64], two_taps[a][64 * b : 64 * b + 64], tap)
            at = 64 * (3 * a + b)
            pk32[at : at + 64] = tap
            pk[at : at + 64] = tap.astype(BF16)
    if nc * share > 576:
        pk32[576:] = jnp.zeros((nc * share - 576, 128), F32)
        pk[576:] = jnp.zeros((nc * share - 576, 128), BF16)

    cols_p, cols_x = [], []
    for d in range(1, nc):
        src = pk.at[pl.ds(pl.multiple_of(col_peer(d) * share, 16), share)]
        cols_p.append(remote(src, p_recv.at[d - 1], ps_sem.at[d - 1], pr_sem.at[d - 1], (row, col_peer(d))))
        cols_x.append(remote(xtra, x_recv.at[d - 1], xs_sem.at[d - 1], xr_sem.at[d - 1], (row, col_peer(d))))
    for copy in cols_p:
        copy.start()

    t_t = t_all.T
    xtra32[...] = jnp.zeros_like(xtra32)
    for a in range(3):
        part = mm(t_t.astype(BF16), k1_ref[a].reshape(192, 64))
        xtra32[8 * a : 8 * a + 32, 0:64] += part[0:32]
    xtra32[16:32, 0:64] += rsum.T[8:24]
    xtra32[48:49, 0:64] = jnp.sum(t_t, axis=0, keepdims=True)[:, 64:128]
    parts = [mm(k1t[b], u_b) for b in range(3)]
    col_part = pltpu.roll(parts[0], wide - 8, 1) + parts[1] + pltpu.roll(parts[2], 8, 1)
    xtra32[64:128] = col_part[:, cols:wide]
    xtra[...] = xtra32[...].astype(BF16)

    for copy in cols_x:
        copy.start()

    col_main = col_part[:, 0:cols] + gsum
    for copy in cols_p:
        copy.wait_recv()
    mine = pk32[pl.ds(pl.multiple_of(col * share, 16), share)]
    for d in range(1, nc):
        mine = mine + p_recv[d - 1].astype(F32)
    dd32[0:share] = mine
    for copy in cols_x:
        copy.wait_recv()
    line = xtra32[0:64]
    for d in range(1, nc):
        line = line + x_recv[d - 1, 0:64].astype(F32)
    side = lax.broadcasted_iota(jnp.int32, (64, 128), 1)
    from_left = jnp.where(jnp.logical_and(side < 16, col > 0), x_recv[0, 64:128].astype(F32), 0.0)
    from_right = jnp.where(jnp.logical_and(side >= 112, col < nc - 1), x_recv[nc - 2, 64:128].astype(F32), 0.0)

    dd32[share : share + 64] = col_main[:, 0:128] + from_left
    dd32[share + 64 : share + 128] = col_main[:, 128:256] + from_right
    dd32[share + 128 : share + 144] = line[48:64]
    if n * chunk > share + 144:
        dd32[share + 144 :] = jnp.zeros((n * chunk - share - 144, 128), F32)
    dd[...] = dd32[...].astype(BF16)
    nb[...] = line[0:48].astype(BF16)
    scatter = []
    far_first = sorted(range(1, n), key=lambda d: abs(2 * d - n))
    for d in far_first:
        src = dd.at[pl.ds(pl.multiple_of(row_peer(d) * chunk, 16), chunk)]
        scatter.append(remote(src, d_recv.at[pl.ds((d - 1) * chunk, chunk)], ds_sem.at[0], dr_sem.at[0], (row_peer(d), col)))
    near = [
        remote(nb.at[pl.ds(32, 16)], nb_recv.at[0], ns_sem.at[0], nr_sem.at[0], (row_peer(1), col)),
        remote(nb.at[pl.ds(0, 16)], nb_recv.at[1], ns_sem.at[1], nr_sem.at[1], (row_peer(n - 1), col)),
    ]
    for copy in scatter + near:
        copy.start()
    spot = pl.ds(pl.multiple_of(row * chunk, 16), chunk)
    done = dd32[spot]
    most = (n - 1) * chunk
    all_in = remote(dd.at[pl.ds(0, most)], d_recv, ds_sem.at[0], dr_sem.at[0], (row_peer(1), col))
    all_in.wait_recv()
    for d in range(1, n):
        done = done + d_recv[(d - 1) * chunk : d * chunk].astype(F32)
    full[spot] = done.astype(BF16)
    gather = []
    for d in far_first:
        gather.append(remote(full.at[spot], full.at[spot], as_sem.at[0], ar_sem.at[0], (row_peer(d), col)))
    for copy in gather:
        copy.start()
    for copy in near:
        copy.wait_recv()
    low = jnp.where(row > 0, nb_recv[0].astype(F32), 0.0)
    high = jnp.where(row < n - 1, nb_recv[1].astype(F32), 0.0)
    rg_ref[...] = line[16:32] + low + high
    all_out = remote(full.at[pl.ds(0, most)], full.at[pl.ds(0, most)], as_sem.at[0], ar_sem.at[0], (row_peer(1), col))
    all_out.wait_recv()

    own = pl.ds(pl.multiple_of(col * share, 16), share)
    last = []
    for d in range(1, nc):
        last.append(remote(full.at[pl.ds(0, share)], pfull.at[own], cs_sem.at[d - 1], cr_sem.at[d - 1], (row, col_peer(d))))
    for copy in last:
        copy.start()
    pfull[own] = full[0:share]
    for d in range(1, nc):
        other = pl.ds(pl.multiple_of(col_peer(nc - d) * share, 16), share)
        remote(full.at[pl.ds(0, share)], pfull.at[other], cs_sem.at[d - 1], cr_sem.at[d - 1], (row, col_peer(d))).wait_recv()
    for copy in feats + cols_p + cols_x + [all_in, all_out] + near + last:
        copy.wait_send()


def finish(n, nc, share, rg_in, full, pfull, rg_ref, cg_ref, g1_ref, gb_ref, g2_ref):
    whole = 1.0 / math.sqrt(16 * n * 256 * nc)
    tall = 1.0 / math.sqrt(16 * n)
    rg_ref[...] = rg_in[:, 0:64] * (1.0 / math.sqrt(256 * nc))
    cg_ref[:, 0:128] = full[share : share + 64].astype(F32) * tall
    cg_ref[:, 128:256] = full[share + 64 : share + 128].astype(F32) * tall
    gb_ref[...] = full[share + 128 : share + 144].astype(F32)[0:1, 0:64] * whole
    for a in range(3):
        for b in range(3):
            at = 64 * (3 * a + b)
            tap = pfull[at : at + 64].astype(F32) * whole
            g1_ref[a, b] = tap[:, 0:64]
            g2_ref[a, b] = tap[:, 64:128]


def shards(n, nc, grad_out, row_feat, col_feat, conv_one, bias_one, conv_two):
    share = round_up(-(-576 // nc), 16)
    chunk = round_up(-(-(share + 144) // n), 16)
    vmem = pl.BlockSpec(memory_space=pltpu.VMEM)
    dma = pltpu.SemaphoreType.DMA
    scratch = [
        pltpu.VMEM((64, 16, 256), BF16),
        pltpu.VMEM((16, 64), BF16),
        pltpu.VMEM((64, 256), BF16),
        pltpu.VMEM((3, 3, 64, 64), BF16),
        pltpu.VMEM((1, 64), F32),
        pltpu.VMEM((3, 3, 64, 64), BF16),
        pltpu.VMEM((2, 16, 64), BF16),
        dma((6,)),
        pltpu.VMEM((3, 64, 192), BF16),
        pltpu.VMEM((192, 192), BF16),
        pltpu.VMEM((160, 128), F32),
        pltpu.VMEM((400, 128), F32),
        pltpu.VMEM((2, 16, 64), BF16),
        pltpu.VMEM((2, 16, 64), BF16),
        pltpu.VMEM((8, 192, 768), BF16),
        pltpu.VMEM((4, 8, 64, 384), F32),
        pltpu.VMEM((4, 8, 64, 384), BF16),
        pltpu.VMEM((512, 384), BF16),
        pltpu.VMEM((4, 128, 128), F32),
        pltpu.VMEM((192, 384), F32),
        pltpu.VMEM((64, 256), F32),
        pltpu.VMEM((192, 384), F32),
        pltpu.VMEM((384, 256), BF16),
        pltpu.VMEM((64, 384), F32),
        pltpu.VMEM((64, 384), F32),
        pltpu.VMEM((nc * share, 128), BF16),
        pltpu.VMEM((nc * share, 128), F32),
        pltpu.VMEM((128, 128), BF16),
        pltpu.VMEM((128, 128), F32),
        pltpu.VMEM((nc - 1, share, 128), BF16),
        pltpu.VMEM((nc - 1, 128, 128), BF16),
        pltpu.VMEM((n * chunk, 128), BF16),
        pltpu.VMEM((n * chunk, 128), F32),
        pltpu.VMEM((48, 128), BF16),
        pltpu.VMEM((2, 16, 128), BF16),
        pltpu.VMEM(((n - 1) * chunk, 128), BF16),
        dma((4,)), dma((4,)),
        dma((nc - 1,)), dma((nc - 1,)),
        dma((nc - 1,)), dma((nc - 1,)),
        dma((1,)), dma((1,)),
        dma((2,)), dma((2,)),
        dma((1,)), dma((1,)),
        dma((nc - 1,)), dma((nc - 1,)),
    ]
    sums = pl.pallas_call(
        functools.partial(kernel, n, nc, share, chunk),
        out_shape=(
            jax.ShapeDtypeStruct((16, 128), F32),
            jax.ShapeDtypeStruct((n * chunk, 128), BF16),
            jax.ShapeDtypeStruct((nc * share, 128), BF16),
        ),
        in_specs=[pl.BlockSpec(memory_space=pltpu.HBM)] * 6,
        out_specs=(vmem,) * 3,
        scratch_shapes=scratch,
        compiler_params=pltpu.CompilerParams(
            collective_id=0, has_side_effects=True, vmem_limit_bytes=60 * 2**20
        ),
    )(grad_out, row_feat, col_feat.T, conv_one, bias_one.reshape(1, 64), conv_two)
    out = pl.pallas_call(
        functools.partial(finish, n, nc, share),
        out_shape=(
            jax.ShapeDtypeStruct((16, 64), F32),
            jax.ShapeDtypeStruct((64, 256), F32),
            jax.ShapeDtypeStruct((3, 3, 64, 64), F32),
            jax.ShapeDtypeStruct((1, 64), F32),
            jax.ShapeDtypeStruct((3, 3, 64, 64), F32),
        ),
        in_specs=[vmem] * 3,
        out_specs=(vmem,) * 5,
        compiler_params=pltpu.CompilerParams(vmem_limit_bytes=60 * 2**20),
    )(*sums)
    return (out[0], out[1].T, out[2], out[3].reshape(64), out[4])


def solution(mesh):
    n, nc = mesh.shape["row"], mesh.shape["col"]
    in_specs = (P(None, "row", "col"), P("row", None), P("col", None), P(), P(), P())
    out_specs = (P("row", None), P("col", None), P(), P(), P())
    return jax.shard_map(
        functools.partial(shards, n, nc), mesh=mesh, in_specs=in_specs, out_specs=out_specs, check_vma=False
    )
```

```python
import functools
import math

import jax
import jax.numpy as jnp
from jax import lax
from jax.experimental import pallas as pl
from jax.experimental.pallas import tpu as pltpu
from jax.sharding import PartitionSpec as P

F32 = jnp.float32
BF16 = jnp.bfloat16
MESH = pl.DeviceIdType.MESH
NN = (((1,), (0,)), ((), ()))
NT = (((1,), (1,)), ((), ()))


def mm(x, y, dims=NN):
    return lax.dot_general(x, y, dims, preferred_element_type=F32)


def round_up(value, unit):
    return -(-value // unit) * unit


def kernel(
    n, nc, share, chunk,
    g_hbm, row_hbm, col_hbm, k1_hbm, bias_hbm, k2_hbm,
    rg_ref, full, pfull,
    g_ref, row_ref, col_ref, k1_ref, bias_ref, k2_ref, csend, in_sem, k1t, k2t,
    rowbuf, colbuf, rrecv, crecv,
    gs, zb, act_s, inn_s, a_s, b_s, t_s, u_s, m3, base_s, v_s,
    pk, pk32, xtra, xtra32, p_recv, x_recv,
    dd, dd32, nb, nb_recv, d_recv,
    fs_sem, fr_sem, ps_sem, pr_sem, xs_sem, xr_sem,
    ds_sem, dr_sem, ns_sem, nr_sem, as_sem, ar_sem, cs_sem, cr_sem,
):
    row = lax.axis_index("row")
    col = lax.axis_index("col")
    rows, cols, wide = 16, 256, 384

    def row_peer(d):
        return lax.rem(row + d, n)

    def col_peer(d):
        return lax.rem(col + d, nc)

    loads = [
        pltpu.make_async_copy(src, dst, in_sem.at[i])
        for i, (src, dst) in enumerate(
            [(g_hbm, g_ref), (row_hbm, row_ref), (col_hbm, col_ref), (k1_hbm, k1_ref), (bias_hbm, bias_ref), (k2_hbm, k2_ref)]
        )
    ]
    for load in loads:
        load.start()
    barrier = pltpu.get_barrier_semaphore()
    for d in range(1, n):
        pl.semaphore_signal(barrier, inc=1, device_id=(row_peer(d), col), device_id_type=MESH)
    for d in range(1, nc):
        pl.semaphore_signal(barrier, inc=1, device_id=(row, col_peer(d)), device_id_type=MESH)

    def remote(src, dst, send, recv, to):
        return pltpu.make_async_remote_copy(
            src_ref=src, dst_ref=dst, send_sem=send, recv_sem=recv, device_id=to, device_id_type=MESH
        )

    pa = lax.broadcasted_iota(jnp.int32, (256, 256), 0)
    pb = lax.broadcasted_iota(jnp.int32, (256, 256), 1)
    perm = ((pa & 15) * 16 + (pa >> 4) == pb).astype(F32).astype(BF16)
    sa = lax.broadcasted_iota(jnp.int32, (256, wide), 0)
    sb = lax.broadcasted_iota(jnp.int32, (256, wide), 1)
    gap = sb - sa
    shifts = jnp.concatenate(
        [
            jnp.logical_or(gap == -8, gap == wide - 8).astype(F32).astype(BF16),
            (gap == 8).astype(F32).astype(BF16),
        ],
        axis=1,
    )
    rowbuf[...] = jnp.zeros_like(rowbuf)
    colbuf[...] = jnp.zeros_like(colbuf)
    loads[1].wait()
    loads[2].wait()
    rowbuf[16:32, 0:64] = row_ref[...].astype(F32)
    col_t = col_ref[...].astype(F32).T
    colbuf[8 : 8 + cols, 0:64] = col_t
    colbuf[392:400, 0:64] = col_t[0:8]
    csend[0] = col_t[cols - 16 : cols].astype(BF16)
    csend[1] = col_t[0:16].astype(BF16)
    loads[0].wait()

    blank = jnp.zeros((256, wide - cols), BF16)

    def build(og):
        x = g_ref[pl.ds(og * 16, 16)].reshape(256, cols)
        plain = mm(perm, x).astype(BF16)
        moved = mm(plain, shifts).astype(BF16)
        turns = [moved[:, :wide], jnp.concatenate([plain, blank], axis=1), moved[:, wide:]]
        for r in range(rows):
            h, k = r // 8, r % 8
            for b in range(3):
                gs[k, pl.ds(b * 64 + og * 16, 16), h * wide : (h + 1) * wide] = turns[b][16 * r : 16 * r + 16]

    for og in range(4):
        build(og)

    pl.semaphore_wait(barrier, (n - 1) + (nc - 1))
    feats = [
        remote(row_ref, rrecv.at[0], fs_sem.at[0], fr_sem.at[0], (row_peer(1), col)),
        remote(row_ref, rrecv.at[1], fs_sem.at[1], fr_sem.at[1], (row_peer(n - 1), col)),
        remote(csend.at[0], crecv.at[0], fs_sem.at[2], fr_sem.at[2], (row, col_peer(1))),
        remote(csend.at[1], crecv.at[1], fs_sem.at[3], fr_sem.at[3], (row, col_peer(nc - 1))),
    ]
    for copy in feats:
        copy.start()

    for load in loads[3:]:
        load.wait()
    for a in range(3):
        k2t[64 * a : 64 * a + 64] = (0.5 * k2_ref[a].reshape(192, 64).astype(F32).T).astype(BF16)
    w2 = k2t[...]
    lane = lax.broadcasted_iota(jnp.int32, (64, 128), 1)

    def spread(k, carry):
        gsum, rsum = carry
        both = gs[k]
        z = mm(w2, both)
        lo, hi = z[:, :wide], z[:, wide:]
        zb[0, k] = lo[0:64]
        zb[1, k] = lo[64:128] + hi[0:64]
        zb[2, k] = lo[128:192] + hi[64:128]
        zb[3, k] = hi[128:192]
        mid = both[64:128].astype(F32)
        first, second = mid[:, 0:cols], mid[:, wide : wide + cols]
        rsum = jnp.where(lane == 8 + k, jnp.sum(first, axis=1, keepdims=True), rsum)
        rsum = jnp.where(lane == 16 + k, jnp.sum(second, axis=1, keepdims=True), rsum)
        return gsum + first + second, rsum

    gsum, rsum = lax.fori_loop(
        0, 8, spread, (jnp.zeros((64, cols), F32), jnp.zeros((64, 128), F32)), unroll=2
    )

    ma = lax.broadcasted_iota(jnp.int32, (wide, 128), 0)
    cut_low = jnp.logical_and(ma < 8, col == 0)
    cut_high = jnp.logical_and(jnp.logical_and(ma >= cols - 8, ma < cols), col == nc - 1)
    m3[:, 0:128] = jnp.ones((wide, 128), BF16)
    m3[:, 128:256] = jnp.where(jnp.logical_or(cut_low, cut_high), 1.0, 0.0).astype(BF16)
    for b in range(3):
        k1_b = jnp.concatenate([k1_ref[a, b] for a in range(3)], axis=0)
        k1t[b] = k1_b.astype(F32).T.astype(BF16)
    for copy in feats:
        copy.wait_recv()
    rowbuf[0:16, 0:64] = jnp.where(row > 0, rrecv[0].astype(F32), 0.0)
    rowbuf[32:48, 0:64] = jnp.where(row < n - 1, rrecv[1].astype(F32), 0.0)
    left = jnp.where(col > 0, crecv[0].astype(F32), 0.0)
    colbuf[376:392, 0:64] = left
    colbuf[0:8, 0:64] = left[8:16]
    colbuf[264:280, 0:64] = jnp.where(col < nc - 1, crecv[1].astype(F32), 0.0)

    a_all = jnp.zeros((192, 128), F32)
    for a in range(3):
        a_all += mm(
            k1_ref[a].reshape(192, 64), rowbuf[8 * a : 8 * a + 128, 0:64].astype(BF16), NT
        )
    a_all = 0.5 * a_all
    for g in range(4):
        turned = a_all if g == 0 else pltpu.roll(a_all, 128 - 8 * g, 1)
        a_s[g, 0:64] = turned[0:64] + turned[64:128] + turned[128:192]
        a_s[g, 64:128] = jnp.where(col == 0, turned[0:64], turned[128:192])
    b_all = jnp.zeros((192, wide), F32)
    for b in range(3):
        k1_b = jnp.concatenate([k1_ref[a, b] for a in range(3)], axis=0)
        b_all += mm(k1_b, colbuf[8 * b : 8 * b + wide, 0:64].astype(BF16), NT)
    eye = lax.broadcasted_iota(jnp.int32, (64, 64), 0) == lax.broadcasted_iota(jnp.int32, (64, 64), 1)
    bias = 0.5 * jnp.sum(jnp.where(eye, bias_ref[...], 0.0), axis=1, keepdims=True)
    b_s[...] = 0.5 * b_all

    lanes = lax.broadcasted_iota(jnp.int32, (1, wide), 1)
    on_left = jnp.logical_and(lanes >= wide - 8, col > 0)
    on_right = jnp.logical_and(jnp.logical_and(lanes >= cols, lanes < cols + 8), col < nc - 1)
    inside_cols = jnp.where(
        jnp.logical_or(lanes < cols, jnp.logical_or(on_left, on_right)), 1.0, 0.0
    ).astype(F32)
    lane1 = lax.broadcasted_iota(jnp.int32, (1, 128), 1)
    low_cut = jnp.where(jnp.logical_and(lane1 < 8, col == 0), 1.0, 0.0).astype(F32)
    high_cut = jnp.where(jnp.logical_and(lane1 >= 120, col == nc - 1), 1.0, 0.0).astype(F32)
    total = rows * n
    lane2 = lax.broadcasted_iota(jnp.int32, (64, 256), 1) & 127
    t_s[...] = jnp.zeros_like(t_s)
    u_s[...] = jnp.zeros_like(u_s)

    def group(g, carry):
        start = row * rows + 8 * (g - 1)

        def flag(first):
            return jnp.where(jnp.logical_and(first >= 0, first < total), 1.0, 0.0).astype(F32)

        flags = [flag(start + 8 * (a - 1)) for a in range(3)]
        base_s[...] = bias + sum(b_s[64 * a : 64 * a + 64] * flags[a] for a in range(3))
        in_map = flag(start)
        masks = [in_map, in_map, inside_cols[:, 256:384] * in_map]
        cuts = [low_cut, high_cut, None]
        a_g = a_s[g]
        v_s[...] = jnp.zeros_like(v_s)
        for k in range(8):
            row_term = jnp.broadcast_to(a_g[0:64, k : k + 1], (64, 128))
            border = jnp.broadcast_to(a_g[64:128, k : k + 1], (64, 128))
            for tile in range(3):
                at = slice(128 * tile, 128 * tile + 128)
                half = base_s[:, at] + row_term
                if cuts[tile] is not None:
                    half = half - border * cuts[tile]
                p = (1.0 + jnp.tanh(half)) * masks[tile]
                act = half * p
                act_s[g, k, :, at] = act.astype(BF16)
                inner = zb[g, k, :, at] * (p + act * (2.0 - p))
                inn_s[64 * k : 64 * k + 64, at] = inner.astype(BF16)
                v_s[:, at] += inner
        v = v_s[...]
        for a in range(3):
            u_s[64 * a : 64 * a + 64] += v * flags[a]
        sums = mm(inn_s[...], m3[...])
        t = t_s[...]
        for k in range(8):
            t = jnp.where(lane2 == 8 * g + k, sums[64 * k : 64 * k + 64], t)
        t_s[...] = t
        return carry

    lax.fori_loop(0, 4, group, 0)

    def second(k, acc):
        a0, a1, a2, a3 = act_s[0, k], act_s[1, k], act_s[2, k], act_s[3, k]
        low = jnp.concatenate([a2, a0, a2, a1], axis=0)
        high = jnp.concatenate([a3, a1, a3, a2], axis=0)
        return acc + mm(gs[k], jnp.concatenate([low, high], axis=1), NT)

    two = lax.fori_loop(0, 8, second, jnp.zeros((192, 256), F32), unroll=4)
    hi_half = lax.broadcasted_iota(jnp.int32, (192, 128), 1) >= 64
    two_taps = [two[:, 0:128], two[:, 128:256], pltpu.roll(two[:, 0:128], 64, 1)]

    t_mid, t_cut = t_s[:, 0:128], t_s[:, 128:256]
    t_all = jnp.concatenate(
        [jnp.where(col == 0, t_mid - t_cut, t_mid), t_mid, jnp.where(col == nc - 1, t_mid - t_cut, t_mid)], axis=0
    )
    t_b = t_all.astype(BF16)
    u_all = u_s[...]
    u_b = u_all.astype(BF16)
    by_col = [mm(u_b, colbuf[8 * b : 8 * b + wide].astype(BF16)) for b in range(3)]
    for a in range(3):
        by_row = mm(t_b, rowbuf[8 * a : 8 * a + 128].astype(BF16))
        for b in range(3):
            tap = by_row[64 * b : 64 * b + 64] + by_col[b][64 * a : 64 * a + 64]
            tap = jnp.where(hi_half[0:64], two_taps[a][64 * b : 64 * b + 64], tap)
            at = 64 * (3 * a + b)
            pk32[at : at + 64] = tap
            pk[at : at + 64] = tap.astype(BF16)
    if nc * share > 576:
        pk32[576:] = jnp.zeros((nc * share - 576, 128), F32)
        pk[576:] = jnp.zeros((nc * share - 576, 128), BF16)

    cols_p, cols_x = [], []
    for d in range(1, nc):
        src = pk.at[pl.ds(pl.multiple_of(col_peer(d) * share, 16), share)]
        cols_p.append(remote(src, p_recv.at[d - 1], ps_sem.at[d - 1], pr_sem.at[d - 1], (row, col_peer(d))))
        cols_x.append(remote(xtra, x_recv.at[d - 1], xs_sem.at[d - 1], xr_sem.at[d - 1], (row, col_peer(d))))
    for copy in cols_p:
        copy.start()

    t_t = t_all.T
    xtra32[...] = jnp.zeros_like(xtra32)
    for a in range(3):
        part = mm(t_t.astype(BF16), k1_ref[a].reshape(192, 64))
        xtra32[8 * a : 8 * a + 32, 0:64] += part[0:32]
    xtra32[16:32, 0:64] += rsum.T[8:24]
    xtra32[48:49, 0:64] = jnp.sum(t_t, axis=0, keepdims=True)[:, 64:128]
    parts = [mm(k1t[b], u_b) for b in range(3)]
    col_part = pltpu.roll(parts[0], wide - 8, 1) + parts[1] + pltpu.roll(parts[2], 8, 1)
    xtra32[64:128] = col_part[:, cols:wide]
    xtra[...] = xtra32[...].astype(BF16)

    for copy in cols_x:
        copy.start()

    col_main = col_part[:, 0:cols] + gsum
    for copy in cols_p:
        copy.wait_recv()
    mine = pk32[pl.ds(pl.multiple_of(col * share, 16), share)]
    for d in range(1, nc):
        mine = mine + p_recv[d - 1].astype(F32)
    dd32[0:share] = mine
    for copy in cols_x:
        copy.wait_recv()
    line = xtra32[0:64]
    for d in range(1, nc):
        line = line + x_recv[d - 1, 0:64].astype(F32)
    side = lax.broadcasted_iota(jnp.int32, (64, 128), 1)
    from_left = jnp.where(jnp.logical_and(side < 16, col > 0), x_recv[0, 64:128].astype(F32), 0.0)
    from_right = jnp.where(jnp.logical_and(side >= 112, col < nc - 1), x_recv[nc - 2, 64:128].astype(F32), 0.0)

    dd32[share : share + 64] = col_main[:, 0:128] + from_left
    dd32[share + 64 : share + 128] = col_main[:, 128:256] + from_right
    dd32[share + 128 : share + 144] = line[48:64]
    if n * chunk > share + 144:
        dd32[share + 144 :] = jnp.zeros((n * chunk - share - 144, 128), F32)
    dd[...] = dd32[...].astype(BF16)
    nb[...] = line[0:48].astype(BF16)
    scatter = []
    for d in range(1, n):
        src = dd.at[pl.ds(pl.multiple_of(row_peer(d) * chunk, 16), chunk)]
        scatter.append(remote(src, d_recv.at[pl.ds((d - 1) * chunk, chunk)], ds_sem.at[0], dr_sem.at[0], (row_peer(d), col)))
    near = [
        remote(nb.at[pl.ds(32, 16)], nb_recv.at[0], ns_sem.at[0], nr_sem.at[0], (row_peer(1), col)),
        remote(nb.at[pl.ds(0, 16)], nb_recv.at[1], ns_sem.at[1], nr_sem.at[1], (row_peer(n - 1), col)),
    ]
    for copy in scatter + near:
        copy.start()
    spot = pl.ds(pl.multiple_of(row * chunk, 16), chunk)
    done = dd32[spot]
    most = (n - 1) * chunk
    all_in = remote(dd.at[pl.ds(0, most)], d_recv, ds_sem.at[0], dr_sem.at[0], (row_peer(1), col))
    all_in.wait_recv()
    for d in range(1, n):
        done = done + d_recv[(d - 1) * chunk : d * chunk].astype(F32)
    full[spot] = done.astype(BF16)
    gather = []
    for d in range(1, n):
        gather.append(remote(full.at[spot], full.at[spot], as_sem.at[0], ar_sem.at[0], (row_peer(d), col)))
    for copy in gather:
        copy.start()
    for copy in near:
        copy.wait_recv()
    low = jnp.where(row > 0, nb_recv[0].astype(F32), 0.0)
    high = jnp.where(row < n - 1, nb_recv[1].astype(F32), 0.0)
    rg_ref[...] = line[16:32] + low + high
    all_out = remote(full.at[pl.ds(0, most)], full.at[pl.ds(0, most)], as_sem.at[0], ar_sem.at[0], (row_peer(1), col))
    all_out.wait_recv()

    own = pl.ds(pl.multiple_of(col * share, 16), share)
    last = []
    for d in range(1, nc):
        last.append(remote(full.at[pl.ds(0, share)], pfull.at[own], cs_sem.at[d - 1], cr_sem.at[d - 1], (row, col_peer(d))))
    for copy in last:
        copy.start()
    pfull[own] = full[0:share]
    for d in range(1, nc):
        other = pl.ds(pl.multiple_of(col_peer(nc - d) * share, 16), share)
        remote(full.at[pl.ds(0, share)], pfull.at[other], cs_sem.at[d - 1], cr_sem.at[d - 1], (row, col_peer(d))).wait_recv()
    for copy in feats + cols_p + cols_x + [all_in, all_out] + near + last:
        copy.wait_send()


def finish(n, nc, share, rg_in, full, pfull, rg_ref, cg_ref, g1_ref, gb_ref, g2_ref):
    whole = 1.0 / math.sqrt(16 * n * 256 * nc)
    tall = 1.0 / math.sqrt(16 * n)
    rg_ref[...] = rg_in[:, 0:64] * (1.0 / math.sqrt(256 * nc))
    cg_ref[:, 0:128] = full[share : share + 64].astype(F32) * tall
    cg_ref[:, 128:256] = full[share + 64 : share + 128].astype(F32) * tall
    gb_ref[...] = full[share + 128 : share + 144].astype(F32)[0:1, 0:64] * whole
    for a in range(3):
        for b in range(3):
            at = 64 * (3 * a + b)
            tap = pfull[at : at + 64].astype(F32) * whole
            g1_ref[a, b] = tap[:, 0:64]
            g2_ref[a, b] = tap[:, 64:128]


def shards(n, nc, grad_out, row_feat, col_feat, conv_one, bias_one, conv_two):
    share = round_up(-(-576 // nc), 16)
    chunk = round_up(-(-(share + 144) // n), 16)
    vmem = pl.BlockSpec(memory_space=pltpu.VMEM)
    dma = pltpu.SemaphoreType.DMA
    scratch = [
        pltpu.VMEM((64, 16, 256), BF16),
        pltpu.VMEM((16, 64), BF16),
        pltpu.VMEM((64, 256), BF16),
        pltpu.VMEM((3, 3, 64, 64), BF16),
        pltpu.VMEM((1, 64), F32),
        pltpu.VMEM((3, 3, 64, 64), BF16),
        pltpu.VMEM((2, 16, 64), BF16),
        dma((6,)),
        pltpu.VMEM((3, 64, 192), BF16),
        pltpu.VMEM((192, 192), BF16),
        pltpu.VMEM((160, 128), F32),
        pltpu.VMEM((400, 128), F32),
        pltpu.VMEM((2, 16, 64), BF16),
        pltpu.VMEM((2, 16, 64), BF16),
        pltpu.VMEM((8, 192, 768), BF16),
        pltpu.VMEM((4, 8, 64, 384), F32),
        pltpu.VMEM((4, 8, 64, 384), BF16),
        pltpu.VMEM((512, 384), BF16),
        pltpu.VMEM((4, 128, 128), F32),
        pltpu.VMEM((192, 384), F32),
        pltpu.VMEM((64, 256), F32),
        pltpu.VMEM((192, 384), F32),
        pltpu.VMEM((384, 256), BF16),
        pltpu.VMEM((64, 384), F32),
        pltpu.VMEM((64, 384), F32),
        pltpu.VMEM((nc * share, 128), BF16),
        pltpu.VMEM((nc * share, 128), F32),
        pltpu.VMEM((128, 128), BF16),
        pltpu.VMEM((128, 128), F32),
        pltpu.VMEM((nc - 1, share, 128), BF16),
        pltpu.VMEM((nc - 1, 128, 128), BF16),
        pltpu.VMEM((n * chunk, 128), BF16),
        pltpu.VMEM((n * chunk, 128), F32),
        pltpu.VMEM((48, 128), BF16),
        pltpu.VMEM((2, 16, 128), BF16),
        pltpu.VMEM(((n - 1) * chunk, 128), BF16),
        dma((4,)), dma((4,)),
        dma((nc - 1,)), dma((nc - 1,)),
        dma((nc - 1,)), dma((nc - 1,)),
        dma((1,)), dma((1,)),
        dma((2,)), dma((2,)),
        dma((1,)), dma((1,)),
        dma((nc - 1,)), dma((nc - 1,)),
    ]
    sums = pl.pallas_call(
        functools.partial(kernel, n, nc, share, chunk),
        out_shape=(
            jax.ShapeDtypeStruct((16, 128), F32),
            jax.ShapeDtypeStruct((n * chunk, 128), BF16),
            jax.ShapeDtypeStruct((nc * share, 128), BF16),
        ),
        in_specs=[pl.BlockSpec(memory_space=pltpu.HBM)] * 6,
        out_specs=(vmem,) * 3,
        scratch_shapes=scratch,
        compiler_params=pltpu.CompilerParams(
            collective_id=0, has_side_effects=True, vmem_limit_bytes=60 * 2**20
        ),
    )(grad_out, row_feat, col_feat.T, conv_one, bias_one.reshape(1, 64), conv_two)
    out = pl.pallas_call(
        functools.partial(finish, n, nc, share),
        out_shape=(
            jax.ShapeDtypeStruct((16, 64), F32),
            jax.ShapeDtypeStruct((64, 256), F32),
            jax.ShapeDtypeStruct((3, 3, 64, 64), F32),
            jax.ShapeDtypeStruct((1, 64), F32),
            jax.ShapeDtypeStruct((3, 3, 64, 64), F32),
        ),
        in_specs=[vmem] * 3,
        out_specs=(vmem,) * 5,
        compiler_params=pltpu.CompilerParams(vmem_limit_bytes=60 * 2**20),
    )(*sums)
    return (out[0], out[1].T, out[2], out[3].reshape(64), out[4])


def solution(mesh):
    n, nc = mesh.shape["row"], mesh.shape["col"]
    in_specs = (P(None, "row", "col"), P("row", None), P("col", None), P(), P(), P())
    out_specs = (P("row", None), P("col", None), P(), P(), P())
    return jax.shard_map(
        functools.partial(shards, n, nc), mesh=mesh, in_specs=in_specs, out_specs=out_specs, check_vma=False
    )
```
